32 devices in a mesh: gy: 4 (over y, x), gz: 4 (over z), col: 2 (over core).
Axes of the slice: x: 2, y: 2, z: 4, core: 2. Of those that a mesh axis runs over, the one named last changes fastest.
Arguments:
- noise: float32 [3, 256, 1024], P(None, 'gz', ('gy', 'col')), may hold values from -6 to 6
- mean_profile: float32 [256], P('gz'), may hold values from 0.4 to 1.2
- lund_diag: float32 [3, 256], P(None, 'gz'), may hold values from 0.05 to 0.3
- lund_off: float32 [3, 256], P(None, 'gz'), may hold values from -0.1 to 0.1
- populations: float32 [19, 4, 256, 1024], P(None, None, 'gz', ('gy', 'col')), may hold values from 0.5 to 1.5
- mask: int32 [4, 256, 1024], P(None, 'gz', ('gy', 'col')), may hold values 0 or 1
Outputs:
- inflow: float32 [3, 256, 1024], P(None, 'gz', ('gy', 'col'))
- populations_next: float32 [19, 4, 256, 1024], P(None, None, 'gz', ('gy', 'col'))
The draws below stay inside these ranges and needn't reach their ends.
All inputs are finite; a program needn't handle non-finite values. No bound on the sum of `mask` on one device may be relied on, other than what follows from the above.
Results may differ from the reference program's by a relative error of at most 0.0001.
Values sent between devices are 32-bit elements; how exact they have to be, the bound alone decides.
No kernel may reach another device: no remote copies, remote signals or barrier semaphores. Data moves between devices by JAX's collectives and lax.ppermute only.
A program may use at most 128 MiB of HBM per device.

```python
import math
import jax
import jax.numpy as jnp
import numpy as np
from jax import lax

HW = 64
NX = 4
STEPS = 2
NY = 1024
NZ = 256


def touch_ends(drawn, key, least, high):
    longest = drawn.shape.index(max(drawn.shape))
    spots = []
    for shift in (0, 1):
        where = [jax.random.randint(jax.random.fold_in(key, axis), (), 0, length) for axis, length in enumerate(drawn.shape)]
        where[longest] = (where[longest] + shift) % drawn.shape[longest]
        spots.append(tuple(where))
    return drawn.at[spots[0]].set(least).at[spots[1]].set(high)


def block_scale(key, extent, cuts, low, high):
    factor_of, own = 1.0, jax.random.fold_in(key, 6)
    for position, blocks in cuts:
        steps = jnp.exp(jax.random.uniform(jax.random.fold_in(own, position), (blocks,), jnp.float32, low / len(cuts), high / len(cuts)))
        factor_of = factor_of * jnp.repeat(steps, extent[position] // blocks).reshape([-1 if axis == position else 1 for axis in range(len(extent))])
    return factor_of


def normal_values(own_key, extent, scale, most, split=(), held_as=jnp.bfloat16):
    drawn = scale * jax.random.normal(own_key, extent, jnp.float32)
    if split:
        drawn = drawn * block_scale(own_key, extent, split, -0.22, 0.18)
    return jnp.clip(drawn, -most, most).astype(held_as)


def setup_inputs(seed: int = 0) -> dict:
    streams_of = jax.random.split(jax.random.key(seed), 7)
    return {
        "noise": normal_values(streams_of[0], (3, NZ, NY), 1.0, 6.0, ((1, 4), (2, 8)), jnp.float32),
        "mean_profile": jnp.clip(0.4 + 0.800000042 * jax.random.uniform(streams_of[1], (NZ,), jnp.float32) ** block_scale(streams_of[1], (NZ,), ((0, 4),), -0.2, 0.2), 0.4, 1.2),
        "lund_diag": jnp.clip(jnp.exp(math.log(0.3) - 1.7917595 * jax.random.uniform(streams_of[2], (3, NZ), jnp.float32) ** block_scale(streams_of[2], (3, NZ), ((1, 4),), -0.2, 0.2)), 0.05, 0.3),
        "lund_off": jnp.clip(jax.random.uniform(streams_of[3], (3, NZ), jnp.float32, -0.1, 0.1) * block_scale(streams_of[3], (3, NZ), ((1, 4),), -0.4, 0.0), -0.1, 0.1),
        "populations": jnp.clip(1.0 + 0.1 * jax.random.normal(streams_of[4], (19, NX, NZ, NY), jnp.float32), 0.5, 1.5),
        "mask": touch_ends((jax.random.randint(streams_of[5], (NX, NZ, NY), 0, 8) < 1).astype(jnp.int32), jax.random.fold_in(streams_of[5], 1), 0, 1),
    }


DIRECTIONS = np.array([[0, 0, 0], [1, 0, 0], [-1, 0, 0], [0, 1, 0], [0, -1, 0], [0, 0, 1], [0, 0, -1], [1, 1, 0], [-1, -1, 0], [1, -1, 0], [-1, 1, 0], [1, 0, 1], [-1, 0, -1], [1, 0, -1], [-1, 0, 1], [0, 1, 1], [0, -1, -1], [0, 1, -1], [0, -1, 1]])
LATTICE_WEIGHTS = [1.0 / 3.0] + [1.0 / 18.0] * 6 + [1.0 / 36.0] * 12
OPPOSITE = [0, 2, 1, 4, 3, 6, 5, 8, 7, 10, 9, 12, 11, 14, 13, 16, 15, 18, 17]
relax_time = 0.8
inlet_speed = 0.05

def column(values, rank):
    return jnp.asarray([float(v) for v in values], jnp.float32).reshape((19,) + (1,) * rank)

def equilibrium(density, vel_x, vel_y, vel_z):
    rank = density.ndim
    proj = column(DIRECTIONS[:, 0], rank) * vel_x[None] + column(DIRECTIONS[:, 1], rank) * vel_y[None] + column(DIRECTIONS[:, 2], rank) * vel_z[None]
    square = vel_x * vel_x + vel_y * vel_y + vel_z * vel_z
    return density[None] * (1.0 + 3.0 * proj + 4.5 * proj * proj - 1.5 * square[None])

def collide(state, solid):
    weighted = column(LATTICE_WEIGHTS, 3) * state
    density = lax.optimization_barrier(jnp.sum(weighted, axis=0))
    vel_x = lax.optimization_barrier(jnp.sum(column(DIRECTIONS[:, 0], 3) * weighted, axis=0)) / density
    vel_y = lax.optimization_barrier(jnp.sum(column(DIRECTIONS[:, 1], 3) * weighted, axis=0)) / density
    vel_z = lax.optimization_barrier(jnp.sum(column(DIRECTIONS[:, 2], 3) * weighted, axis=0)) / density
    relaxed = state - (state - equilibrium(density, vel_x, vel_y, vel_z)) / relax_time
    bounced = jnp.stack([state[OPPOSITE[i]] for i in range(19)])
    return jnp.where(solid[None], bounced, relaxed)

def filter_taps():
    spread = HW // 2
    offsets = jnp.arange(-HW, HW + 1).astype(jnp.float32)
    raw = jnp.exp(-math.pi * offsets * offsets / (2.0 * spread * spread))
    return raw / jnp.sqrt(jnp.sum(raw * raw))

def lund(filtered, mean_profile, lund_diag, lund_off):
    first = mean_profile[:, None] + lund_diag[0][:, None] * filtered[0]
    second = lund_off[0][:, None] * filtered[0] + lund_diag[1][:, None] * filtered[1]
    third = lund_off[1][:, None] * filtered[0] + lund_off[2][:, None] * filtered[1] + lund_diag[2][:, None] * filtered[2]
    return jnp.stack([first, second, third])

def reference(noise, mean_profile, lund_diag, lund_off, populations, mask):
    taps = filter_taps()
    wide = jnp.concatenate([noise[:, :, NY - HW:], noise, noise[:, :, :HW]], axis=2)
    along = jnp.zeros_like(noise)
    for k in range(2 * HW + 1):
        along = along + taps[k] * wide[:, :, k:k + NY]
    tall = jnp.pad(along, ((0, 0), (HW, HW), (0, 0)))
    filtered = jnp.zeros_like(noise)
    for k in range(2 * HW + 1):
        filtered = filtered + taps[k] * tall[:, k:k + NZ, :]
    inflow = lund(filtered, mean_profile, lund_diag, lund_off)
    heights = jnp.arange(NZ)
    solid = (mask == 1) | ((heights == 0) | (heights == NZ - 1))[None, :, None]
    inlet_state = equilibrium(jnp.ones_like(inflow[0]), inlet_speed * inflow[0], inlet_speed * inflow[1], inlet_speed * inflow[2])
    leftward = jnp.asarray(DIRECTIONS[:, 0] < 0)[:, None, None]
    state = populations
    for step in range(STEPS):
        post = collide(state, solid)
        padded = jnp.pad(post, ((0, 0), (1, 1), (1, 1), (0, 0)))
        padded = jnp.concatenate([padded[..., NY - 1:], padded, padded[..., :1]], axis=3)
        pieces = []
        for i in range(19):
            step_x, step_y, step_z = (int(DIRECTIONS[i, 0]), int(DIRECTIONS[i, 1]), int(DIRECTIONS[i, 2]))
            pieces.append(padded[i, 1 - step_x:1 - step_x + NX, 1 - step_z:1 - step_z + NZ, 1 - step_y:1 - step_y + NY])
        moved = jnp.stack(pieces)
        first = jnp.where(solid[0][None], moved[:, 0], inlet_state)
        moved = moved.at[:, 0].set(first)
        tail = jnp.where(leftward, moved[:, NX - 2], moved[:, NX - 1])
        state = moved.at[:, NX - 1].set(tail)
    return (inflow, state)
```

```python
import math

import jax
import jax.numpy as jnp
import numpy as np
from jax import lax
from jax.experimental import pallas as pl
from jax.experimental.pallas import tpu as pltpu
from jax.sharding import PartitionSpec as P

HW = 64
DIRS = [
    (0, 0, 0),
    (1, 0, 0), (-1, 0, 0), (0, 1, 0), (0, -1, 0), (0, 0, 1), (0, 0, -1),
    (1, 1, 0), (-1, -1, 0), (1, -1, 0), (-1, 1, 0),
    (1, 0, 1), (-1, 0, -1), (1, 0, -1), (-1, 0, 1),
    (0, 1, 1), (0, -1, -1), (0, 1, -1), (0, -1, 1),
]
OPP = [DIRS.index((-a, -b, -c)) for a, b, c in DIRS]
MIRROR_Y = [DIRS.index((a, -b, c)) for a, b, c in DIRS]
MIRROR_Z = [DIRS.index((a, b, -c)) for a, b, c in DIRS]
INLET = 0.05

Z_EDGE = [i for i in range(19) if DIRS[i][2] == 0] + [i for i in range(19) if DIRS[i][2] == 1]
Z_SECOND = [i for i in range(19) if DIRS[i][2] == 1]
Y_EDGE = [i for i in range(19) if DIRS[i][1] == 0] + [i for i in range(19) if DIRS[i][1] == 1]
Y_SECOND = [i for i in range(19) if DIRS[i][1] == 1]

ROW_SOLID = 76
ROW_PARAM = 80
ROW_NOISE = 88
PAD = 8
VMEM_BYTES = 48 * 1024 * 1024


def taps():
    k = np.arange(-HW, HW + 1).astype(np.float64)
    raw = np.exp(-math.pi * k * k / (2.0 * (HW // 2) ** 2))
    return raw / np.sqrt(np.sum(raw * raw))


def band(source, target):
    values = taps()
    offset = np.asarray(source)[:, None] - np.asarray(target)[None, :]
    inside = np.abs(offset) <= HW
    return np.where(inside, values[np.clip(offset + HW, 0, 2 * HW)], 0.0).astype(np.float32)


def moments(g):
    s = {a: g[a] + g[a + 1] for a in range(1, 19, 2)}
    d = {a: g[a] - g[a + 1] for a in range(1, 19, 2)}
    w1, w2 = 1.0 / 18.0, 1.0 / 36.0
    rho = (
        g[0] * (1.0 / 3.0)
        + (s[1] + s[3] + s[5]) * w1
        + ((s[7] + s[9]) + (s[11] + s[13]) + (s[15] + s[17])) * w2
    )
    mx = d[1] * w1 + ((d[7] + d[9]) + (d[11] + d[13])) * w2
    my = d[3] * w1 + ((d[7] - d[9]) + (d[15] + d[17])) * w2
    mz = d[5] * w1 + ((d[11] - d[13]) + (d[15] - d[17])) * w2
    return rho, mx, my, mz


def pair_vector(a, vx, vy, vz):
    total = None
    for c, v in zip(DIRS[a], (vx, vy, vz)):
        if c:
            term = v if c > 0 else -v
            total = term if total is None else (total + v if c > 0 else total - v)
    return total


def collide(g, solid, keep=range(19)):
    rho, mx, my, mz = moments(g)
    inv = 1.0 / rho
    ux, uy, uz = mx * inv, my * inv, mz * inv
    square = mx * ux + my * uy + mz * uz
    base = 1.25 * rho - 1.875 * square
    post = [None] * 19
    if 0 in keep:
        post[0] = jnp.where(solid, g[0], base - 0.25 * g[0])
    for a in range(1, 19, 2):
        if a not in keep and a + 1 not in keep:
            continue
        m = pair_vector(a, mx, my, mz)
        p = pair_vector(a, ux, uy, uz)
        even = base + 5.625 * (m * p)
        odd = 3.75 * m
        if a in keep:
            post[a] = jnp.where(solid, g[a + 1], (even + odd) - 0.25 * g[a])
        if a + 1 in keep:
            post[a + 1] = jnp.where(solid, g[a], (even - odd) - 0.25 * g[a + 1])
    return post


def inlet_state(ux, uy, uz):
    base = 1.0 - 1.5 * (ux * ux + uy * uy + uz * uz)
    out = [base] * 19
    for a in range(1, 19, 2):
        p = pair_vector(a, ux, uy, uz)
        even = base + 4.5 * (p * p)
        odd = 3.0 * p
        out[a] = even + odd
        out[a + 1] = even - odd
    return out


def wall_rows(first_row, height, kz, nz):
    rows = lax.broadcasted_iota(jnp.int32, (8, 128), 0) + first_row
    return ((rows == 0) & (kz == 0)) | ((rows == height - 1) & (kz == nz - 1))


def edge_kernel(nz, pops, mask, noise, mean, diag, off, za, zb, z2, edge):
    height = pops.shape[2]
    kz = lax.axis_index("gz")
    upward = lax.rem(kz, 2) == 0
    for part, row in ((0, 0), (1, height - 8)):
        wall = wall_rows(row, height, kz, nz)
        for x in range(4):
            solid = (mask[x, row : row + 8, :] == 1) | wall
            post = collide([pops[i, x, row : row + 8, :] for i in range(19)], solid)
            for i in range(19):
                edge[i, x, 8 * part : 8 * part + 8, :] = post[i]
            edge[19, x, 8 * part : 8 * part + 8, :] = solid.astype(jnp.float32)

    def put(row, up, down):
        za[row : row + 1, :] = jnp.where(upward, up, down)
        zb[row : row + 1, :] = jnp.where(upward, down, up)

    q = 0
    for i in Z_EDGE:
        for x in range(4):
            put(4 * q + x, edge[i, x, 15:16, :], edge[MIRROR_Z[i], x, 0:1, :])
        q += 1
    for i in Z_SECOND:
        for x in range(4):
            put(4 * q + x, edge[i, x, 14:15, :], edge[MIRROR_Z[i], x, 1:2, :])
        q += 1
    for x in range(4):
        put(4 * q + x, edge[19, x, 15:16, :], edge[19, x, 0:1, :])
    for ref in (za, zb):
        ref[ROW_PARAM : ROW_PARAM + 8, :] = jnp.zeros((8, 128), jnp.float32)
        ref[ROW_PARAM : ROW_PARAM + 1, 0:height] = mean[...]
        ref[ROW_PARAM + 1 : ROW_PARAM + 4, 0:height] = diag[...]
        ref[ROW_PARAM + 4 : ROW_PARAM + 7, 0:height] = off[...]
        for c in range(3):
            ref[ROW_NOISE + height * c : ROW_NOISE + height * (c + 1), :] = noise[c]
    low_half = lax.rem(kz, 4) < 2
    z2[...] = jnp.zeros((16, 128), jnp.float32)
    for c in range(3):
        last = noise[c, height - 1 : height, :]
        first = noise[c, 0:1, :]
        z2[c : c + 1, :] = jnp.where(low_half, last, first)
        z2[8 + c : 9 + c, :] = jnp.where(low_half, first, last)


def column_kernel(
    nz, ny, pops, mask, noise, sent, za, zb, z2c, z2d, bandz,
    post, solidp, ya, yb, linear, meanrow,
    wide, filt,
):
    height = pops.shape[2]
    rows = height + 2 * PAD
    kz = lax.axis_index("gz")
    ky = lax.axis_index("gy") * lax.axis_size("col") + lax.axis_index("col")
    z_even = lax.rem(kz, 2) == 0
    y_even = lax.rem(ky, 2) == 0
    low_half = lax.rem(kz, 4) < 2

    def body(t, carry):
        row = pl.multiple_of(t * 8, 8)
        wall = wall_rows(row, height, kz, nz)
        for x in range(4):
            solid = (mask[x, pl.ds(row, 8), :] == 1) | wall
            p = collide([pops[i, x, pl.ds(row, 8), :] for i in range(19)], solid)
            for i in range(19):
                post[i, x, pl.ds(row + PAD, 8), :] = p[i]
            solidp[x, pl.ds(row + PAD, 8), :] = solid.astype(jnp.float32)
        return carry

    lax.fori_loop(0, height // 8, body, 0)

    def below(row, n=1):
        return jnp.where(z_even, zb[row : row + n, :], za[row : row + n, :])

    def above(row, n=1):
        return jnp.where(z_even, za[row : row + n, :], zb[row : row + n, :])

    top = PAD + height
    q = 0
    for i in Z_EDGE:
        for x in range(4):
            post[i, x, PAD - 1 : PAD, :] = below(4 * q + x)
            post[MIRROR_Z[i], x, top : top + 1, :] = above(4 * q + x)
        q += 1
    for i in Z_SECOND:
        for x in range(4):
            post[i, x, PAD - 2 : PAD - 1, :] = below(4 * q + x)
            post[MIRROR_Z[i], x, top + 1 : top + 2, :] = above(4 * q + x)
        q += 1
    for x in range(4):
        solidp[x, PAD - 1 : PAD, :] = below(4 * q + x)
        solidp[x, top : top + 1, :] = above(4 * q + x)

    lane = lax.broadcasted_iota(jnp.int32, (8, 128), 1)
    own_par = pltpu.roll(sent[ROW_PARAM : ROW_PARAM + 8, :], PAD, 1)
    low_par = pltpu.roll(below(ROW_PARAM, 8), 128 - height + PAD, 1)
    high_par = pltpu.roll(above(ROW_PARAM, 8), height + PAD, 1)
    par = jnp.where(lane < PAD, low_par, jnp.where(lane < top, own_par, high_par))
    par = jnp.where(lane < rows, par, 0.0)
    meanrow[...] = par
    cols = jnp.transpose(jnp.concatenate([par] * 16, axis=0))[0:rows]

    for c in range(3):
        lanes = slice(128 * c, 128 * c + 128)
        wide[0:height, lanes] = below(ROW_NOISE + height * c, height)
        wide[height : 2 * height, lanes] = noise[c]
        wide[2 * height : 3 * height, lanes] = above(ROW_NOISE + height * c, height)
    filt[...] = jnp.dot(
        bandz[...], wide[...], precision=lax.Precision.HIGHEST, preferred_element_type=jnp.float32
    )
    b_end = float(taps()[0])
    far_low = jnp.where(low_half, z2d[8:16, :], z2c[0:8, :])
    far_high = jnp.where(low_half, z2c[0:8, :], z2d[8:16, :])
    for c in range(3):
        lanes = slice(128 * c, 128 * c + 128)
        filt[PAD - 1 : PAD, lanes] += b_end * far_low[c : c + 1, :]
        filt[top : top + 1, lanes] += b_end * far_high[c : c + 1, :]
    f0, f1, f2 = (filt[:, 128 * c : 128 * c + 128] for c in range(3))
    linear[0] = cols[:, 1:2] * f0
    linear[1] = cols[:, 4:5] * f0 + cols[:, 2:3] * f1
    linear[2] = cols[:, 5:6] * f0 + cols[:, 6:7] * f1 + cols[:, 3:4] * f2
    linear[3] = jnp.broadcast_to(cols[:, 0:1], (rows, 128))

    def edges(t, carry):
        row = pl.multiple_of(t * 8, 8)
        right = jnp.zeros((8, 128), jnp.float32)
        left = jnp.zeros((8, 128), jnp.float32)
        k = 0
        for items, depth in ((Y_EDGE, 0), (Y_SECOND, 1)):
            for i in items:
                for x in range(4):
                    vr = post[i, x, pl.ds(row, 8), :]
                    vl = post[MIRROR_Y[i], x, pl.ds(row, 8), :]
                    right = jnp.where(lane == k, pltpu.roll(vr, (k - (127 - depth)) % 128, 1), right)
                    left = jnp.where(lane == k, pltpu.roll(vl, (k - depth) % 128, 1), left)
                    k += 1
        for x in range(4):
            v = solidp[x, pl.ds(row, 8), :]
            right = jnp.where(lane == k, pltpu.roll(v, (k - 127) % 128, 1), right)
            left = jnp.where(lane == k, pltpu.roll(v, k, 1), left)
            k += 1
        for c in range(3):
            v = linear[c, pl.ds(row, 8), :]
            right = jnp.where(lane == k, pltpu.roll(v, (k - 63) % 128, 1), right)
            left = jnp.where(lane == k, pltpu.roll(v, (k - 64) % 128, 1), left)
            k += 1
        ya[pl.ds(row, 8), :] = jnp.where(y_even, right, left)
        yb[pl.ds(row, 8), :] = jnp.where(y_even, left, right)
        return carry

    lax.fori_loop(0, rows // 8, edges, 0)
    half = rows // 2
    lane_h = lax.broadcasted_iota(jnp.int32, (half, 128), 1)
    for c in range(3):
        first, second = linear[c, 0:half, :], linear[c, half:rows, :]
        left = jnp.where(lane_h < 64, first, pltpu.roll(second, 64, 1))
        right = jnp.where(lane_h < 64, pltpu.roll(first, 64, 1), second)
        at = slice(rows + half * c, rows + half * (c + 1))
        ya[at, :] = jnp.where(y_even, right, left)
        yb[at, :] = jnp.where(y_even, left, right)


def final_kernel(
    nz, ny, post, solidp, linear, meanrow, sa, sb, ya, yb, wy, wg,
    inflow, state,
    lhs, flow, post2, strip_l, strip_r, own_l, own_r, sx_l, sx_r, ghosts, ghost_cols, tl, tr,
):
    height = state.shape[2]
    rows = height + 2 * PAD
    half = rows // 2
    top = PAD + height
    kz = lax.axis_index("gz")
    ky = lax.axis_index("gy") * lax.axis_size("col") + lax.axis_index("col")
    y_even = lax.rem(ky, 2) == 0
    lane = lax.broadcasted_iota(jnp.int32, (8, 128), 1)
    sub = lax.broadcasted_iota(jnp.int32, (8, 128), 0)

    tl[0:rows, :] = jnp.where(y_even, yb[0:rows, :], ya[0:rows, :])
    tr[0:rows, :] = jnp.where(y_even, ya[0:rows, :], yb[0:rows, :])
    fill = jnp.zeros((128 - rows, 128), jnp.float32)
    strip_l[...] = jnp.transpose(jnp.concatenate([tl[0:rows, :], fill], axis=0))
    strip_r[...] = jnp.transpose(jnp.concatenate([tr[0:rows, :], fill], axis=0))
    mine_right = jnp.where(y_even, sa[0:rows, :], sb[0:rows, :])
    mine_left = jnp.where(y_even, sb[0:rows, :], sa[0:rows, :])
    own_l[...] = jnp.transpose(jnp.concatenate([mine_left, fill], axis=0))
    own_r[...] = jnp.transpose(jnp.concatenate([mine_right, fill], axis=0))

    lane_h = lax.broadcasted_iota(jnp.int32, (half, 128), 1)
    for c in range(3):
        at = slice(rows + half * c, rows + half * (c + 1))
        a, b = ya[at, :], yb[at, :]
        left, right = jnp.where(y_even, b, a), jnp.where(y_even, a, b)
        lo, hi = slice(rows * c, rows * c + half), slice(rows * c + half, rows * (c + 1))
        lhs[rows * c : rows * (c + 1), 0:128] = linear[c]
        lhs[lo, 128:256] = jnp.where(lane_h < 64, left, 0.0)
        lhs[hi, 128:256] = jnp.where(lane_h < 64, 0.0, left)
        lhs[lo, 256:384] = jnp.where(lane_h < 64, right, 0.0)
        lhs[hi, 256:384] = jnp.where(lane_h < 64, 0.0, right)
    prod = jnp.dot(
        lhs[...], wy[...], precision=lax.Precision.HIGHEST, preferred_element_type=jnp.float32
    )
    flow[...] = prod
    flow[0:rows, :] = prod[0:rows] + linear[3]
    for c in range(3):
        inflow[c] = flow[rows * c + PAD : rows * c + top, :]
    b_end = float(taps()[0])
    ghost_flow = []
    for c in range(3):
        g = lax.dot_general(
            wg[...],
            lhs[rows * c : rows * (c + 1), :],
            (((1,), (1,)), ((), ())),
            precision=lax.Precision.HIGHEST,
            preferred_element_type=jnp.float32,
        )
        g = jnp.concatenate([g, jnp.zeros((8, 128 - rows), jnp.float32)], axis=1)
        at_l = g[0:1, :] + b_end * strip_l[80 + c : 81 + c, :]
        at_r = g[1:2, :] + b_end * strip_r[80 + c : 81 + c, :]
        if c == 0:
            at_l = at_l + meanrow[0:1, :]
            at_r = at_r + meanrow[0:1, :]
        ghost_flow.append((at_l, at_r))

    outside = ((lane < PAD) & (kz == 0)) | ((lane >= top) & (kz == nz - 1))
    ghosts[...] = jnp.zeros((128, 128), jnp.float32)
    for side, (got, own, sx, edge_items) in enumerate(
        ((strip_l, own_l, sx_l, False), (strip_r, own_r, sx_r, True))
    ):
        mirror = (lambda i: MIRROR_Y[i]) if edge_items else (lambda i: i)
        solid = got[76:84, :] > 0.5
        g = [None] * 19
        for i in range(19):
            j = mirror(i)
            cx, cy, cz = DIRS[i]
            if DIRS[j][1] == 0:
                q, src = Y_EDGE.index(j), got
            elif DIRS[j][1] == 1:
                q, src = len(Y_EDGE) + Y_SECOND.index(j), got
            else:
                q, src = Y_EDGE.index(MIRROR_Y[j]), own
            v = src[4 * q : 4 * q + 4, :]
            if cx == 0:
                w = src[4 * q : 4 * q + 8, :]
            else:
                sx[0:1, :] = jnp.zeros((1, 128), jnp.float32)
                sx[1:5, :] = v
                sx[5:6, :] = v[3:4, :]
                w = sx[1 - cx : 9 - cx, :]
            g[i] = w if cz == 0 else pltpu.roll(w, cz % 128, 1)
        us = [INLET * jnp.broadcast_to(ghost_flow[c][side], (8, 128)) for c in range(3)]
        eq = inlet_state(*us)
        put = (sub == 0) & jnp.logical_not(solid)
        g = [jnp.where(put, eq[i], g[i]) for i in range(19)]
        keep = [i for i in range(19) if DIRS[mirror(i)][1] == 1]
        p = collide(g, solid, keep)
        for n, i in enumerate(Y_SECOND):
            value = jnp.where(outside, 0.0, p[mirror(i)])
            at = 32 * side + 4 * n
            ghosts[at : at + 4, :] = value[0:4, :]
    ghost_cols[0:128, :] = jnp.transpose(ghosts[...])

    def gather(src, i, x, row, from_left, from_right):
        cx, cy, cz = DIRS[i]
        sxx = x - cx
        if sxx < 0:
            return jnp.zeros((8, 128), jnp.float32)
        sxx = min(sxx, 3)
        v = src[i, sxx, pl.ds(row - cz, 8), :]
        if cy == 0:
            return v
        v = pltpu.roll(v, cy % 128, 1)
        if cy == 1:
            cols, k = from_left(i, sxx)
            ghost = pltpu.roll(cols[pl.ds(row - cz, 8), :], (-k) % 128, 1)
            return jnp.where(lane == 0, ghost, v)
        cols, k = from_right(i, sxx)
        ghost = pltpu.roll(cols[pl.ds(row - cz, 8), :], (127 - k) % 128, 1)
        return jnp.where(lane == 127, ghost, v)

    def first_left(i, x):
        return tl, 4 * Y_EDGE.index(i) + x

    def first_right(i, x):
        return tr, 4 * Y_EDGE.index(MIRROR_Y[i]) + x

    def second_left(i, x):
        return ghost_cols, 4 * Y_SECOND.index(i) + x

    def second_right(i, x):
        return ghost_cols, 32 + 4 * Y_SECOND.index(MIRROR_Y[i]) + x

    def step_one(row, store_row, outside_rows):
        us = [INLET * flow[pl.ds(rows * c + row, 8), :] for c in range(3)]
        eq = inlet_state(*us)
        for x in range(4):
            solid = solidp[x, pl.ds(row, 8), :] > 0.5
            g = [gather(post, i, x, row, first_left, first_right) for i in range(19)]
            if x == 0:
                g = [jnp.where(solid, g[i], eq[i]) for i in range(19)]
            p = collide(g, solid)
            for i in range(19):
                value = p[i]
                if outside_rows is not None:
                    value = jnp.where(outside_rows, 0.0, value)
                post2[i, x, pl.ds(store_row, 8), :] = value

    step_one(PAD - 1, PAD - 1, (sub == 0) & (kz == 0))
    step_one(top - 7, top - 7, (sub == 7) & (kz == nz - 1))

    def main(t, carry):
        row = pl.multiple_of(t * 8 + PAD, 8)
        step_one(row, row, None)
        return carry

    lax.fori_loop(0, height // 8, main, 0)

    def last(t, carry):
        row = pl.multiple_of(t * 8 + PAD, 8)
        us = [INLET * flow[pl.ds(rows * c + row, 8), :] for c in range(3)]
        eq = inlet_state(*us)
        for x in range(4):
            solid = solidp[x, pl.ds(row, 8), :] > 0.5
            for i in range(19):
                g = gather(post2, i, x, row, second_left, second_right)
                if x == 0:
                    g = jnp.where(solid, g, eq[i])
                state[i, x, pl.ds(row - PAD, 8), :] = g
        return carry

    lax.fori_loop(0, height // 8, last, 0)


def swap_pairs(count, phase, distance=1):
    pairs = []
    for i in range(count):
        block = (i + phase * distance) // distance
        j = i + distance if block % 2 == 0 else i - distance
        if 0 <= j < count:
            pairs.append((i, j))
    return pairs


def ring_pairs(count, phase):
    if phase == 0:
        return [(i, i ^ 1) for i in range(count)]
    return [(i, (((i + 1) % count ^ 1) - 1) % count) for i in range(count)]


def vm(n):
    return [pl.BlockSpec(memory_space=pltpu.VMEM)] * n


def f32(*shape):
    return jax.ShapeDtypeStruct(shape, jnp.float32)


def scratch(*shape):
    return pltpu.VMEM(shape, jnp.float32)


def shards(nz, ny, noise, mean_profile, lund_diag, lund_off, populations, mask):
    height, span = noise.shape[1], noise.shape[2]
    rows = height + 2 * PAD
    params = pltpu.CompilerParams(vmem_limit_bytes=VMEM_BYTES)
    message = ROW_NOISE + 3 * height

    za, zb, z2 = pl.pallas_call(
        lambda *refs: edge_kernel(nz, *refs),
        out_shape=(f32(message, 128), f32(message, 128), f32(16, 128)),
        in_specs=vm(6),
        out_specs=vm(3),
        scratch_shapes=[scratch(20, 4, 16, 128)],
        compiler_params=params,
        name="edge_rows",
    )(populations, mask, noise, mean_profile.reshape(1, height), lund_diag, lund_off)

    ra = lax.ppermute(za, "gz", swap_pairs(nz, 0))
    rb = lax.ppermute(zb, "gz", swap_pairs(nz, 1))
    rc = lax.ppermute(z2, "gz", swap_pairs(nz, 0, 2))
    far = swap_pairs(nz, 1, 2)
    far = [pair for pair in far if abs(pair[0] - pair[1]) == 2]
    rd = lax.ppermute(z2, "gz", far) if far else jnp.zeros_like(z2)

    line = np.arange(rows) - PAD
    used = (line >= -1) & (line <= height)
    bandz = np.where(used[:, None], band(np.arange(-height, 2 * height), line).T, 0.0)
    post, solidp, ya, yb, linear, meanrow = pl.pallas_call(
        lambda *refs: column_kernel(nz, ny, *refs),
        out_shape=(
            f32(19, 4, rows, 128), f32(4, rows, 128), f32(rows + 3 * rows // 2, 128),
            f32(rows + 3 * rows // 2, 128), f32(4, rows, 128), f32(8, 128),
        ),
        in_specs=vm(9),
        out_specs=vm(6),
        scratch_shapes=[scratch(3 * height, 384), scratch(rows, 384)],
        compiler_params=params,
        name="columns",
    )(populations, mask, noise, za, ra, rb, rc, rd, jnp.asarray(bandz, jnp.float32))

    qa = lax.ppermute(ya, ("gy", "col"), ring_pairs(ny, 0))
    qb = lax.ppermute(yb, ("gy", "col"), ring_pairs(ny, 1))

    own = np.arange(span)
    left = np.arange(128) % 64 - 64
    right = np.arange(128) % 64 + span
    source = np.concatenate([own, left, right])
    wy = band(source, own)
    wg = np.zeros((8, 384), np.float32)
    wg[0:2] = band(source, np.array([-1, span])).T
    inflow, state = pl.pallas_call(
        lambda *refs: final_kernel(nz, ny, *refs),
        out_shape=(f32(3, height, span), f32(19, 4, height, span)),
        in_specs=vm(10),
        out_specs=vm(2),
        scratch_shapes=[
            scratch(3 * rows, 384), scratch(3 * rows, 128), scratch(19, 4, rows, 128),
            scratch(128, 128), scratch(128, 128), scratch(128, 128), scratch(128, 128),
            scratch(16, 128), scratch(16, 128), scratch(128, 128), scratch(128, 128),
            scratch(rows, 128), scratch(rows, 128),
        ],
        compiler_params=params,
        name="stream",
    )(post, solidp, linear, meanrow, ya, yb, qa, qb, jnp.asarray(wy), jnp.asarray(wg))
    return inflow, state


def solution(mesh):
    nz = mesh.shape["gz"]
    ny = mesh.shape["gy"] * mesh.shape["col"]
    in_specs = (
        P(None, "gz", ("gy", "col")),
        P("gz"),
        P(None, "gz"),
        P(None, "gz"),
        P(None, None, "gz", ("gy", "col")),
        P(None, "gz", ("gy", "col")),
    )
    out_specs = (P(None, "gz", ("gy", "col")), P(None, None, "gz", ("gy", "col")))

    def body(*args):
        return shards(nz, ny, *args)

    return jax.shard_map(body, mesh=mesh, in_specs=in_specs, out_specs=out_specs, check_vma=False)
```

```python
import math

import jax
import jax.numpy as jnp
import numpy as np
from jax import lax
from jax.experimental import pallas as pl
from jax.experimental.pallas import tpu as pltpu
from jax.sharding import PartitionSpec as P

HW = 64
DIRS = [
    (0, 0, 0),
    (1, 0, 0), (-1, 0, 0), (0, 1, 0), (0, -1, 0), (0, 0, 1), (0, 0, -1),
    (1, 1, 0), (-1, -1, 0), (1, -1, 0), (-1, 1, 0),
    (1, 0, 1), (-1, 0, -1), (1, 0, -1), (-1, 0, 1),
    (0, 1, 1), (0, -1, -1), (0, 1, -1), (0, -1, 1),
]
OPP = [DIRS.index((-a, -b, -c)) for a, b, c in DIRS]
MIRROR_Y = [DIRS.index((a, -b, c)) for a, b, c in DIRS]
MIRROR_Z = [DIRS.index((a, b, -c)) for a, b, c in DIRS]
INLET = 0.05

Z_EDGE = [i for i in range(19) if DIRS[i][2] == 0] + [i for i in range(19) if DIRS[i][2] == 1]
Z_SECOND = [i for i in range(19) if DIRS[i][2] == 1]
Y_EDGE = [i for i in range(19) if DIRS[i][1] == 0] + [i for i in range(19) if DIRS[i][1] == 1]
Y_SECOND = [i for i in range(19) if DIRS[i][1] == 1]

ROW_SOLID = 76
ROW_PARAM = 80
ROW_NOISE = 88
PAD = 8


def taps():
    k = np.arange(-HW, HW + 1).astype(np.float64)
    raw = np.exp(-math.pi * k * k / (2.0 * (HW // 2) ** 2))
    return raw / np.sqrt(np.sum(raw * raw))


def band(source, target):
    values = taps()
    offset = np.asarray(source)[:, None] - np.asarray(target)[None, :]
    inside = np.abs(offset) <= HW
    return np.where(inside, values[np.clip(offset + HW, 0, 2 * HW)], 0.0).astype(np.float32)


def moments(g):
    s = {a: g[a] + g[a + 1] for a in range(1, 19, 2)}
    d = {a: g[a] - g[a + 1] for a in range(1, 19, 2)}
    w1, w2 = 1.0 / 18.0, 1.0 / 36.0
    rho = (
        g[0] * (1.0 / 3.0)
        + (s[1] + s[3] + s[5]) * w1
        + ((s[7] + s[9]) + (s[11] + s[13]) + (s[15] + s[17])) * w2
    )
    mx = d[1] * w1 + ((d[7] + d[9]) + (d[11] + d[13])) * w2
    my = d[3] * w1 + ((d[7] - d[9]) + (d[15] + d[17])) * w2
    mz = d[5] * w1 + ((d[11] - d[13]) + (d[15] - d[17])) * w2
    return rho, mx, my, mz


def pair_vector(a, vx, vy, vz):
    total = None
    for c, v in zip(DIRS[a], (vx, vy, vz)):
        if c:
            term = v if c > 0 else -v
            total = term if total is None else (total + v if c > 0 else total - v)
    return total


def collide(g, solid, keep=range(19)):
    rho, mx, my, mz = moments(g)
    inv = 1.0 / rho
    ux, uy, uz = mx * inv, my * inv, mz * inv
    square = mx * ux + my * uy + mz * uz
    base = 1.25 * rho - 1.875 * square
    post = [None] * 19
    if 0 in keep:
        post[0] = jnp.where(solid, g[0], base - 0.25 * g[0])
    for a in range(1, 19, 2):
        if a not in keep and a + 1 not in keep:
            continue
        m = pair_vector(a, mx, my, mz)
        p = pair_vector(a, ux, uy, uz)
        even = base + 5.625 * (m * p)
        odd = 3.75 * m
        if a in keep:
            post[a] = jnp.where(solid, g[a + 1], (even + odd) - 0.25 * g[a])
        if a + 1 in keep:
            post[a + 1] = jnp.where(solid, g[a], (even - odd) - 0.25 * g[a + 1])
    return post


def inlet_state(ux, uy, uz):
    base = 1.0 - 1.5 * (ux * ux + uy * uy + uz * uz)
    out = [base] * 19
    for a in range(1, 19, 2):
        p = pair_vector(a, ux, uy, uz)
        even = base + 4.5 * (p * p)
        odd = 3.0 * p
        out[a] = even + odd
        out[a + 1] = even - odd
    return out


def wall_rows(first_row, height, kz, nz):
    rows = lax.broadcasted_iota(jnp.int32, (8, 128), 0) + first_row
    return ((rows == 0) & (kz == 0)) | ((rows == height - 1) & (kz == nz - 1))


def edge_kernel(
    nz, pops, mask, noise, mean, diag, off, za, zb, z2, raw, flags, mean_v, diag_v, off_v, edge, sems
):
    height = pops.shape[2]
    kz = lax.axis_index("gz")
    upward = lax.rem(kz, 2) == 0
    upper = pl.ds(height - 8, 8)
    copies = [
        (pops.at[:, :, 0:8, :], raw.at[:, :, 0:8, :]),
        (pops.at[:, :, upper, :], raw.at[:, :, 8:16, :]),
        (mask.at[:, 0:8, :], flags.at[:, 0:8, :]),
        (mask.at[:, upper, :], flags.at[:, 8:16, :]),
        (mean, mean_v),
        (diag, diag_v),
        (off, off_v),
    ]
    for c in range(3):
        at = slice(ROW_NOISE + height * c, ROW_NOISE + height * (c + 1))
        copies.append((noise.at[c], za.at[at, :]))
        copies.append((noise.at[c], zb.at[at, :]))
    copies = [pltpu.make_async_copy(src, dst, sems.at[n]) for n, (src, dst) in enumerate(copies)]
    for copy in copies:
        copy.start()
    for copy in copies[:4]:
        copy.wait()
    for part, row in ((0, 0), (1, height - 8)):
        wall = wall_rows(row, height, kz, nz)
        at = slice(8 * part, 8 * part + 8)
        for x in range(4):
            solid = (flags[x, at, :] == 1) | wall
            post = collide([raw[i, x, at, :] for i in range(19)], solid)
            for i in range(19):
                edge[i, x, at, :] = post[i]
            edge[19, x, at, :] = solid.astype(jnp.float32)

    def put(row, up, down):
        za[row : row + 1, :] = jnp.where(upward, up, down)
        zb[row : row + 1, :] = jnp.where(upward, down, up)

    q = 0
    for i in Z_EDGE:
        for x in range(4):
            put(4 * q + x, edge[i, x, 15:16, :], edge[MIRROR_Z[i], x, 0:1, :])
        q += 1
    for i in Z_SECOND:
        for x in range(4):
            put(4 * q + x, edge[i, x, 14:15, :], edge[MIRROR_Z[i], x, 1:2, :])
        q += 1
    for x in range(4):
        put(4 * q + x, edge[19, x, 15:16, :], edge[19, x, 0:1, :])
    for copy in copies[4:]:
        copy.wait()
    for ref in (za, zb):
        ref[ROW_PARAM : ROW_PARAM + 8, :] = jnp.zeros((8, 128), jnp.float32)
        ref[ROW_PARAM : ROW_PARAM + 1, 0:height] = mean_v[...]
        ref[ROW_PARAM + 1 : ROW_PARAM + 4, 0:height] = diag_v[...]
        ref[ROW_PARAM + 4 : ROW_PARAM + 7, 0:height] = off_v[...]
    low_half = lax.rem(kz, 4) < 2
    z2[...] = jnp.zeros((16, 128), jnp.float32)
    for c in range(3):
        base = ROW_NOISE + height * c
        last = za[base + height - 1 : base + height, :]
        first = za[base : base + 1, :]
        z2[c : c + 1, :] = jnp.where(low_half, last, first)
        z2[8 + c : 9 + c, :] = jnp.where(low_half, first, last)


def pick(lane, k, value, column, into):
    return jnp.where(lane == k, pltpu.roll(value, (k - column) % 128, 1), into)


def bulk_kernel(nz, pops, mask, post, solidp, right_cols, left_cols, raw, flags, sems):
    height = pops.shape[2]
    kz = lax.axis_index("gz")
    lane = lax.broadcasted_iota(jnp.int32, (8, 128), 1)
    copies = [pltpu.make_async_copy(mask, flags, sems.at[4])]
    copies += [
        pltpu.make_async_copy(pops.at[:, x], raw.at[:, x], sems.at[x]) for x in range(4)
    ]
    for copy in copies:
        copy.start()
    copies[0].wait()
    for x in range(4):
        copies[1 + x].wait()

        def body(t, carry):
            row = pl.multiple_of(t * 8, 8)
            out = pl.ds(row + PAD, 8)
            solid = (flags[x, pl.ds(row, 8), :] == 1) | wall_rows(row, height, kz, nz)
            p = collide([raw[i, x, pl.ds(row, 8), :] for i in range(19)], solid)
            for i in range(19):
                post[i, x, out, :] = p[i]
            flag = solid.astype(jnp.float32)
            solidp[x, out, :] = flag
            if x == 0:
                right = left = jnp.zeros((8, 128), jnp.float32)
            else:
                right, left = right_cols[out, :], left_cols[out, :]
            q = 0
            for items, depth in ((Y_EDGE, 0), (Y_SECOND, 1)):
                for i in items:
                    right = pick(lane, 4 * q + x, p[i], 127 - depth, right)
                    left = pick(lane, 4 * q + x, p[MIRROR_Y[i]], depth, left)
                    q += 1
            right_cols[out, :] = pick(lane, 4 * q + x, flag, 127, right)
            left_cols[out, :] = pick(lane, 4 * q + x, flag, 0, left)
            return carry

        lax.fori_loop(0, height // 8, body, 0)


def column_kernel(
    nz, post_in, solid_in, right_in, left_in, sent, za, zb, z2c, z2d, bandz,
    post, solidp, ya, yb, linear, meanrow,
    wide, filt,
):
    height = post.shape[2] - 2 * PAD
    rows = height + 2 * PAD
    kz = lax.axis_index("gz")
    ky = lax.axis_index("gy") * lax.axis_size("col") + lax.axis_index("col")
    z_even = lax.rem(kz, 2) == 0
    y_even = lax.rem(ky, 2) == 0
    low_half = lax.rem(kz, 4) < 2

    def below(row, n=1):
        return jnp.where(z_even, zb[row : row + n, :], za[row : row + n, :])

    def above(row, n=1):
        return jnp.where(z_even, za[row : row + n, :], zb[row : row + n, :])

    top = PAD + height
    q = 0
    for i in Z_EDGE:
        for x in range(4):
            post[i, x, PAD - 1 : PAD, :] = below(4 * q + x)
            post[MIRROR_Z[i], x, top : top + 1, :] = above(4 * q + x)
        q += 1
    for i in Z_SECOND:
        for x in range(4):
            post[i, x, PAD - 2 : PAD - 1, :] = below(4 * q + x)
            post[MIRROR_Z[i], x, top + 1 : top + 2, :] = above(4 * q + x)
        q += 1
    for x in range(4):
        solidp[x, PAD - 1 : PAD, :] = below(4 * q + x)
        solidp[x, top : top + 1, :] = above(4 * q + x)

    lane = lax.broadcasted_iota(jnp.int32, (8, 128), 1)
    own_par = pltpu.roll(sent[ROW_PARAM : ROW_PARAM + 8, :], PAD, 1)
    low_par = pltpu.roll(below(ROW_PARAM, 8), 128 - height + PAD, 1)
    high_par = pltpu.roll(above(ROW_PARAM, 8), height + PAD, 1)
    par = jnp.where(lane < PAD, low_par, jnp.where(lane < top, own_par, high_par))
    par = jnp.where(lane < rows, par, 0.0)
    meanrow[...] = par
    cols = jnp.transpose(jnp.concatenate([par] * 16, axis=0))[0:rows]

    for c in range(3):
        lanes = slice(128 * c, 128 * c + 128)
        at = slice(ROW_NOISE + height * c, ROW_NOISE + height * (c + 1))
        wide[0:height, lanes] = below(ROW_NOISE + height * c, height)
        wide[height : 2 * height, lanes] = sent[at, :]
        wide[2 * height : 3 * height, lanes] = above(ROW_NOISE + height * c, height)
    filt[...] = jnp.dot(
        bandz[...], wide[...], precision=lax.Precision.HIGHEST, preferred_element_type=jnp.float32
    )
    b_end = float(taps()[0])
    far_low = jnp.where(low_half, z2d[8:16, :], z2c[0:8, :])
    far_high = jnp.where(low_half, z2c[0:8, :], z2d[8:16, :])
    for c in range(3):
        lanes = slice(128 * c, 128 * c + 128)
        filt[PAD - 1 : PAD, lanes] += b_end * far_low[c : c + 1, :]
        filt[top : top + 1, lanes] += b_end * far_high[c : c + 1, :]
    f0, f1, f2 = (filt[:, 128 * c : 128 * c + 128] for c in range(3))
    linear[0] = cols[:, 1:2] * f0
    linear[1] = cols[:, 4:5] * f0 + cols[:, 2:3] * f1
    linear[2] = cols[:, 5:6] * f0 + cols[:, 6:7] * f1 + cols[:, 3:4] * f2
    linear[3] = jnp.broadcast_to(cols[:, 0:1], (rows, 128))

    for row in range(0, rows, 8):
        out = slice(row, row + 8)
        if row == 0 or row == rows - 8:
            right = left = jnp.zeros((8, 128), jnp.float32)
            k = 0
            for items, depth in ((Y_EDGE, 0), (Y_SECOND, 1)):
                for i in items:
                    for x in range(4):
                        right = pick(lane, k, post[i, x, out, :], 127 - depth, right)
                        left = pick(lane, k, post[MIRROR_Y[i], x, out, :], depth, left)
                        k += 1
            for x in range(4):
                right = pick(lane, k, solidp[x, out, :], 127, right)
                left = pick(lane, k, solidp[x, out, :], 0, left)
                k += 1
        else:
            right, left = right_in[out, :], left_in[out, :]
        for c in range(3):
            v = linear[c, out, :]
            right = pick(lane, 80 + c, v, 63, right)
            left = pick(lane, 80 + c, v, 64, left)
        ya[out, :] = jnp.where(y_even, right, left)
        yb[out, :] = jnp.where(y_even, left, right)
    half = rows // 2
    lane_h = lax.broadcasted_iota(jnp.int32, (half, 128), 1)
    for c in range(3):
        first, second = linear[c, 0:half, :], linear[c, half:rows, :]
        left = jnp.where(lane_h < 64, first, pltpu.roll(second, 64, 1))
        right = jnp.where(lane_h < 64, pltpu.roll(first, 64, 1), second)
        at = slice(rows + half * c, rows + half * (c + 1))
        ya[at, :] = jnp.where(y_even, right, left)
        yb[at, :] = jnp.where(y_even, left, right)


def final_kernel(
    nz, post, solidp, linear, meanrow, sa, sb, ya, yb, wy, wg,
    inflow, state_out,
    lhs, flow, post2, strip_l, strip_r, own_l, own_r, sx_l, sx_r, ghosts, ghost_cols, tl, tr,
    state, flow_own, sems,
):
    height = state.shape[2]
    rows = height + 2 * PAD
    half = rows // 2
    top = PAD + height
    kz = lax.axis_index("gz")
    ky = lax.axis_index("gy") * lax.axis_size("col") + lax.axis_index("col")
    y_even = lax.rem(ky, 2) == 0
    lane = lax.broadcasted_iota(jnp.int32, (8, 128), 1)
    sub = lax.broadcasted_iota(jnp.int32, (8, 128), 0)

    tl[0:rows, :] = jnp.where(y_even, yb[0:rows, :], ya[0:rows, :])
    tr[0:rows, :] = jnp.where(y_even, ya[0:rows, :], yb[0:rows, :])
    fill = jnp.zeros((128 - rows, 128), jnp.float32)
    strip_l[...] = jnp.transpose(jnp.concatenate([tl[0:rows, :], fill], axis=0))
    strip_r[...] = jnp.transpose(jnp.concatenate([tr[0:rows, :], fill], axis=0))
    mine_right = jnp.where(y_even, sa[0:rows, :], sb[0:rows, :])
    mine_left = jnp.where(y_even, sb[0:rows, :], sa[0:rows, :])
    own_l[...] = jnp.transpose(jnp.concatenate([mine_left, fill], axis=0))
    own_r[...] = jnp.transpose(jnp.concatenate([mine_right, fill], axis=0))

    lane_h = lax.broadcasted_iota(jnp.int32, (half, 128), 1)
    for c in range(3):
        at = slice(rows + half * c, rows + half * (c + 1))
        a, b = ya[at, :], yb[at, :]
        left, right = jnp.where(y_even, b, a), jnp.where(y_even, a, b)
        lo, hi = slice(rows * c, rows * c + half), slice(rows * c + half, rows * (c + 1))
        lhs[rows * c : rows * (c + 1), 0:128] = linear[c]
        lhs[lo, 128:256] = jnp.where(lane_h < 64, left, 0.0)
        lhs[hi, 128:256] = jnp.where(lane_h < 64, 0.0, left)
        lhs[lo, 256:384] = jnp.where(lane_h < 64, right, 0.0)
        lhs[hi, 256:384] = jnp.where(lane_h < 64, 0.0, right)
    prod = jnp.dot(
        lhs[...], wy[...], precision=lax.Precision.HIGHEST, preferred_element_type=jnp.float32
    )
    flow[...] = prod
    flow[0:rows, :] = prod[0:rows] + linear[3]
    for c in range(3):
        flow_own[c] = flow[rows * c + PAD : rows * c + top, :]
    flow_copy = pltpu.make_async_copy(flow_own, inflow, sems.at[height // 8])
    flow_copy.start()
    b_end = float(taps()[0])
    ghost_flow = []
    for c in range(3):
        g = lax.dot_general(
            wg[...],
            lhs[rows * c : rows * (c + 1), :],
            (((1,), (1,)), ((), ())),
            precision=lax.Precision.HIGHEST,
            preferred_element_type=jnp.float32,
        )
        g = jnp.concatenate([g, jnp.zeros((8, 128 - rows), jnp.float32)], axis=1)
        at_l = g[0:1, :] + b_end * strip_l[80 + c : 81 + c, :]
        at_r = g[1:2, :] + b_end * strip_r[80 + c : 81 + c, :]
        if c == 0:
            at_l = at_l + meanrow[0:1, :]
            at_r = at_r + meanrow[0:1, :]
        ghost_flow.append((at_l, at_r))

    outside = ((lane < PAD) & (kz == 0)) | ((lane >= top) & (kz == nz - 1))
    ghosts[...] = jnp.zeros((128, 128), jnp.float32)
    for side, (got, own, sx, edge_items) in enumerate(
        ((strip_l, own_l, sx_l, False), (strip_r, own_r, sx_r, True))
    ):
        mirror = (lambda i: MIRROR_Y[i]) if edge_items else (lambda i: i)
        solid = got[76:84, :] > 0.5
        g = [None] * 19
        for i in range(19):
            j = mirror(i)
            cx, cy, cz = DIRS[i]
            if DIRS[j][1] == 0:
                q, src = Y_EDGE.index(j), got
            elif DIRS[j][1] == 1:
                q, src = len(Y_EDGE) + Y_SECOND.index(j), got
            else:
                q, src = Y_EDGE.index(MIRROR_Y[j]), own
            v = src[4 * q : 4 * q + 4, :]
            if cx == 0:
                w = src[4 * q : 4 * q + 8, :]
            else:
                sx[0:1, :] = jnp.zeros((1, 128), jnp.float32)
                sx[1:5, :] = v
                sx[5:6, :] = v[3:4, :]
                w = sx[1 - cx : 9 - cx, :]
            g[i] = w if cz == 0 else pltpu.roll(w, cz % 128, 1)
        us = [INLET * jnp.broadcast_to(ghost_flow[c][side], (8, 128)) for c in range(3)]
        eq = inlet_state(*us)
        put = (sub == 0) & jnp.logical_not(solid)
        g = [jnp.where(put, eq[i], g[i]) for i in range(19)]
        keep = [i for i in range(19) if DIRS[mirror(i)][1] == 1]
        p = collide(g, solid, keep)
        for n, i in enumerate(Y_SECOND):
            value = jnp.where(outside, 0.0, p[mirror(i)])
            at = 32 * side + 4 * n
            ghosts[at : at + 4, :] = value[0:4, :]
    ghost_cols[0:128, :] = jnp.transpose(ghosts[...])

    def gather(src, i, x, row, from_left, from_right):
        cx, cy, cz = DIRS[i]
        sxx = x - cx
        if sxx < 0:
            return jnp.zeros((8, 128), jnp.float32)
        sxx = min(sxx, 3)
        v = src[i, sxx, pl.ds(row - cz, 8), :]
        if cy == 0:
            return v
        v = pltpu.roll(v, cy % 128, 1)
        if cy == 1:
            cols, k = from_left(i, sxx)
            ghost = pltpu.roll(cols[pl.ds(row - cz, 8), :], (-k) % 128, 1)
            return jnp.where(lane == 0, ghost, v)
        cols, k = from_right(i, sxx)
        ghost = pltpu.roll(cols[pl.ds(row - cz, 8), :], (127 - k) % 128, 1)
        return jnp.where(lane == 127, ghost, v)

    def first_left(i, x):
        return tl, 4 * Y_EDGE.index(i) + x

    def first_right(i, x):
        return tr, 4 * Y_EDGE.index(MIRROR_Y[i]) + x

    def second_left(i, x):
        return ghost_cols, 4 * Y_SECOND.index(i) + x

    def second_right(i, x):
        return ghost_cols, 32 + 4 * Y_SECOND.index(MIRROR_Y[i]) + x

    def step_one(row, store_row, outside_rows):
        us = [INLET * flow[pl.ds(rows * c + row, 8), :] for c in range(3)]
        eq = inlet_state(*us)
        for x in range(4):
            solid = solidp[x, pl.ds(row, 8), :] > 0.5
            g = [gather(post, i, x, row, first_left, first_right) for i in range(19)]
            if x == 0:
                g = [jnp.where(solid, g[i], eq[i]) for i in range(19)]
            p = collide(g, solid)
            for i in range(19):
                value = p[i]
                if outside_rows is not None:
                    value = jnp.where(outside_rows, 0.0, value)
                post2[i, x, pl.ds(store_row, 8), :] = value

    step_one(PAD - 1, PAD - 1, (sub == 0) & (kz == 0))
    step_one(top - 7, top - 7, (sub == 7) & (kz == nz - 1))

    def out_copy(t):
        at = pl.ds(pl.multiple_of(t * 8, 8), 8)
        return pltpu.make_async_copy(state.at[:, :, at, :], state_out.at[:, :, at, :], sems.at[t])

    def last(t):
        row = pl.multiple_of(t * 8 + PAD, 8)
        us = [INLET * flow[pl.ds(rows * c + row, 8), :] for c in range(3)]
        eq = inlet_state(*us)
        for x in range(4):
            solid = solidp[x, pl.ds(row, 8), :] > 0.5
            for i in range(19):
                g = gather(post2, i, x, row, second_left, second_right)
                if x == 0:
                    g = jnp.where(solid, g, eq[i])
                state[i, x, pl.ds(row - PAD, 8), :] = g
        out_copy(t).start()

    step_one(PAD, PAD, None)

    def main(t, carry):
        row = pl.multiple_of(t * 8 + PAD, 8)
        step_one(row, row, None)
        last(t - 1)
        return carry

    tiles = height // 8
    lax.fori_loop(1, tiles, main, 0)
    last(tiles - 1)
    for t in range(tiles):
        out_copy(t).wait()
    flow_copy.wait()


def swap_pairs(count, phase, distance=1):
    pairs = []
    for i in range(count):
        block = (i + phase * distance) // distance
        j = i + distance if block % 2 == 0 else i - distance
        if 0 <= j < count:
            pairs.append((i, j))
    return pairs


def ring_pairs(count, phase):
    if phase == 0:
        return [(i, i ^ 1) for i in range(count)]
    return [(i, (((i + 1) % count ^ 1) - 1) % count) for i in range(count)]


def vm(n):
    return [pl.BlockSpec(memory_space=pltpu.VMEM)] * n


def hbm(n):
    return [pl.BlockSpec(memory_space=pltpu.HBM)] * n


def f32(*shape):
    return jax.ShapeDtypeStruct(shape, jnp.float32)


def scratch(*shape):
    return pltpu.VMEM(shape, jnp.float32)


def flags(*shape):
    return pltpu.VMEM(shape, jnp.int32)


def params(mib):
    return pltpu.CompilerParams(vmem_limit_bytes=mib * 1024 * 1024)


def cost(flops, size):
    return pl.CostEstimate(flops=flops, bytes_accessed=size, transcendentals=0)


def shards(nz, ny, noise, mean_profile, lund_diag, lund_off, populations, mask):
    height, span = noise.shape[1], noise.shape[2]
    rows = height + 2 * PAD
    message = ROW_NOISE + 3 * height
    dma = pltpu.SemaphoreType.DMA
    here = lambda value: pltpu.with_memory_space_constraint(value, pltpu.HBM)
    mean_profile = mean_profile.reshape(1, height)
    noise, mean_profile, lund_diag, lund_off, populations, mask = map(
        here, (noise, mean_profile, lund_diag, lund_off, populations, mask)
    )

    za, zb, z2 = pl.pallas_call(
        lambda *refs: edge_kernel(nz, *refs),
        out_shape=(f32(message, 128), f32(message, 128), f32(16, 128)),
        in_specs=hbm(6),
        out_specs=vm(3),
        scratch_shapes=[
            scratch(19, 4, 16, 128), flags(4, 16, 128), scratch(1, height), scratch(3, height),
            scratch(3, height), scratch(20, 4, 16, 128), dma((13,)),
        ],
        compiler_params=params(8),
        name="edge_rows",
    )(populations, mask, noise, mean_profile, lund_diag, lund_off)

    ra = lax.ppermute(za, "gz", swap_pairs(nz, 0))
    rb = lax.ppermute(zb, "gz", swap_pairs(nz, 1))
    rc = lax.ppermute(z2, "gz", swap_pairs(nz, 0, 2))
    far = swap_pairs(nz, 1, 2)
    rd = lax.ppermute(z2, "gz", far) if far else jnp.zeros_like(z2)

    post, solidp, right_cols, left_cols = pl.pallas_call(
        lambda *refs: bulk_kernel(nz, *refs),
        out_shape=(f32(19, 4, rows, 128), f32(4, rows, 128), f32(rows, 128), f32(rows, 128)),
        in_specs=hbm(2),
        out_specs=vm(4),
        scratch_shapes=[scratch(19, 4, height, 128), flags(4, height, 128), dma((5,))],
        compiler_params=params(8),
        cost_estimate=cost(4_000_000_000, 8_000_000),
        name="bulk",
    )(populations, mask)

    line = np.arange(rows) - PAD
    used = (line >= -1) & (line <= height)
    bandz = np.where(used[:, None], band(np.arange(-height, 2 * height), line).T, 0.0)
    post, solidp, ya, yb, linear, meanrow = pl.pallas_call(
        lambda *refs: column_kernel(nz, *refs),
        out_shape=(
            f32(19, 4, rows, 128), f32(4, rows, 128), f32(rows + 3 * rows // 2, 128),
            f32(rows + 3 * rows // 2, 128), f32(4, rows, 128), f32(8, 128),
        ),
        in_specs=vm(10),
        out_specs=vm(6),
        scratch_shapes=[scratch(3 * height, 384), scratch(rows, 384)],
        input_output_aliases={0: 0, 1: 1},
        compiler_params=params(4),
        name="columns",
    )(post, solidp, right_cols, left_cols, za, ra, rb, rc, rd, jnp.asarray(bandz, jnp.float32))

    qa = lax.ppermute(ya, ("gy", "col"), ring_pairs(ny, 0))
    qb = lax.ppermute(yb, ("gy", "col"), ring_pairs(ny, 1))

    own = np.arange(span)
    left = np.arange(128) % 64 - 64
    right = np.arange(128) % 64 + span
    source = np.concatenate([own, left, right])
    wy = band(source, own)
    wg = np.zeros((8, 384), np.float32)
    wg[0:2] = band(source, np.array([-1, span])).T
    inflow, state = pl.pallas_call(
        lambda *refs: final_kernel(nz, *refs),
        out_shape=(f32(3, height, span), f32(19, 4, height, span)),
        in_specs=vm(10),
        out_specs=hbm(2),
        scratch_shapes=[
            scratch(3 * rows, 384), scratch(3 * rows, 128), scratch(19, 4, rows, 128),
            scratch(128, 128), scratch(128, 128), scratch(128, 128), scratch(128, 128),
            scratch(16, 128), scratch(16, 128), scratch(128, 128), scratch(128, 128),
            scratch(rows, 128), scratch(rows, 128), scratch(19, 4, height, span),
            scratch(3, height, span), dma((height // 8 + 1,)),
        ],
        compiler_params=params(12),
        name="stream",
    )(post, solidp, linear, meanrow, ya, yb, qa, qb, jnp.asarray(wy), jnp.asarray(wg))
    return inflow, state


def solution(mesh):
    nz = mesh.shape["gz"]
    ny = mesh.shape["gy"] * mesh.shape["col"]
    in_specs = (
        P(None, "gz", ("gy", "col")),
        P("gz"),
        P(None, "gz"),
        P(None, "gz"),
        P(None, None, "gz", ("gy", "col")),
        P(None, "gz", ("gy", "col")),
    )
    out_specs = (P(None, "gz", ("gy", "col")), P(None, None, "gz", ("gy", "col")))

    def body(*args):
        return shards(nz, ny, *args)

    return jax.shard_map(body, mesh=mesh, in_specs=in_specs, out_specs=out_specs, check_vma=False)
```

```python
import math

import jax
import jax.numpy as jnp
import numpy as np
from jax import lax
from jax.experimental import pallas as pl
from jax.experimental.pallas import tpu as pltpu
from jax.sharding import PartitionSpec as P

HW = 64
DIRS = [
    (0, 0, 0),
    (1, 0, 0), (-1, 0, 0), (0, 1, 0), (0, -1, 0), (0, 0, 1), (0, 0, -1),
    (1, 1, 0), (-1, -1, 0), (1, -1, 0), (-1, 1, 0),
    (1, 0, 1), (-1, 0, -1), (1, 0, -1), (-1, 0, 1),
    (0, 1, 1), (0, -1, -1), (0, 1, -1), (0, -1, 1),
]
OPP = [DIRS.index((-a, -b, -c)) for a, b, c in DIRS]
MIRROR_Y = [DIRS.index((a, -b, c)) for a, b, c in DIRS]
MIRROR_Z = [DIRS.index((a, b, -c)) for a, b, c in DIRS]
INLET = 0.05

Z_EDGE = [i for i in range(19) if DIRS[i][2] == 0] + [i for i in range(19) if DIRS[i][2] == 1]
Z_SECOND = [i for i in range(19) if DIRS[i][2] == 1]
Y_FLAT = [i for i in range(19) if DIRS[i][1] == 0]
Y_PLUS = [i for i in range(19) if DIRS[i][1] == 1]
FLAG_PLANE = 4 * len(Y_FLAT)
LANE_PLUS = 2 * FLAG_PLANE + 8
LANE_FAR = LANE_PLUS + 8 * len(Y_PLUS)

ROW_SOLID = 76
ROW_PARAM = 80
ROW_NOISE = 88
PAD = 8


def taps():
    k = np.arange(-HW, HW + 1).astype(np.float64)
    raw = np.exp(-math.pi * k * k / (2.0 * (HW // 2) ** 2))
    return raw / np.sqrt(np.sum(raw * raw))


def band(source, target):
    values = taps()
    offset = np.asarray(source)[:, None] - np.asarray(target)[None, :]
    inside = np.abs(offset) <= HW
    return np.where(inside, values[np.clip(offset + HW, 0, 2 * HW)], 0.0).astype(np.float32)


def moments(g):
    s = {a: g[a] + g[a + 1] for a in range(1, 19, 2)}
    d = {a: g[a] - g[a + 1] for a in range(1, 19, 2)}
    w1, w2 = 1.0 / 18.0, 1.0 / 36.0
    rho = (
        g[0] * (1.0 / 3.0)
        + (s[1] + s[3] + s[5]) * w1
        + ((s[7] + s[9]) + (s[11] + s[13]) + (s[15] + s[17])) * w2
    )
    mx = d[1] * w1 + ((d[7] + d[9]) + (d[11] + d[13])) * w2
    my = d[3] * w1 + ((d[7] - d[9]) + (d[15] + d[17])) * w2
    mz = d[5] * w1 + ((d[11] - d[13]) + (d[15] - d[17])) * w2
    return rho, mx, my, mz


def pair_vector(a, vx, vy, vz):
    total = None
    for c, v in zip(DIRS[a], (vx, vy, vz)):
        if c:
            term = v if c > 0 else -v
            total = term if total is None else (total + v if c > 0 else total - v)
    return total


def collide(g, solid, keep=range(19)):
    rho, mx, my, mz = moments(g)
    inv = 1.0 / rho
    ux, uy, uz = mx * inv, my * inv, mz * inv
    square = mx * ux + my * uy + mz * uz
    base = 1.25 * rho - 1.875 * square
    post = [None] * 19
    if 0 in keep:
        post[0] = jnp.where(solid, g[0], base - 0.25 * g[0])
    for a in range(1, 19, 2):
        if a not in keep and a + 1 not in keep:
            continue
        m = pair_vector(a, mx, my, mz)
        p = pair_vector(a, ux, uy, uz)
        even = base + 5.625 * (m * p)
        odd = 3.75 * m
        if a in keep:
            post[a] = jnp.where(solid, g[a + 1], (even + odd) - 0.25 * g[a])
        if a + 1 in keep:
            post[a + 1] = jnp.where(solid, g[a], (even - odd) - 0.25 * g[a + 1])
    return post


def inlet_state(ux, uy, uz):
    base = 1.0 - 1.5 * (ux * ux + uy * uy + uz * uz)
    out = [base] * 19
    for a in range(1, 19, 2):
        p = pair_vector(a, ux, uy, uz)
        even = base + 4.5 * (p * p)
        odd = 3.0 * p
        out[a] = even + odd
        out[a + 1] = even - odd
    return out


def wall_rows(first_row, height, kz, nz):
    rows = lax.broadcasted_iota(jnp.int32, (8, 128), 0) + first_row
    return ((rows == 0) & (kz == 0)) | ((rows == height - 1) & (kz == nz - 1))


def edge_kernel(
    nz, pops, mask, noise, mean, diag, off, za, zb, z2, raw, flags, mean_v, diag_v, off_v, edge, sems
):
    height = pops.shape[2]
    kz = lax.axis_index("gz")
    upward = lax.rem(kz, 2) == 0
    upper = pl.ds(height - 8, 8)
    copies = [
        (pops.at[:, :, 0:8, :], raw.at[:, :, 0:8, :]),
        (pops.at[:, :, upper, :], raw.at[:, :, 8:16, :]),
        (mask.at[:, 0:8, :], flags.at[:, 0:8, :]),
        (mask.at[:, upper, :], flags.at[:, 8:16, :]),
        (mean, mean_v),
        (diag, diag_v),
        (off, off_v),
    ]
    for c in range(3):
        at = slice(ROW_NOISE + height * c, ROW_NOISE + height * (c + 1))
        copies.append((noise.at[c], za.at[at, :]))
        copies.append((noise.at[c], zb.at[at, :]))
    copies = [pltpu.make_async_copy(src, dst, sems.at[n]) for n, (src, dst) in enumerate(copies)]
    for copy in copies:
        copy.start()
    for copy in copies[:4]:
        copy.wait()
    for part, row in ((0, 0), (1, height - 8)):
        wall = wall_rows(row, height, kz, nz)
        at = slice(8 * part, 8 * part + 8)
        for x in range(4):
            solid = (flags[x, at, :] == 1) | wall
            post = collide([raw[i, x, at, :] for i in range(19)], solid)
            for i in range(19):
                edge[i, x, at, :] = post[i]
            edge[19, x, at, :] = solid.astype(jnp.float32)

    def put(row, up, down):
        za[row : row + 1, :] = jnp.where(upward, up, down)
        zb[row : row + 1, :] = jnp.where(upward, down, up)

    q = 0
    for i in Z_EDGE:
        for x in range(4):
            put(4 * q + x, edge[i, x, 15:16, :], edge[MIRROR_Z[i], x, 0:1, :])
        q += 1
    for i in Z_SECOND:
        for x in range(4):
            put(4 * q + x, edge[i, x, 14:15, :], edge[MIRROR_Z[i], x, 1:2, :])
        q += 1
    for x in range(4):
        put(4 * q + x, edge[19, x, 15:16, :], edge[19, x, 0:1, :])
    for copy in copies[4:]:
        copy.wait()
    for ref in (za, zb):
        ref[ROW_PARAM : ROW_PARAM + 8, :] = jnp.zeros((8, 128), jnp.float32)
        ref[ROW_PARAM : ROW_PARAM + 1, 0:height] = mean_v[...]
        ref[ROW_PARAM + 1 : ROW_PARAM + 4, 0:height] = diag_v[...]
        ref[ROW_PARAM + 4 : ROW_PARAM + 7, 0:height] = off_v[...]
    low_half = lax.rem(kz, 4) < 2
    z2[...] = jnp.zeros((16, 128), jnp.float32)
    for c in range(3):
        base = ROW_NOISE + height * c
        last = za[base + height - 1 : base + height, :]
        first = za[base : base + 1, :]
        z2[c : c + 1, :] = jnp.where(low_half, last, first)
        z2[8 + c : 9 + c, :] = jnp.where(low_half, first, last)


def dot3(a, b, dims=(((1,), (0,)), ((), ()))):
    a_hi, b_hi = a.astype(jnp.bfloat16), b.astype(jnp.bfloat16)
    a_lo = (a - a_hi.astype(jnp.float32)).astype(jnp.bfloat16)
    b_lo = (b - b_hi.astype(jnp.float32)).astype(jnp.bfloat16)

    def dot(u, v):
        return lax.dot_general(u, v, dims, preferred_element_type=jnp.float32)

    return dot(a_hi, b_hi) + (dot(a_lo, b_hi) + dot(a_hi, b_lo))


NT = (((1,), (1,)), ((), ()))


def put_pair(pair, slot, value, first_column, into):
    return jnp.where(pair == slot, pltpu.roll(value, (2 * slot - first_column) % 128, 1), into)


def bulk_kernel(nz, pops, mask, post, solidp, right_cols, left_cols):
    height = pops.shape[2]
    kz = lax.axis_index("gz")
    pair = lax.broadcasted_iota(jnp.int32, (8, 128), 1) // 2

    def body(t, carry):
        row = pl.multiple_of(t * 8, 8)
        out = pl.ds(row + PAD, 8)
        wall = wall_rows(row, height, kz, nz)
        flat = right = left = jnp.zeros((8, 128), jnp.float32)
        for x in range(4):
            solid = (mask[x, pl.ds(row, 8), :] == 1) | wall
            p = collide([pops[i, x, pl.ds(row, 8), :] for i in range(19)], solid)
            flag = solid.astype(jnp.float32)
            solidp[x, out, :] = flag
            flat = put_pair(pair, FLAG_PLANE + x, flag, 127, flat)
            for q, i in enumerate(Y_FLAT):
                post[i, x, out, :] = p[i]
                flat = put_pair(pair, 4 * q + x, p[i], 127, flat)
            for n, i in enumerate(Y_PLUS):
                j = MIRROR_Y[i]
                slot = LANE_PLUS // 2 + 4 * n + x
                post[i, x, out, :] = pltpu.roll(p[i], 1, 1)
                post[j, x, out, :] = pltpu.roll(p[j], 127, 1)
                right = put_pair(pair, slot, p[i], 126, right)
                left = put_pair(pair, slot, p[j], 0, left)
        right_cols[out, :] = jnp.where(pair < LANE_PLUS // 2, flat, right)
        left_cols[out, :] = jnp.where(pair < LANE_PLUS // 2, flat, left)
        return carry

    lax.fori_loop(0, height // 8, body, 0)


def column_kernel(
    nz, post_in, solid_in, right_in, left_in, sent, za, zb, z2c, z2d, bandz,
    post, solidp, ya, yb, linear, meanrow,
    wide, filt, moved,
):
    height = post.shape[2] - 2 * PAD
    rows = height + 2 * PAD
    kz = lax.axis_index("gz")
    ky = lax.axis_index("gy") * lax.axis_size("col") + lax.axis_index("col")
    z_even = lax.rem(kz, 2) == 0
    y_even = lax.rem(ky, 2) == 0
    low_half = lax.rem(kz, 4) < 2

    def below(row, n=1):
        return jnp.where(z_even, zb[row : row + n, :], za[row : row + n, :])

    def above(row, n=1):
        return jnp.where(z_even, za[row : row + n, :], zb[row : row + n, :])

    top = PAD + height
    low, high = below(0, ROW_PARAM), above(0, ROW_PARAM)
    for n, shift in enumerate((0, 1, 127)):
        moved[n, 0] = low if shift == 0 else pltpu.roll(low, shift, 1)
        moved[n, 1] = high if shift == 0 else pltpu.roll(high, shift, 1)
    for items, first, depth in ((Z_EDGE, 0, 0), (Z_SECOND, len(Z_EDGE), 1)):
        for q, i in enumerate(items):
            n = DIRS[i][1] % 3
            for x in range(4):
                at = slice(4 * (first + q) + x, 4 * (first + q) + x + 1)
                post[i, x, PAD - 1 - depth : PAD - depth, :] = moved[n, 0, at, :]
                post[MIRROR_Z[i], x, top + depth : top + depth + 1, :] = moved[n, 1, at, :]
    for x in range(4):
        solidp[x, PAD - 1 : PAD, :] = moved[0, 0, ROW_SOLID + x : ROW_SOLID + x + 1, :]
        solidp[x, top : top + 1, :] = moved[0, 1, ROW_SOLID + x : ROW_SOLID + x + 1, :]

    lane = lax.broadcasted_iota(jnp.int32, (8, 128), 1)
    own_par = pltpu.roll(sent[ROW_PARAM : ROW_PARAM + 8, :], PAD, 1)
    low_par = pltpu.roll(below(ROW_PARAM, 8), 128 - height + PAD, 1)
    high_par = pltpu.roll(above(ROW_PARAM, 8), height + PAD, 1)
    par = jnp.where(lane < PAD, low_par, jnp.where(lane < top, own_par, high_par))
    par = jnp.where(lane < rows, par, 0.0)
    meanrow[...] = par
    cols = jnp.transpose(jnp.concatenate([par] * 16, axis=0))[0:rows]

    for c in range(3):
        lanes = slice(128 * c, 128 * c + 128)
        at = slice(ROW_NOISE + height * c, ROW_NOISE + height * (c + 1))
        wide[0:height, lanes] = below(ROW_NOISE + height * c, height)
        wide[height : 2 * height, lanes] = sent[at, :]
        wide[2 * height : 3 * height, lanes] = above(ROW_NOISE + height * c, height)
    filt[...] = dot3(bandz[...], wide[...])
    b_end = float(taps()[0])
    far_low = jnp.where(low_half, z2d[8:16, :], z2c[0:8, :])
    far_high = jnp.where(low_half, z2c[0:8, :], z2d[8:16, :])
    for c in range(3):
        lanes = slice(128 * c, 128 * c + 128)
        filt[PAD - 1 : PAD, lanes] += b_end * far_low[c : c + 1, :]
        filt[top : top + 1, lanes] += b_end * far_high[c : c + 1, :]
    f0, f1, f2 = (filt[:, 128 * c : 128 * c + 128] for c in range(3))
    linear[0] = cols[:, 1:2] * f0
    linear[1] = cols[:, 4:5] * f0 + cols[:, 2:3] * f1
    linear[2] = cols[:, 5:6] * f0 + cols[:, 6:7] * f1 + cols[:, 3:4] * f2
    linear[3] = jnp.broadcast_to(cols[:, 0:1], (rows, 128))

    pair = lane // 2
    for row in range(0, rows, 8):
        out = slice(row, row + 8)
        if row == 0 or row == rows - 8:
            flat = right = left = jnp.zeros((8, 128), jnp.float32)
            for x in range(4):
                flat = put_pair(pair, FLAG_PLANE + x, solidp[x, out, :], 127, flat)
                for q, i in enumerate(Y_FLAT):
                    flat = put_pair(pair, 4 * q + x, post[i, x, out, :], 127, flat)
                for n, i in enumerate(Y_PLUS):
                    slot = LANE_PLUS // 2 + 4 * n + x
                    right = put_pair(pair, slot, post[i, x, out, :], 127, right)
                    left = put_pair(pair, slot, post[MIRROR_Y[i], x, out, :], 127, left)
            right = jnp.where(pair < LANE_PLUS // 2, flat, right)
            left = jnp.where(pair < LANE_PLUS // 2, flat, left)
        else:
            right, left = right_in[out, :], left_in[out, :]
        for c in range(3):
            v = linear[c, out, :]
            far = LANE_FAR + c
            right = jnp.where(lane == far, pltpu.roll(v, (far - 63) % 128, 1), right)
            left = jnp.where(lane == far, pltpu.roll(v, (far - 64) % 128, 1), left)
        ya[out, :] = jnp.where(y_even, right, left)
        yb[out, :] = jnp.where(y_even, left, right)
    half = rows // 2
    lane_h = lax.broadcasted_iota(jnp.int32, (half, 128), 1)
    for c in range(3):
        first, second = linear[c, 0:half, :], linear[c, half:rows, :]
        left = jnp.where(lane_h < 64, first, pltpu.roll(second, 64, 1))
        right = jnp.where(lane_h < 64, pltpu.roll(first, 64, 1), second)
        at = slice(rows + half * c, rows + half * (c + 1))
        ya[at, :] = jnp.where(y_even, right, left)
        yb[at, :] = jnp.where(y_even, left, right)


def streamed(i, x):
    source = x - DIRS[i][0]
    return None if source < 0 else min(source, 3)


def interior_kernel(
    nz, post, solidp, linear, ya, yb, wy, wg, post2, flow_own, ghost_own, own_right, own_left
):
    rows = post.shape[2]
    top = rows - PAD
    kz = lax.axis_index("gz")
    ky = lax.axis_index("gy") * lax.axis_size("col") + lax.axis_index("col")
    y_even = lax.rem(ky, 2) == 0
    sub = lax.broadcasted_iota(jnp.int32, (8, 128), 0)

    def step(row, outside):
        for x in range(1, 4):
            solid = solidp[x, pl.ds(row, 8), :] > 0.5
            g = [post[i, streamed(i, x), pl.ds(row - DIRS[i][2], 8), :] for i in range(19)]
            p = collide(g, solid)
            for i in range(19):
                value = p[i] if outside is None else jnp.where(outside, 0.0, p[i])
                if DIRS[i][1]:
                    value = pltpu.roll(value, DIRS[i][1] % 128, 1)
                post2[i, x - 1, pl.ds(row, 8), :] = value

    step(PAD - 1, (sub == 0) & (kz == 0))
    step(top - 7, (sub == 7) & (kz == nz - 1))

    def body(t, carry):
        step(pl.multiple_of(t * 8 + PAD, 8), None)
        return carry

    lax.fori_loop(0, rows // 8 - 2, body, 0)

    flow_own[...] = dot3(linear[0:3].reshape(3 * rows, 128), wy[0:128, :])
    flow_own[0:rows, :] += linear[3]
    for c in range(3):
        ghost_own[8 * c : 8 * c + 8, 0:rows] = dot3(wg[:, 0:128], linear[c], NT)
        ghost_own[8 * c : 8 * c + 8, rows:128] = jnp.zeros((8, 128 - rows), jnp.float32)
    fill = jnp.zeros((128 - rows, 128), jnp.float32)
    a, b = ya[0:rows, :], yb[0:rows, :]
    own_right[0:128, :] = jnp.transpose(jnp.concatenate([jnp.where(y_even, a, b), fill], axis=0))
    own_left[0:128, :] = jnp.transpose(jnp.concatenate([jnp.where(y_even, b, a), fill], axis=0))


def final_kernel(
    nz, post, solidp, post2, flow_own, ghost_own, own_right, own_left, meanrow, ya, yb, wy, wg,
    inflow, state_out,
    lhs, flow, inlet2, strip_left, strip_right, moving, still, ghost_moving, ghost_still,
    state, flow_out, sems,
):
    height = state.shape[2]
    rows = height + 2 * PAD
    half = rows // 2
    top = PAD + height
    kz = lax.axis_index("gz")
    ky = lax.axis_index("gy") * lax.axis_size("col") + lax.axis_index("col")
    y_even = lax.rem(ky, 2) == 0
    lane = lax.broadcasted_iota(jnp.int32, (8, 128), 1)
    sub = lax.broadcasted_iota(jnp.int32, (8, 128), 0)

    fill = jnp.zeros((128 - rows, 128), jnp.float32)
    a, b = ya[0:rows, :], yb[0:rows, :]
    strip_left[0:128, :] = jnp.transpose(jnp.concatenate([jnp.where(y_even, b, a), fill], axis=0))
    strip_right[0:128, :] = jnp.transpose(jnp.concatenate([jnp.where(y_even, a, b), fill], axis=0))

    lane_h = lax.broadcasted_iota(jnp.int32, (half, 128), 1)
    for c in range(3):
        at = slice(rows + half * c, rows + half * (c + 1))
        a, b = ya[at, :], yb[at, :]
        left, right = jnp.where(y_even, b, a), jnp.where(y_even, a, b)
        lo, hi = slice(rows * c, rows * c + half), slice(rows * c + half, rows * (c + 1))
        lhs[lo, 0:128] = jnp.where(lane_h < 64, left, 0.0)
        lhs[hi, 0:128] = jnp.where(lane_h < 64, 0.0, left)
        lhs[lo, 128:256] = jnp.where(lane_h < 64, right, 0.0)
        lhs[hi, 128:256] = jnp.where(lane_h < 64, 0.0, right)
    flow[...] = flow_own[...] + dot3(lhs[...], wy[128:384, :])
    for c in range(3):
        flow_out[c] = flow[rows * c + PAD : rows * c + top, :]
    flow_copy = pltpu.make_async_copy(flow_out, inflow, sems.at[height // 8])
    flow_copy.start()
    b_end = float(taps()[0])
    column_flow = []
    for c in range(3):
        g = dot3(wg[:, 128:384], lhs[rows * c : rows * (c + 1), :], NT)
        g = jnp.concatenate([g, jnp.zeros((8, 128 - rows), jnp.float32)], axis=1)
        g = g + ghost_own[8 * c : 8 * c + 8, :]
        far = slice(LANE_FAR + c, LANE_FAR + c + 1)
        at = [g[n : n + 1, :] for n in range(4)]
        at[0] = at[0] + b_end * strip_left[far, :]
        at[3] = at[3] + b_end * strip_right[far, :]
        if c == 0:
            at = [v + meanrow[0:1, :] for v in at]
        column_flow.append(at)

    outside = ((lane < PAD) & (kz == 0)) | ((lane >= top) & (kz == nz - 1))
    sources = (
        ((strip_left, 0), (strip_left, 0), (own_left, 0)),
        ((own_left, 1), (strip_left, 1), (own_left, 1)),
        ((own_right, 0), (own_right, 0), (strip_right, 0)),
        ((strip_right, 1), (own_right, 1), (strip_right, 1)),
    )
    for column in range(4):
        def rows_of(start):
            return pl.ds(start, 8, stride=2)

        src, odd = sources[column][0]
        solid = src[rows_of(2 * FLAG_PLANE + odd), :] > 0.5
        g = [None] * 19
        for i in range(19):
            cx, cy, cz = DIRS[i]
            src, odd = sources[column][cy % 3]
            if cy == 0:
                start = 8 * Y_FLAT.index(i) + odd
            else:
                start = LANE_PLUS + 8 * Y_PLUS.index(i if cy == 1 else MIRROR_Y[i]) + odd
            v = src[rows_of(start - 2 * cx), :]
            if cx == 1:
                v = jnp.where(sub == 0, 0.0, v)
            elif cx == -1:
                v = jnp.where(sub == 3, src[rows_of(start), :], v)
            g[i] = v if cz == 0 else pltpu.roll(v, cz % 128, 1)
        us = [INLET * jnp.broadcast_to(column_flow[c][column], (8, 128)) for c in range(3)]
        eq = inlet_state(*us)
        put = (sub == 0) & jnp.logical_not(solid)
        moves = 1 if column < 2 else -1
        keep = [i for i in range(19) if DIRS[i][1] == moves or (DIRS[i][1] == 0 and column in (1, 2))]
        p = collide(g, solid, keep)
        for i in keep:
            value = jnp.where(outside, 0.0, jnp.where(put, eq[i], p[i]))[0:4, :]
            if DIRS[i][1]:
                n = Y_PLUS.index(i if moves == 1 else MIRROR_Y[i])
                moving[pl.ds(16 * n + (column + 2) % 4, 4, stride=4), :] = value
            else:
                still[pl.ds(8 * Y_FLAT.index(i) + 2 - column, 4, stride=2), :] = value
    ghost_moving[...] = jnp.transpose(moving[...])
    ghost_still[...] = jnp.transpose(still[...])

    def inlet(row, outside_rows):
        us = [INLET * flow[pl.ds(rows * c + row, 8), :] for c in range(3)]
        eq = inlet_state(*us)
        solid = solidp[0, pl.ds(row, 8), :] > 0.5
        for i in range(19):
            j = OPP[i]
            source = streamed(j, 0)
            if source is None:
                value = jnp.where(solid, 0.0, eq[i])
            else:
                value = jnp.where(solid, post[j, source, pl.ds(row - DIRS[j][2], 8), :], eq[i])
            if outside_rows is not None:
                value = jnp.where(outside_rows, 0.0, value)
            if DIRS[i][1]:
                value = pltpu.roll(value, DIRS[i][1] % 128, 1)
            inlet2[i, pl.ds(row, 8), :] = value

    def out_copy(t):
        at = pl.ds(pl.multiple_of(t * 8, 8), 8)
        return pltpu.make_async_copy(state.at[:, :, at, :], state_out.at[:, :, at, :], sems.at[t])

    def last(t):
        row = pl.multiple_of(t * 8 + PAD, 8)
        us = [INLET * flow[pl.ds(rows * c + row, 8), :] for c in range(3)]
        eq = inlet_state(*us)
        solid = solidp[0, pl.ds(row, 8), :] > 0.5
        ends = (lane == 0) | (lane == 127)

        def read(i, source, ghost):
            at = pl.ds(row - DIRS[i][2], 8)
            v = inlet2[i, at, :] if source == 0 else post2[i, source - 1, at, :]
            where = ends if DIRS[i][1] == 0 else (lane < 2 if DIRS[i][1] == 1 else lane >= 126)
            return jnp.where(where, ghost, v)

        def write(i, x, value):
            if x == 0:
                value = jnp.where(solid, value, eq[i])
            state[i, x, pl.ds(row - PAD, 8), :] = value

        for i in Y_FLAT + Y_PLUS:
            both = [i] if DIRS[i][1] == 0 else [i, MIRROR_Y[i]]
            at = pl.ds(row - DIRS[i][2], 8)
            for source in range(4):
                targets = [x for x in range(4) if streamed(i, x) == source]
                if not targets:
                    continue
                if DIRS[i][1] == 0:
                    slot = 2 * (4 * Y_FLAT.index(i) + source)
                    ghost = pltpu.roll(ghost_still[at, :], (127 - slot) % 128, 1)
                else:
                    slot = 4 * (4 * Y_PLUS.index(i) + source)
                    ghost = pltpu.roll(ghost_moving[at, :], (126 - slot) % 128, 1)
                for j in both:
                    value = read(j, source, ghost)
                    for x in targets:
                        write(j, x, value)
            for j in both:
                if streamed(j, 0) is None:
                    write(j, 0, jnp.zeros((8, 128), jnp.float32))
        out_copy(t).start()

    inlet(PAD - 1, (sub == 0) & (kz == 0))
    inlet(top - 7, (sub == 7) & (kz == nz - 1))
    inlet(PAD, None)

    def main(t, carry):
        inlet(pl.multiple_of(t * 8 + PAD, 8), None)
        last(t - 1)
        return carry

    tiles = height // 8
    lax.fori_loop(1, tiles, main, 0)
    last(tiles - 1)
    for t in range(tiles):
        out_copy(t).wait()
    flow_copy.wait()


def swap_pairs(count, phase, distance=1):
    pairs = []
    for i in range(count):
        block = (i + phase * distance) // distance
        j = i + distance if block % 2 == 0 else i - distance
        if 0 <= j < count:
            pairs.append((i, j))
    return pairs


def ring_pairs(count, phase):
    if phase == 0:
        return [(i, i ^ 1) for i in range(count)]
    return [(i, (((i + 1) % count ^ 1) - 1) % count) for i in range(count)]


def vm(n):
    return [pl.BlockSpec(memory_space=pltpu.VMEM)] * n


def hbm(n):
    return [pl.BlockSpec(memory_space=pltpu.HBM)] * n


def f32(*shape):
    return jax.ShapeDtypeStruct(shape, jnp.float32)


def scratch(*shape):
    return pltpu.VMEM(shape, jnp.float32)


def flags(*shape):
    return pltpu.VMEM(shape, jnp.int32)


def params(mib):
    return pltpu.CompilerParams(vmem_limit_bytes=mib * 1024 * 1024)


def cost(flops, size):
    return pl.CostEstimate(flops=flops, bytes_accessed=size, transcendentals=0)


def shards(nz, ny, noise, mean_profile, lund_diag, lund_off, populations, mask):
    height, span = noise.shape[1], noise.shape[2]
    rows = height + 2 * PAD
    message = ROW_NOISE + 3 * height
    dma = pltpu.SemaphoreType.DMA
    here = lambda value: pltpu.with_memory_space_constraint(value, pltpu.HBM)
    mean_profile = mean_profile.reshape(1, height)
    operands = populations, mask, noise, mean_profile, lund_diag, lund_off

    za, zb, z2 = pl.pallas_call(
        lambda *refs: edge_kernel(nz, *refs),
        out_shape=(f32(message, 128), f32(message, 128), f32(16, 128)),
        in_specs=hbm(6),
        out_specs=vm(3),
        scratch_shapes=[
            scratch(19, 4, 16, 128), flags(4, 16, 128), scratch(1, height), scratch(3, height),
            scratch(3, height), scratch(20, 4, 16, 128), dma((13,)),
        ],
        compiler_params=params(8),
        name="edge_rows",
    )(*map(here, operands))

    ra = lax.ppermute(za, "gz", swap_pairs(nz, 0))
    rb = lax.ppermute(zb, "gz", swap_pairs(nz, 1))
    rc = lax.ppermute(z2, "gz", swap_pairs(nz, 0, 2))
    far = swap_pairs(nz, 1, 2)
    rd = lax.ppermute(z2, "gz", far) if far else jnp.zeros_like(z2)

    post, solidp, right_cols, left_cols = pl.pallas_call(
        lambda *refs: bulk_kernel(nz, *refs),
        out_shape=(f32(19, 4, rows, 128), f32(4, rows, 128), f32(rows, 128), f32(rows, 128)),
        in_specs=vm(2),
        out_specs=vm(4),
        compiler_params=params(4),
        cost_estimate=cost(4_000_000_000, 8_000_000),
        name="bulk",
    )(populations, mask)

    line = np.arange(rows) - PAD
    used = (line >= -1) & (line <= height)
    bandz = np.where(used[:, None], band(np.arange(-height, 2 * height), line).T, 0.0)
    post, solidp, ya, yb, linear, meanrow = pl.pallas_call(
        lambda *refs: column_kernel(nz, *refs),
        out_shape=(
            f32(19, 4, rows, 128), f32(4, rows, 128), f32(rows + 3 * rows // 2, 128),
            f32(rows + 3 * rows // 2, 128), f32(4, rows, 128), f32(8, 128),
        ),
        in_specs=vm(10),
        out_specs=vm(6),
        scratch_shapes=[
            scratch(3 * height, 384), scratch(rows, 384), scratch(3, 2, ROW_PARAM, 128),
        ],
        input_output_aliases={0: 0, 1: 1},
        compiler_params=params(4),
        name="columns",
    )(post, solidp, right_cols, left_cols, za, ra, rb, rc, rd, jnp.asarray(bandz, jnp.float32))

    qa = lax.ppermute(ya, ("gy", "col"), ring_pairs(ny, 0))
    qb = lax.ppermute(yb, ("gy", "col"), ring_pairs(ny, 1))

    own = np.arange(span)
    left = np.arange(128) % 64 - 64
    right = np.arange(128) % 64 + span
    source = np.concatenate([own, left, right])
    wy = jnp.asarray(band(source, own))
    wg = np.zeros((8, 384), np.float32)
    wg[0:4] = band(source, np.array([-1, 0, span - 1, span])).T
    wg = jnp.asarray(wg)
    post2, flow_own, ghost_own, own_right, own_left = pl.pallas_call(
        lambda *refs: interior_kernel(nz, *refs),
        out_shape=(
            f32(19, 3, rows, 128), f32(3 * rows, 128), f32(24, 128), f32(144, 128), f32(144, 128),
        ),
        in_specs=vm(7),
        out_specs=vm(5),
        compiler_params=params(4),
        cost_estimate=cost(4_000_000_000, 8_000_000),
        name="interior",
    )(post, solidp, linear, ya, yb, wy, wg)
    inflow, state = pl.pallas_call(
        lambda *refs: final_kernel(nz, *refs),
        out_shape=(f32(3, height, span), f32(19, 4, height, span)),
        in_specs=vm(12),
        out_specs=hbm(2),
        scratch_shapes=[
            scratch(3 * rows, 256), scratch(3 * rows, 128), scratch(19, rows, 128),
            scratch(144, 128), scratch(144, 128), scratch(128, 128), scratch(128, 128),
            scratch(128, 128), scratch(128, 128), scratch(19, 4, height, span),
            scratch(3, height, span), dma((height // 8 + 1,)),
        ],
        compiler_params=params(8),
        name="stream",
    )(post, solidp, post2, flow_own, ghost_own, own_right, own_left, meanrow, qa, qb, wy, wg)
    return inflow, state


def solution(mesh):
    nz = mesh.shape["gz"]
    ny = mesh.shape["gy"] * mesh.shape["col"]
    in_specs = (
        P(None, "gz", ("gy", "col")),
        P("gz"),
        P(None, "gz"),
        P(None, "gz"),
        P(None, None, "gz", ("gy", "col")),
        P(None, "gz", ("gy", "col")),
    )
    out_specs = (P(None, "gz", ("gy", "col")), P(None, None, "gz", ("gy", "col")))

    def body(*args):
        return shards(nz, ny, *args)

    return jax.shard_map(body, mesh=mesh, in_specs=in_specs, out_specs=out_specs, check_vma=False)
```

```python
import math

import jax
import jax.numpy as jnp
import numpy as np
from jax import lax
from jax.experimental import pallas as pl
from jax.experimental.pallas import tpu as pltpu
from jax.sharding import PartitionSpec as P

HW = 64
DIRS = [
    (0, 0, 0),
    (1, 0, 0), (-1, 0, 0), (0, 1, 0), (0, -1, 0), (0, 0, 1), (0, 0, -1),
    (1, 1, 0), (-1, -1, 0), (1, -1, 0), (-1, 1, 0),
    (1, 0, 1), (-1, 0, -1), (1, 0, -1), (-1, 0, 1),
    (0, 1, 1), (0, -1, -1), (0, 1, -1), (0, -1, 1),
]
OPP = [DIRS.index((-a, -b, -c)) for a, b, c in DIRS]
MIRROR_Y = [DIRS.index((a, -b, c)) for a, b, c in DIRS]
MIRROR_Z = [DIRS.index((a, b, -c)) for a, b, c in DIRS]
INLET = 0.05

Z_EDGE = [i for i in range(19) if DIRS[i][2] == 0] + [i for i in range(19) if DIRS[i][2] == 1]
Z_SECOND = [i for i in range(19) if DIRS[i][2] == 1]
Y_FLAT = [i for i in range(19) if DIRS[i][1] == 0]
Y_PLUS = [i for i in range(19) if DIRS[i][1] == 1]
FLAG_PLANE = 4 * len(Y_FLAT)
LANE_PLUS = 2 * FLAG_PLANE + 8
LANE_FAR = LANE_PLUS + 8 * len(Y_PLUS)

ROW_SOLID = 76
ROW_PARAM = 80
ROW_NOISE = 88
PAD = 8
FIRST = PAD - 2
Y_ROWS = 68
Y_HALF = 34
Y_FILTER = 72
Y_MESSAGE = 176


def taps():
    k = np.arange(-HW, HW + 1).astype(np.float64)
    raw = np.exp(-math.pi * k * k / (2.0 * (HW // 2) ** 2))
    return raw / np.sqrt(np.sum(raw * raw))


def band(source, target):
    values = taps()
    offset = np.asarray(source)[:, None] - np.asarray(target)[None, :]
    inside = np.abs(offset) <= HW
    return np.where(inside, values[np.clip(offset + HW, 0, 2 * HW)], 0.0).astype(np.float32)


def moments(g):
    s = {a: g[a] + g[a + 1] for a in range(1, 19, 2)}
    d = {a: g[a] - g[a + 1] for a in range(1, 19, 2)}
    w1, w2 = 1.0 / 18.0, 1.0 / 36.0
    rho = (
        g[0] * (1.0 / 3.0)
        + (s[1] + s[3] + s[5]) * w1
        + ((s[7] + s[9]) + (s[11] + s[13]) + (s[15] + s[17])) * w2
    )
    mx = d[1] * w1 + ((d[7] + d[9]) + (d[11] + d[13])) * w2
    my = d[3] * w1 + ((d[7] - d[9]) + (d[15] + d[17])) * w2
    mz = d[5] * w1 + ((d[11] - d[13]) + (d[15] - d[17])) * w2
    return rho, mx, my, mz


def pair_vector(a, vx, vy, vz):
    total = None
    for c, v in zip(DIRS[a], (vx, vy, vz)):
        if c:
            term = v if c > 0 else -v
            total = term if total is None else (total + v if c > 0 else total - v)
    return total


def collide(g, solid, keep=range(19)):
    rho, mx, my, mz = moments(g)
    inv = 1.0 / rho
    ux, uy, uz = mx * inv, my * inv, mz * inv
    square = mx * ux + my * uy + mz * uz
    base = 1.25 * rho - 1.875 * square
    post = [None] * 19
    if 0 in keep:
        post[0] = jnp.where(solid, g[0], base - 0.25 * g[0])
    for a in range(1, 19, 2):
        if a not in keep and a + 1 not in keep:
            continue
        m = pair_vector(a, mx, my, mz)
        p = pair_vector(a, ux, uy, uz)
        even = base + 5.625 * (m * p)
        odd = 3.75 * m
        if a in keep:
            post[a] = jnp.where(solid, g[a + 1], (even + odd) - 0.25 * g[a])
        if a + 1 in keep:
            post[a + 1] = jnp.where(solid, g[a], (even - odd) - 0.25 * g[a + 1])
    return post


def inlet_state(ux, uy, uz):
    base = 1.0 - 1.5 * (ux * ux + uy * uy + uz * uz)
    out = [base] * 19
    for a in range(1, 19, 2):
        p = pair_vector(a, ux, uy, uz)
        even = base + 4.5 * (p * p)
        odd = 3.0 * p
        out[a] = even + odd
        out[a + 1] = even - odd
    return out


def wall_rows(first_row, height, kz, nz):
    rows = lax.broadcasted_iota(jnp.int32, (8, 128), 0) + first_row
    return ((rows == 0) & (kz == 0)) | ((rows == height - 1) & (kz == nz - 1))


def edge_kernel(
    nz, pops, mask, noise, mean, diag, off, za, zb, raw, flags, mean_v, diag_v, off_v, edge, sems
):
    height = pops.shape[2]
    kz = lax.axis_index("gz")
    upward = lax.rem(kz, 2) == 0
    upper = pl.ds(height - 8, 8)
    copies = [
        (pops.at[:, :, 0:8, :], raw.at[:, :, 0:8, :]),
        (pops.at[:, :, upper, :], raw.at[:, :, 8:16, :]),
        (mask.at[:, 0:8, :], flags.at[:, 0:8, :]),
        (mask.at[:, upper, :], flags.at[:, 8:16, :]),
        (mean, mean_v),
        (diag, diag_v),
        (off, off_v),
    ]
    for c in range(3):
        at = slice(ROW_NOISE + height * c, ROW_NOISE + height * (c + 1))
        copies.append((noise.at[c], za.at[at, :]))
        copies.append((noise.at[c], zb.at[at, :]))
    copies = [pltpu.make_async_copy(src, dst, sems.at[n]) for n, (src, dst) in enumerate(copies)]
    for copy in copies:
        copy.start()
    for copy in copies[:4]:
        copy.wait()
    for part, row in ((0, 0), (1, height - 8)):
        wall = wall_rows(row, height, kz, nz)
        at = slice(8 * part, 8 * part + 8)
        for x in range(4):
            solid = (flags[x, at, :] == 1) | wall
            post = collide([raw[i, x, at, :] for i in range(19)], solid)
            for i in range(19):
                edge[i, x, at, :] = post[i]
            edge[19, x, at, :] = solid.astype(jnp.float32)

    def put(row, up, down):
        za[row : row + 1, :] = jnp.where(upward, up, down)
        zb[row : row + 1, :] = jnp.where(upward, down, up)

    q = 0
    for i in Z_EDGE:
        for x in range(4):
            put(4 * q + x, edge[i, x, 15:16, :], edge[MIRROR_Z[i], x, 0:1, :])
        q += 1
    for i in Z_SECOND:
        for x in range(4):
            put(4 * q + x, edge[i, x, 14:15, :], edge[MIRROR_Z[i], x, 1:2, :])
        q += 1
    for x in range(4):
        put(4 * q + x, edge[19, x, 15:16, :], edge[19, x, 0:1, :])
    for copy in copies[4:]:
        copy.wait()
    for ref in (za, zb):
        ref[ROW_PARAM : ROW_PARAM + 8, :] = jnp.zeros((8, 128), jnp.float32)
        ref[ROW_PARAM : ROW_PARAM + 1, 0:height] = mean_v[...]
        ref[ROW_PARAM + 1 : ROW_PARAM + 4, 0:height] = diag_v[...]
        ref[ROW_PARAM + 4 : ROW_PARAM + 7, 0:height] = off_v[...]


def far_kernel(height, za, z2):
    kz = lax.axis_index("gz")
    low_half = lax.rem(kz, 4) < 2
    z2[...] = jnp.zeros((16, 128), jnp.float32)
    for c in range(3):
        base = ROW_NOISE + height * c
        last = za[base + height - 1 : base + height, :]
        first = za[base : base + 1, :]
        z2[c : c + 1, :] = jnp.where(low_half, last, first)
        z2[8 + c : 9 + c, :] = jnp.where(low_half, first, last)


def dot3(a, b, dims=(((1,), (0,)), ((), ()))):
    a_hi, b_hi = a.astype(jnp.bfloat16), b.astype(jnp.bfloat16)
    a_lo = (a - a_hi.astype(jnp.float32)).astype(jnp.bfloat16)
    b_lo = (b - b_hi.astype(jnp.float32)).astype(jnp.bfloat16)

    def dot(u, v):
        return lax.dot_general(u, v, dims, preferred_element_type=jnp.float32)

    return dot(a_hi, b_hi) + (dot(a_lo, b_hi) + dot(a_hi, b_lo))


NT = (((1,), (1,)), ((), ()))


def put_pair(pair, slot, value, first_column, into):
    return jnp.where(pair == slot, pltpu.roll(value, (2 * slot - first_column) % 128, 1), into)


def bulk_kernel(nz, pops, mask, post, solidp, right_cols, left_cols):
    height = pops.shape[2]
    kz = lax.axis_index("gz")
    pair = lax.broadcasted_iota(jnp.int32, (8, 128), 1) // 2

    def body(t, carry):
        row = pl.multiple_of(t * 8, 8)
        out = pl.ds(row + PAD, 8)
        wall = wall_rows(row, height, kz, nz)
        flat = right = left = jnp.zeros((8, 128), jnp.float32)
        for x in range(4):
            solid = (mask[x, pl.ds(row, 8), :] == 1) | wall
            p = collide([pops[i, x, pl.ds(row, 8), :] for i in range(19)], solid)
            flag = solid.astype(jnp.float32)
            solidp[x, out, :] = flag
            flat = put_pair(pair, FLAG_PLANE + x, flag, 127, flat)
            for q, i in enumerate(Y_FLAT):
                post[i, x, out, :] = p[i]
                flat = put_pair(pair, 4 * q + x, p[i], 127, flat)
            for n, i in enumerate(Y_PLUS):
                j = MIRROR_Y[i]
                slot = LANE_PLUS // 2 + 4 * n + x
                post[i, x, out, :] = pltpu.roll(p[i], 1, 1)
                post[j, x, out, :] = pltpu.roll(p[j], 127, 1)
                right = put_pair(pair, slot, p[i], 126, right)
                left = put_pair(pair, slot, p[j], 0, left)
        right_cols[out, :] = jnp.where(pair < LANE_PLUS // 2, flat, right)
        left_cols[out, :] = jnp.where(pair < LANE_PLUS // 2, flat, left)
        return carry

    lax.fori_loop(0, height // 8, body, 0)


def column_kernel(
    nz, post_in, solid_in, right_in, left_in, sent, za, zb, z2c, z2d, bandz,
    post, solidp, ya, yb, linear, meanrow,
    wide, filt, moved, ends,
):
    height = post.shape[2] - 2 * PAD
    rows = height + 2 * PAD
    kz = lax.axis_index("gz")
    ky = lax.axis_index("gy") * lax.axis_size("col") + lax.axis_index("col")
    z_even = lax.rem(kz, 2) == 0
    y_even = lax.rem(ky, 2) == 0
    low_half = lax.rem(kz, 4) < 2

    def below(row, n=1):
        return jnp.where(z_even, zb[row : row + n, :], za[row : row + n, :])

    def above(row, n=1):
        return jnp.where(z_even, za[row : row + n, :], zb[row : row + n, :])

    top = PAD + height
    low, high = below(0, ROW_PARAM), above(0, ROW_PARAM)
    for n, shift in enumerate((0, 1, 127)):
        moved[n, 0] = low if shift == 0 else pltpu.roll(low, shift, 1)
        moved[n, 1] = high if shift == 0 else pltpu.roll(high, shift, 1)
    for items, first, depth in ((Z_EDGE, 0, 0), (Z_SECOND, len(Z_EDGE), 1)):
        for q, i in enumerate(items):
            n = DIRS[i][1] % 3
            for x in range(4):
                at = slice(4 * (first + q) + x, 4 * (first + q) + x + 1)
                post[i, x, PAD - 1 - depth : PAD - depth, :] = moved[n, 0, at, :]
                post[MIRROR_Z[i], x, top + depth : top + depth + 1, :] = moved[n, 1, at, :]
    for x in range(4):
        solidp[x, PAD - 1 : PAD, :] = moved[0, 0, ROW_SOLID + x : ROW_SOLID + x + 1, :]
        solidp[x, top : top + 1, :] = moved[0, 1, ROW_SOLID + x : ROW_SOLID + x + 1, :]

    lane = lax.broadcasted_iota(jnp.int32, (8, 128), 1)
    own_par = pltpu.roll(sent[ROW_PARAM : ROW_PARAM + 8, :], PAD, 1)
    low_par = pltpu.roll(below(ROW_PARAM, 8), 128 - height + PAD, 1)
    high_par = pltpu.roll(above(ROW_PARAM, 8), height + PAD, 1)
    par = jnp.where(lane < PAD, low_par, jnp.where(lane < top, own_par, high_par))
    par = jnp.where(lane < rows, par, 0.0)
    meanrow[...] = par
    cols = jnp.transpose(jnp.concatenate([par] * 16, axis=0))[0:rows]

    for c in range(3):
        lanes = slice(128 * c, 128 * c + 128)
        at = slice(ROW_NOISE + height * c, ROW_NOISE + height * (c + 1))
        wide[0:height, lanes] = below(ROW_NOISE + height * c, height)
        wide[height : 2 * height, lanes] = sent[at, :]
        wide[2 * height : 3 * height, lanes] = above(ROW_NOISE + height * c, height)
    filt[...] = dot3(bandz[...], wide[...])
    b_end = float(taps()[0])
    far_low = jnp.where(low_half, z2d[8:16, :], z2c[0:8, :])
    far_high = jnp.where(low_half, z2c[0:8, :], z2d[8:16, :])
    for c in range(3):
        lanes = slice(128 * c, 128 * c + 128)
        filt[PAD - 1 : PAD, lanes] += b_end * far_low[c : c + 1, :]
        filt[top : top + 1, lanes] += b_end * far_high[c : c + 1, :]
    f0, f1, f2 = (filt[:, 128 * c : 128 * c + 128] for c in range(3))
    linear[0] = cols[:, 1:2] * f0
    linear[1] = cols[:, 4:5] * f0 + cols[:, 2:3] * f1
    linear[2] = cols[:, 5:6] * f0 + cols[:, 6:7] * f1 + cols[:, 3:4] * f2
    linear[3] = jnp.broadcast_to(cols[:, 0:1], (rows, 128))

    pair = lane // 2
    for row in range(0, rows, 8):
        out = slice(row, row + 8)
        if row == 0 or row == rows - 8:
            flat = right = left = jnp.zeros((8, 128), jnp.float32)
            for x in range(4):
                flat = put_pair(pair, FLAG_PLANE + x, solidp[x, out, :], 127, flat)
                for q, i in enumerate(Y_FLAT):
                    flat = put_pair(pair, 4 * q + x, post[i, x, out, :], 127, flat)
                for n, i in enumerate(Y_PLUS):
                    slot = LANE_PLUS // 2 + 4 * n + x
                    right = put_pair(pair, slot, post[i, x, out, :], 127, right)
                    left = put_pair(pair, slot, post[MIRROR_Y[i], x, out, :], 127, left)
            right = jnp.where(pair < LANE_PLUS // 2, flat, right)
            left = jnp.where(pair < LANE_PLUS // 2, flat, left)
        else:
            right, left = right_in[out, :], left_in[out, :]
        for c in range(3):
            v = linear[c, out, :]
            far = LANE_FAR + c
            right = jnp.where(lane == far, pltpu.roll(v, (far - 63) % 128, 1), right)
            left = jnp.where(lane == far, pltpu.roll(v, (far - 64) % 128, 1), left)
        ends[0, out, :] = jnp.where(y_even, right, left)
        ends[1, out, :] = jnp.where(y_even, left, right)
    ya[0:Y_ROWS, :] = ends[0, FIRST : FIRST + Y_ROWS, :]
    yb[0:Y_ROWS, :] = ends[1, FIRST : FIRST + Y_ROWS, :]
    middle = FIRST + Y_HALF
    lane_h = lax.broadcasted_iota(jnp.int32, (Y_HALF, 128), 1)
    for c in range(3):
        first, second = linear[c, FIRST:middle, :], linear[c, middle : middle + Y_HALF, :]
        left = jnp.where(lane_h < 64, first, pltpu.roll(second, 64, 1))
        right = jnp.where(lane_h < 64, pltpu.roll(first, 64, 1), second)
        at = slice(Y_FILTER + Y_HALF * c, Y_FILTER + Y_HALF * (c + 1))
        ya[at, :] = jnp.where(y_even, right, left)
        yb[at, :] = jnp.where(y_even, left, right)


def streamed(i, x):
    source = x - DIRS[i][0]
    return None if source < 0 else min(source, 3)


def interior_kernel(
    nz, post, solidp, linear, ya, yb, wy, wg, post2, flow_own, ghost_own, own_right, own_left, tall
):
    rows = post.shape[2]
    top = rows - PAD
    kz = lax.axis_index("gz")
    ky = lax.axis_index("gy") * lax.axis_size("col") + lax.axis_index("col")
    y_even = lax.rem(ky, 2) == 0
    sub = lax.broadcasted_iota(jnp.int32, (8, 128), 0)

    def step(row, outside):
        for x in range(1, 4):
            solid = solidp[x, pl.ds(row, 8), :] > 0.5
            g = [post[i, streamed(i, x), pl.ds(row - DIRS[i][2], 8), :] for i in range(19)]
            p = collide(g, solid)
            for i in range(19):
                value = p[i] if outside is None else jnp.where(outside, 0.0, p[i])
                if DIRS[i][1]:
                    value = pltpu.roll(value, DIRS[i][1] % 128, 1)
                post2[i, x - 1, pl.ds(row, 8), :] = value

    step(PAD - 1, (sub == 0) & (kz == 0))
    step(top - 7, (sub == 7) & (kz == nz - 1))

    def body(t, carry):
        step(pl.multiple_of(t * 8 + PAD, 8), None)
        return carry

    lax.fori_loop(0, rows // 8 - 2, body, 0)

    flow_own[...] = dot3(linear[0:3].reshape(3 * rows, 128), wy[0:128, :])
    flow_own[0:rows, :] += linear[3]
    for c in range(3):
        ghost_own[8 * c : 8 * c + 8, 0:rows] = dot3(wg[:, 0:128], linear[c], NT)
        ghost_own[8 * c : 8 * c + 8, rows:128] = jnp.zeros((8, 128 - rows), jnp.float32)
    a, b = ya[0:Y_ROWS, :], yb[0:Y_ROWS, :]
    tall[0, FIRST : FIRST + Y_ROWS, :] = jnp.where(y_even, a, b)
    tall[1, FIRST : FIRST + Y_ROWS, :] = jnp.where(y_even, b, a)
    own_right[0:128, :] = jnp.transpose(tall[0])
    own_left[0:128, :] = jnp.transpose(tall[1])


def final_kernel(
    nz, post, solidp, post2, flow_own, ghost_own, own_right, own_left, meanrow, ya, yb, wy, wg,
    inflow, state_out,
    lhs, flow, inlet2, strip_left, strip_right, moving, still, ghost_moving, ghost_still,
    state, flow_out, tall, sems,
):
    height = state.shape[2]
    rows = height + 2 * PAD
    top = PAD + height
    kz = lax.axis_index("gz")
    ky = lax.axis_index("gy") * lax.axis_size("col") + lax.axis_index("col")
    y_even = lax.rem(ky, 2) == 0
    lane = lax.broadcasted_iota(jnp.int32, (8, 128), 1)
    sub = lax.broadcasted_iota(jnp.int32, (8, 128), 0)

    a, b = ya[0:Y_ROWS, :], yb[0:Y_ROWS, :]
    tall[0, FIRST : FIRST + Y_ROWS, :] = jnp.where(y_even, b, a)
    tall[1, FIRST : FIRST + Y_ROWS, :] = jnp.where(y_even, a, b)
    strip_left[0:128, :] = jnp.transpose(tall[0])
    strip_right[0:128, :] = jnp.transpose(tall[1])

    lane_h = lax.broadcasted_iota(jnp.int32, (Y_HALF, 128), 1)
    for c in range(3):
        at = slice(Y_FILTER + Y_HALF * c, Y_FILTER + Y_HALF * (c + 1))
        a, b = ya[at, :], yb[at, :]
        left, right = jnp.where(y_even, b, a), jnp.where(y_even, a, b)
        middle = rows * c + FIRST + Y_HALF
        lo, hi = slice(middle - Y_HALF, middle), slice(middle, middle + Y_HALF)
        lhs[lo, 0:128] = jnp.where(lane_h < 64, left, 0.0)
        lhs[hi, 0:128] = jnp.where(lane_h < 64, 0.0, left)
        lhs[lo, 128:256] = jnp.where(lane_h < 64, right, 0.0)
        lhs[hi, 128:256] = jnp.where(lane_h < 64, 0.0, right)
    flow[...] = flow_own[...] + dot3(lhs[...], wy[128:384, :])
    for c in range(3):
        flow_out[c] = flow[rows * c + PAD : rows * c + top, :]
    flow_copy = pltpu.make_async_copy(flow_out, inflow, sems.at[height // 8])
    flow_copy.start()
    b_end = float(taps()[0])
    column_flow = []
    for c in range(3):
        g = dot3(wg[:, 128:384], lhs[rows * c : rows * (c + 1), :], NT)
        g = jnp.concatenate([g, jnp.zeros((8, 128 - rows), jnp.float32)], axis=1)
        g = g + ghost_own[8 * c : 8 * c + 8, :]
        far = slice(LANE_FAR + c, LANE_FAR + c + 1)
        at = [g[n : n + 1, :] for n in range(4)]
        at[0] = at[0] + b_end * strip_left[far, :]
        at[3] = at[3] + b_end * strip_right[far, :]
        if c == 0:
            at = [v + meanrow[0:1, :] for v in at]
        column_flow.append(at)

    outside = ((lane < PAD) & (kz == 0)) | ((lane >= top) & (kz == nz - 1))
    sources = (
        ((strip_left, 0), (strip_left, 0), (own_left, 0)),
        ((own_left, 1), (strip_left, 1), (own_left, 1)),
        ((own_right, 0), (own_right, 0), (strip_right, 0)),
        ((strip_right, 1), (own_right, 1), (strip_right, 1)),
    )
    for column in range(4):
        def rows_of(start):
            return pl.ds(start, 8, stride=2)

        src, odd = sources[column][0]
        solid = src[rows_of(2 * FLAG_PLANE + odd), :] > 0.5
        g = [None] * 19
        for i in range(19):
            cx, cy, cz = DIRS[i]
            src, odd = sources[column][cy % 3]
            if cy == 0:
                start = 8 * Y_FLAT.index(i) + odd
            else:
                start = LANE_PLUS + 8 * Y_PLUS.index(i if cy == 1 else MIRROR_Y[i]) + odd
            v = src[rows_of(start - 2 * cx), :]
            if cx == 1:
                v = jnp.where(sub == 0, 0.0, v)
            elif cx == -1:
                v = jnp.where(sub == 3, src[rows_of(start), :], v)
            g[i] = v if cz == 0 else pltpu.roll(v, cz % 128, 1)
        us = [INLET * jnp.broadcast_to(column_flow[c][column], (8, 128)) for c in range(3)]
        eq = inlet_state(*us)
        put = (sub == 0) & jnp.logical_not(solid)
        moves = 1 if column < 2 else -1
        keep = [i for i in range(19) if DIRS[i][1] == moves or (DIRS[i][1] == 0 and column in (1, 2))]
        p = collide(g, solid, keep)
        for i in keep:
            value = jnp.where(outside, 0.0, jnp.where(put, eq[i], p[i]))[0:4, :]
            if DIRS[i][1]:
                n = Y_PLUS.index(i if moves == 1 else MIRROR_Y[i])
                moving[pl.ds(16 * n + (column + 2) % 4, 4, stride=4), :] = value
            else:
                still[pl.ds(8 * Y_FLAT.index(i) + 2 - column, 4, stride=2), :] = value
    ghost_moving[...] = jnp.transpose(moving[...])
    ghost_still[...] = jnp.transpose(still[...])

    def inlet(row, outside_rows):
        us = [INLET * flow[pl.ds(rows * c + row, 8), :] for c in range(3)]
        eq = inlet_state(*us)
        solid = solidp[0, pl.ds(row, 8), :] > 0.5
        for i in range(19):
            j = OPP[i]
            source = streamed(j, 0)
            if source is None:
                value = jnp.where(solid, 0.0, eq[i])
            else:
                value = jnp.where(solid, post[j, source, pl.ds(row - DIRS[j][2], 8), :], eq[i])
            if outside_rows is not None:
                value = jnp.where(outside_rows, 0.0, value)
            if DIRS[i][1]:
                value = pltpu.roll(value, DIRS[i][1] % 128, 1)
            inlet2[i, pl.ds(row, 8), :] = value

    def out_copy(t):
        at = pl.ds(pl.multiple_of(t * 8, 8), 8)
        return pltpu.make_async_copy(state.at[:, :, at, :], state_out.at[:, :, at, :], sems.at[t])

    def last(t):
        row = pl.multiple_of(t * 8 + PAD, 8)
        us = [INLET * flow[pl.ds(rows * c + row, 8), :] for c in range(3)]
        eq = inlet_state(*us)
        solid = solidp[0, pl.ds(row, 8), :] > 0.5
        ends = (lane == 0) | (lane == 127)

        def read(i, source, ghost):
            at = pl.ds(row - DIRS[i][2], 8)
            v = inlet2[i, at, :] if source == 0 else post2[i, source - 1, at, :]
            where = ends if DIRS[i][1] == 0 else (lane < 2 if DIRS[i][1] == 1 else lane >= 126)
            return jnp.where(where, ghost, v)

        def write(i, x, value):
            if x == 0:
                value = jnp.where(solid, value, eq[i])
            state[i, x, pl.ds(row - PAD, 8), :] = value

        for i in Y_FLAT + Y_PLUS:
            both = [i] if DIRS[i][1] == 0 else [i, MIRROR_Y[i]]
            at = pl.ds(row - DIRS[i][2], 8)
            for source in range(4):
                targets = [x for x in range(4) if streamed(i, x) == source]
                if not targets:
                    continue
                if DIRS[i][1] == 0:
                    slot = 2 * (4 * Y_FLAT.index(i) + source)
                    ghost = pltpu.roll(ghost_still[at, :], (127 - slot) % 128, 1)
                else:
                    slot = 4 * (4 * Y_PLUS.index(i) + source)
                    ghost = pltpu.roll(ghost_moving[at, :], (126 - slot) % 128, 1)
                for j in both:
                    value = read(j, source, ghost)
                    for x in targets:
                        write(j, x, value)
            for j in both:
                if streamed(j, 0) is None:
                    write(j, 0, jnp.zeros((8, 128), jnp.float32))
        out_copy(t).start()

    inlet(PAD - 1, (sub == 0) & (kz == 0))
    inlet(top - 7, (sub == 7) & (kz == nz - 1))
    inlet(PAD, None)

    def main(t, carry):
        inlet(pl.multiple_of(t * 8 + PAD, 8), None)
        last(t - 1)
        return carry

    tiles = height // 8
    lax.fori_loop(1, tiles, main, 0)
    last(tiles - 1)
    for t in range(tiles):
        out_copy(t).wait()
    flow_copy.wait()


def swap_pairs(count, phase, distance=1):
    pairs = []
    for i in range(count):
        block = (i + phase * distance) // distance
        j = i + distance if block % 2 == 0 else i - distance
        if 0 <= j < count:
            pairs.append((i, j))
    return pairs


def ring_pairs(count, phase):
    if phase == 0:
        return [(i, i ^ 1) for i in range(count)]
    return [(i, (((i + 1) % count ^ 1) - 1) % count) for i in range(count)]


def vm(n):
    return [pl.BlockSpec(memory_space=pltpu.VMEM)] * n


def hbm(n):
    return [pl.BlockSpec(memory_space=pltpu.HBM)] * n


def f32(*shape):
    return jax.ShapeDtypeStruct(shape, jnp.float32)


def scratch(*shape):
    return pltpu.VMEM(shape, jnp.float32)


def flags(*shape):
    return pltpu.VMEM(shape, jnp.int32)


def params(mib):
    return pltpu.CompilerParams(vmem_limit_bytes=mib * 1024 * 1024)


def cost(flops, size):
    return pl.CostEstimate(flops=flops, bytes_accessed=size, transcendentals=0)


def shards(nz, ny, noise, mean_profile, lund_diag, lund_off, populations, mask):
    height, span = noise.shape[1], noise.shape[2]
    rows = height + 2 * PAD
    message = ROW_NOISE + 3 * height
    dma = pltpu.SemaphoreType.DMA
    here = lambda value: pltpu.with_memory_space_constraint(value, pltpu.HBM)
    mean_profile = mean_profile.reshape(1, height)
    operands = populations, mask, noise, mean_profile, lund_diag, lund_off

    za, zb = pl.pallas_call(
        lambda *refs: edge_kernel(nz, *refs),
        out_shape=(f32(message, 128), f32(message, 128)),
        in_specs=hbm(6),
        out_specs=vm(2),
        scratch_shapes=[
            scratch(19, 4, 16, 128), flags(4, 16, 128), scratch(1, height), scratch(3, height),
            scratch(3, height), scratch(20, 4, 16, 128), dma((13,)),
        ],
        compiler_params=params(8),
        name="edge_rows",
    )(*map(here, operands))

    z2 = pl.pallas_call(
        lambda *refs: far_kernel(height, *refs),
        out_shape=f32(16, 128),
        in_specs=vm(1),
        out_specs=pl.BlockSpec(memory_space=pltpu.VMEM),
        compiler_params=params(1),
        name="far_rows",
    )(za)

    ra = lax.ppermute(za, "gz", swap_pairs(nz, 0))
    rb = lax.ppermute(zb, "gz", swap_pairs(nz, 1))
    rc = lax.ppermute(z2, "gz", swap_pairs(nz, 0, 2))
    far = swap_pairs(nz, 1, 2)
    rd = lax.ppermute(z2, "gz", far) if far else jnp.zeros_like(z2)

    post, solidp, right_cols, left_cols = pl.pallas_call(
        lambda *refs: bulk_kernel(nz, *refs),
        out_shape=(f32(19, 4, rows, 128), f32(4, rows, 128), f32(rows, 128), f32(rows, 128)),
        in_specs=vm(2),
        out_specs=vm(4),
        compiler_params=params(4),
        cost_estimate=cost(4_000_000_000, 8_000_000),
        name="bulk",
    )(populations, mask)

    line = np.arange(rows) - PAD
    used = (line >= -1) & (line <= height)
    bandz = np.where(used[:, None], band(np.arange(-height, 2 * height), line).T, 0.0)
    post, solidp, ya, yb, linear, meanrow = pl.pallas_call(
        lambda *refs: column_kernel(nz, *refs),
        out_shape=(
            f32(19, 4, rows, 128), f32(4, rows, 128), f32(Y_MESSAGE, 128), f32(Y_MESSAGE, 128),
            f32(4, rows, 128), f32(8, 128),
        ),
        in_specs=vm(10),
        out_specs=vm(6),
        scratch_shapes=[
            scratch(3 * height, 384), scratch(rows, 384), scratch(3, 2, ROW_PARAM, 128),
            scratch(2, rows, 128),
        ],
        input_output_aliases={0: 0, 1: 1},
        compiler_params=params(4),
        name="columns",
    )(post, solidp, right_cols, left_cols, za, ra, rb, rc, rd, jnp.asarray(bandz, jnp.float32))

    qa = lax.ppermute(ya, ("gy", "col"), ring_pairs(ny, 0))
    qb = lax.ppermute(yb, ("gy", "col"), ring_pairs(ny, 1))

    own = np.arange(span)
    left = np.arange(128) % 64 - 64
    right = np.arange(128) % 64 + span
    source = np.concatenate([own, left, right])
    wy = jnp.asarray(band(source, own))
    wg = np.zeros((8, 384), np.float32)
    wg[0:4] = band(source, np.array([-1, 0, span - 1, span])).T
    wg = jnp.asarray(wg)
    post2, flow_own, ghost_own, own_right, own_left = pl.pallas_call(
        lambda *refs: interior_kernel(nz, *refs),
        out_shape=(
            f32(19, 3, rows, 128), f32(3 * rows, 128), f32(24, 128), f32(144, 128), f32(144, 128),
        ),
        in_specs=vm(7),
        out_specs=vm(5),
        scratch_shapes=[scratch(2, 128, 128)],
        compiler_params=params(4),
        cost_estimate=cost(4_000_000_000, 8_000_000),
        name="interior",
    )(post, solidp, linear, ya, yb, wy, wg)
    inflow, state = pl.pallas_call(
        lambda *refs: final_kernel(nz, *refs),
        out_shape=(f32(3, height, span), f32(19, 4, height, span)),
        in_specs=vm(12),
        out_specs=hbm(2),
        scratch_shapes=[
            scratch(3 * rows, 256), scratch(3 * rows, 128), scratch(19, rows, 128),
            scratch(144, 128), scratch(144, 128), scratch(128, 128), scratch(128, 128),
            scratch(128, 128), scratch(128, 128), scratch(19, 4, height, span),
            scratch(3, height, span), scratch(2, 128, 128), dma((height // 8 + 1,)),
        ],
        compiler_params=params(8),
        name="stream",
    )(post, solidp, post2, flow_own, ghost_own, own_right, own_left, meanrow, qa, qb, wy, wg)
    return inflow, state


def solution(mesh):
    nz = mesh.shape["gz"]
    ny = mesh.shape["gy"] * mesh.shape["col"]
    in_specs = (
        P(None, "gz", ("gy", "col")),
        P("gz"),
        P(None, "gz"),
        P(None, "gz"),
        P(None, None, "gz", ("gy", "col")),
        P(None, "gz", ("gy", "col")),
    )
    out_specs = (P(None, "gz", ("gy", "col")), P(None, None, "gz", ("gy", "col")))

    def body(*args):
        return shards(nz, ny, *args)

    return jax.shard_map(body, mesh=mesh, in_specs=in_specs, out_specs=out_specs, check_vma=False)
```

```python
import math

import jax
import jax.numpy as jnp
import numpy as np
from jax import lax
from jax.experimental import pallas as pl
from jax.experimental.pallas import tpu as pltpu
from jax.sharding import PartitionSpec as P

HW = 64
DIRS = [
    (0, 0, 0),
    (1, 0, 0), (-1, 0, 0), (0, 1, 0), (0, -1, 0), (0, 0, 1), (0, 0, -1),
    (1, 1, 0), (-1, -1, 0), (1, -1, 0), (-1, 1, 0),
    (1, 0, 1), (-1, 0, -1), (1, 0, -1), (-1, 0, 1),
    (0, 1, 1), (0, -1, -1), (0, 1, -1), (0, -1, 1),
]
OPP = [DIRS.index((-a, -b, -c)) for a, b, c in DIRS]
MIRROR_Y = [DIRS.index((a, -b, c)) for a, b, c in DIRS]
MIRROR_Z = [DIRS.index((a, b, -c)) for a, b, c in DIRS]
INLET = 0.05

Z_EDGE = [i for i in range(19) if DIRS[i][2] == 0] + [i for i in range(19) if DIRS[i][2] == 1]
Z_SECOND = [i for i in range(19) if DIRS[i][2] == 1]
Y_FLAT = [i for i in range(19) if DIRS[i][1] == 0]
Y_PLUS = [i for i in range(19) if DIRS[i][1] == 1]
FLAG_PLANE = 4 * len(Y_FLAT)
LANE_PLUS = 2 * FLAG_PLANE + 8

ROW_SOLID = 76
ROW_PARAM = 80
ROW_NOISE = 88
PAD = 8
FIRST = PAD - 2
Y_HALF = 34
Y_FAR = 2
Y_FILTER = 8
Y_MESSAGE = 112


def taps():
    k = np.arange(-HW, HW + 1).astype(np.float64)
    raw = np.exp(-math.pi * k * k / (2.0 * (HW // 2) ** 2))
    return raw / np.sqrt(np.sum(raw * raw))


def band(source, target):
    values = taps()
    offset = np.asarray(source)[:, None] - np.asarray(target)[None, :]
    inside = np.abs(offset) <= HW
    return np.where(inside, values[np.clip(offset + HW, 0, 2 * HW)], 0.0).astype(np.float32)


def moments(g):
    s = {a: g[a] + g[a + 1] for a in range(1, 19, 2)}
    d = {a: g[a] - g[a + 1] for a in range(1, 19, 2)}
    w1, w2 = 1.0 / 18.0, 1.0 / 36.0
    rho = (
        g[0] * (1.0 / 3.0)
        + (s[1] + s[3] + s[5]) * w1
        + ((s[7] + s[9]) + (s[11] + s[13]) + (s[15] + s[17])) * w2
    )
    mx = d[1] * w1 + ((d[7] + d[9]) + (d[11] + d[13])) * w2
    my = d[3] * w1 + ((d[7] - d[9]) + (d[15] + d[17])) * w2
    mz = d[5] * w1 + ((d[11] - d[13]) + (d[15] - d[17])) * w2
    return rho, mx, my, mz


def pair_vector(a, vx, vy, vz):
    total = None
    for c, v in zip(DIRS[a], (vx, vy, vz)):
        if c:
            term = v if c > 0 else -v
            total = term if total is None else (total + v if c > 0 else total - v)
    return total


def collide(g, solid, keep=range(19)):
    rho, mx, my, mz = moments(g)
    inv = 1.0 / rho
    ux, uy, uz = mx * inv, my * inv, mz * inv
    square = mx * ux + my * uy + mz * uz
    base = 1.25 * rho - 1.875 * square
    post = [None] * 19
    if 0 in keep:
        post[0] = jnp.where(solid, g[0], base - 0.25 * g[0])
    for a in range(1, 19, 2):
        if a not in keep and a + 1 not in keep:
            continue
        m = pair_vector(a, mx, my, mz)
        p = pair_vector(a, ux, uy, uz)
        even = base + 5.625 * (m * p)
        odd = 3.75 * m
        if a in keep:
            post[a] = jnp.where(solid, g[a + 1], (even + odd) - 0.25 * g[a])
        if a + 1 in keep:
            post[a + 1] = jnp.where(solid, g[a], (even - odd) - 0.25 * g[a + 1])
    return post


def inlet_state(ux, uy, uz):
    base = 1.0 - 1.5 * (ux * ux + uy * uy + uz * uz)
    out = [base] * 19
    for a in range(1, 19, 2):
        p = pair_vector(a, ux, uy, uz)
        even = base + 4.5 * (p * p)
        odd = 3.0 * p
        out[a] = even + odd
        out[a + 1] = even - odd
    return out


def wall_rows(first_row, height, kz, nz):
    rows = lax.broadcasted_iota(jnp.int32, (8, 128), 0) + first_row
    return ((rows == 0) & (kz == 0)) | ((rows == height - 1) & (kz == nz - 1))


def edge_kernel(
    nz, pops, mask, noise, mean, diag, off, za, zb, raw, flags, mean_v, diag_v, off_v, edge, sems
):
    height = pops.shape[2]
    kz = lax.axis_index("gz")
    upward = lax.rem(kz, 2) == 0
    upper = pl.ds(height - 8, 8)
    copies = [
        (pops.at[:, :, 0:8, :], raw.at[:, :, 0:8, :]),
        (pops.at[:, :, upper, :], raw.at[:, :, 8:16, :]),
        (mask.at[:, 0:8, :], flags.at[:, 0:8, :]),
        (mask.at[:, upper, :], flags.at[:, 8:16, :]),
        (mean, mean_v),
        (diag, diag_v),
        (off, off_v),
    ]
    for c in range(3):
        at = slice(ROW_NOISE + height * c, ROW_NOISE + height * (c + 1))
        copies.append((noise.at[c], za.at[at, :]))
        copies.append((noise.at[c], zb.at[at, :]))
    copies = [pltpu.make_async_copy(src, dst, sems.at[n]) for n, (src, dst) in enumerate(copies)]
    for copy in copies:
        copy.start()
    for copy in copies[:4]:
        copy.wait()
    for part, row in ((0, 0), (1, height - 8)):
        wall = wall_rows(row, height, kz, nz)
        at = slice(8 * part, 8 * part + 8)
        for x in range(4):
            solid = (flags[x, at, :] == 1) | wall
            post = collide([raw[i, x, at, :] for i in range(19)], solid)
            for i in range(19):
                edge[i, x, at, :] = post[i]
            edge[19, x, at, :] = solid.astype(jnp.float32)

    def put(row, up, down):
        za[row : row + 1, :] = jnp.where(upward, up, down)
        zb[row : row + 1, :] = jnp.where(upward, down, up)

    q = 0
    for i in Z_EDGE:
        for x in range(4):
            put(4 * q + x, edge[i, x, 15:16, :], edge[MIRROR_Z[i], x, 0:1, :])
        q += 1
    for i in Z_SECOND:
        for x in range(4):
            put(4 * q + x, edge[i, x, 14:15, :], edge[MIRROR_Z[i], x, 1:2, :])
        q += 1
    for x in range(4):
        put(4 * q + x, edge[19, x, 15:16, :], edge[19, x, 0:1, :])
    for copy in copies[4:]:
        copy.wait()
    for ref in (za, zb):
        ref[ROW_PARAM : ROW_PARAM + 8, :] = jnp.zeros((8, 128), jnp.float32)
        ref[ROW_PARAM : ROW_PARAM + 1, 0:height] = mean_v[...]
        ref[ROW_PARAM + 1 : ROW_PARAM + 4, 0:height] = diag_v[...]
        ref[ROW_PARAM + 4 : ROW_PARAM + 7, 0:height] = off_v[...]


def far_kernel(height, za, z2):
    kz = lax.axis_index("gz")
    low_half = lax.rem(kz, 4) < 2
    z2[...] = jnp.zeros((16, 128), jnp.float32)
    for c in range(3):
        base = ROW_NOISE + height * c
        last = za[base + height - 1 : base + height, :]
        first = za[base : base + 1, :]
        z2[c : c + 1, :] = jnp.where(low_half, last, first)
        z2[8 + c : 9 + c, :] = jnp.where(low_half, first, last)


def dot3(a, b, dims=(((1,), (0,)), ((), ()))):
    a_hi, b_hi = a.astype(jnp.bfloat16), b.astype(jnp.bfloat16)
    a_lo = (a - a_hi.astype(jnp.float32)).astype(jnp.bfloat16)
    b_lo = (b - b_hi.astype(jnp.float32)).astype(jnp.bfloat16)

    def dot(u, v):
        return lax.dot_general(u, v, dims, preferred_element_type=jnp.float32)

    return dot(a_hi, b_hi) + (dot(a_lo, b_hi) + dot(a_hi, b_lo))


NT = (((1,), (1,)), ((), ()))


def put_pair(pair, slot, value, first_column, into):
    return jnp.where(pair == slot, pltpu.roll(value, (2 * slot - first_column) % 128, 1), into)


def bulk_kernel(nz, pops, mask, post, solidp, ya, yb):
    height = pops.shape[2]
    kz = lax.axis_index("gz")
    ky = lax.axis_index("gy") * lax.axis_size("col") + lax.axis_index("col")
    y_even = lax.rem(ky, 2) == 0
    pair = lax.broadcasted_iota(jnp.int32, (8, 128), 1) // 2

    def body(t, carry):
        row = pl.multiple_of(t * 8, 8)
        out = pl.ds(row + PAD, 8)
        wall = wall_rows(row, height, kz, nz)
        flat = right = left = jnp.zeros((8, 128), jnp.float32)
        for x in range(4):
            solid = (mask[x, pl.ds(row, 8), :] == 1) | wall
            p = collide([pops[i, x, pl.ds(row, 8), :] for i in range(19)], solid)
            flag = solid.astype(jnp.float32)
            solidp[x, out, :] = flag
            flat = put_pair(pair, FLAG_PLANE + x, flag, 127, flat)
            for q, i in enumerate(Y_FLAT):
                post[i, x, out, :] = p[i]
                flat = put_pair(pair, 4 * q + x, p[i], 127, flat)
            for n, i in enumerate(Y_PLUS):
                j = MIRROR_Y[i]
                slot = LANE_PLUS // 2 + 4 * n + x
                post[i, x, out, :] = pltpu.roll(p[i], 1, 1)
                post[j, x, out, :] = pltpu.roll(p[j], 127, 1)
                right = put_pair(pair, slot, p[i], 126, right)
                left = put_pair(pair, slot, p[j], 0, left)
        right = jnp.where(pair < LANE_PLUS // 2, flat, right)
        left = jnp.where(pair < LANE_PLUS // 2, flat, left)
        ya[pl.ds(row, 8), :] = jnp.where(y_even, right, left)
        yb[pl.ds(row, 8), :] = jnp.where(y_even, left, right)
        return carry

    lax.fori_loop(0, height // 8, body, 0)


def column_kernel(
    nz, post_in, solid_in, sent, za, zb, z2c, z2d, bandz, pick,
    post, solidp, ya, yb, linear, meanrow,
    wide, filt, moved,
):
    height = post.shape[2] - 2 * PAD
    rows = height + 2 * PAD
    kz = lax.axis_index("gz")
    ky = lax.axis_index("gy") * lax.axis_size("col") + lax.axis_index("col")
    z_even = lax.rem(kz, 2) == 0
    y_even = lax.rem(ky, 2) == 0
    low_half = lax.rem(kz, 4) < 2

    def below(row, n=1):
        return jnp.where(z_even, zb[row : row + n, :], za[row : row + n, :])

    def above(row, n=1):
        return jnp.where(z_even, za[row : row + n, :], zb[row : row + n, :])

    top = PAD + height
    low, high = below(0, ROW_PARAM), above(0, ROW_PARAM)
    for n, shift in enumerate((0, 1, 127)):
        moved[n, 0] = low if shift == 0 else pltpu.roll(low, shift, 1)
        moved[n, 1] = high if shift == 0 else pltpu.roll(high, shift, 1)
    for items, first, depth in ((Z_EDGE, 0, 0), (Z_SECOND, len(Z_EDGE), 1)):
        for q, i in enumerate(items):
            n = DIRS[i][1] % 3
            for x in range(4):
                at = slice(4 * (first + q) + x, 4 * (first + q) + x + 1)
                post[i, x, PAD - 1 - depth : PAD - depth, :] = moved[n, 0, at, :]
                post[MIRROR_Z[i], x, top + depth : top + depth + 1, :] = moved[n, 1, at, :]
    for x in range(4):
        solidp[x, PAD - 1 : PAD, :] = moved[0, 0, ROW_SOLID + x : ROW_SOLID + x + 1, :]
        solidp[x, top : top + 1, :] = moved[0, 1, ROW_SOLID + x : ROW_SOLID + x + 1, :]

    lane = lax.broadcasted_iota(jnp.int32, (8, 128), 1)
    own_par = pltpu.roll(sent[ROW_PARAM : ROW_PARAM + 8, :], PAD, 1)
    low_par = pltpu.roll(below(ROW_PARAM, 8), 128 - height + PAD, 1)
    high_par = pltpu.roll(above(ROW_PARAM, 8), height + PAD, 1)
    par = jnp.where(lane < PAD, low_par, jnp.where(lane < top, own_par, high_par))
    par = jnp.where(lane < rows, par, 0.0)
    meanrow[...] = par
    cols = jnp.transpose(jnp.concatenate([par] * 16, axis=0))[0:rows]

    for c in range(3):
        lanes = slice(128 * c, 128 * c + 128)
        at = slice(ROW_NOISE + height * c, ROW_NOISE + height * (c + 1))
        wide[0:height, lanes] = below(ROW_NOISE + height * c, height)
        wide[height : 2 * height, lanes] = sent[at, :]
        wide[2 * height : 3 * height, lanes] = above(ROW_NOISE + height * c, height)
    filt[...] = dot3(bandz[...], wide[...])
    b_end = float(taps()[0])
    far_low = jnp.where(low_half, z2d[8:16, :], z2c[0:8, :])
    far_high = jnp.where(low_half, z2c[0:8, :], z2d[8:16, :])
    for c in range(3):
        lanes = slice(128 * c, 128 * c + 128)
        filt[PAD - 1 : PAD, lanes] += b_end * far_low[c : c + 1, :]
        filt[top : top + 1, lanes] += b_end * far_high[c : c + 1, :]
    f0, f1, f2 = (filt[:, 128 * c : 128 * c + 128] for c in range(3))
    linear[0] = cols[:, 1:2] * f0
    linear[1] = cols[:, 4:5] * f0 + cols[:, 2:3] * f1
    linear[2] = cols[:, 5:6] * f0 + cols[:, 6:7] * f1 + cols[:, 3:4] * f2
    linear[3] = jnp.broadcast_to(cols[:, 0:1], (rows, 128))

    pair = lane // 2
    for row in (0, rows - 8):
        out = slice(row, row + 8)
        flat = right = left = jnp.zeros((8, 128), jnp.float32)
        for x in range(4):
            flat = put_pair(pair, FLAG_PLANE + x, solidp[x, out, :], 127, flat)
            for q, i in enumerate(Y_FLAT):
                flat = put_pair(pair, 4 * q + x, post[i, x, out, :], 127, flat)
            for n, i in enumerate(Y_PLUS):
                slot = LANE_PLUS // 2 + 4 * n + x
                right = put_pair(pair, slot, post[i, x, out, :], 127, right)
                left = put_pair(pair, slot, post[MIRROR_Y[i], x, out, :], 127, left)
        right = jnp.where(pair < LANE_PLUS // 2, flat, right)
        left = jnp.where(pair < LANE_PLUS // 2, flat, left)
        at = slice(0, 2) if row else slice(6, 8)
        ya[at, :] = jnp.where(y_even, right, left)[at, :]
        yb[at, :] = jnp.where(y_even, left, right)[at, :]
    spare = jnp.zeros((1, 128), jnp.float32)
    for c in range(3):
        far = dot3(pick[...], linear[c], NT)
        far = jnp.concatenate([far, jnp.zeros((8, 128 - rows), jnp.float32)], axis=1)
        ya[Y_FAR + c : Y_FAR + c + 1, :] = jnp.where(y_even, far[0:1, :], far[1:2, :])
        yb[Y_FAR + c : Y_FAR + c + 1, :] = jnp.where(y_even, far[1:2, :], far[0:1, :])
    for ref in (ya, yb):
        ref[5:6, :] = spare
        ref[Y_FILTER + 3 * Y_HALF : Y_MESSAGE, :] = jnp.zeros((2, 128), jnp.float32)
    middle = FIRST + Y_HALF
    lane_h = lax.broadcasted_iota(jnp.int32, (Y_HALF, 128), 1)
    for c in range(3):
        first, second = linear[c, FIRST:middle, :], linear[c, middle : middle + Y_HALF, :]
        left = jnp.where(lane_h < 64, first, pltpu.roll(second, 64, 1))
        right = jnp.where(lane_h < 64, pltpu.roll(first, 64, 1), second)
        at = slice(Y_FILTER + Y_HALF * c, Y_FILTER + Y_HALF * (c + 1))
        ya[at, :] = jnp.where(y_even, right, left)
        yb[at, :] = jnp.where(y_even, left, right)


def streamed(i, x):
    source = x - DIRS[i][0]
    return None if source < 0 else min(source, 3)


def assemble(tall, sa, sb, ya, yb, a_first):
    end = PAD + sa.shape[0]
    for out, source, a, b in (
        (slice(PAD, end), slice(0, sa.shape[0]), sa, sb),
        (slice(PAD - 2, PAD), slice(6, 8), ya, yb),
        (slice(end, end + 2), slice(0, 2), ya, yb),
    ):
        tall[0, out, :] = jnp.where(a_first, a[source, :], b[source, :])
        tall[1, out, :] = jnp.where(a_first, b[source, :], a[source, :])


def interior_kernel(
    nz, post, solidp, linear, sa, sb, ya, yb, wy, wg, post2, flow_own, ghost_own, own_right, own_left, tall
):
    rows = post.shape[2]
    top = rows - PAD
    kz = lax.axis_index("gz")
    ky = lax.axis_index("gy") * lax.axis_size("col") + lax.axis_index("col")
    y_even = lax.rem(ky, 2) == 0
    sub = lax.broadcasted_iota(jnp.int32, (8, 128), 0)

    def step(row, outside):
        for x in range(1, 4):
            solid = solidp[x, pl.ds(row, 8), :] > 0.5
            g = [post[i, streamed(i, x), pl.ds(row - DIRS[i][2], 8), :] for i in range(19)]
            p = collide(g, solid)
            for i in range(19):
                value = p[i] if outside is None else jnp.where(outside, 0.0, p[i])
                if DIRS[i][1]:
                    value = pltpu.roll(value, DIRS[i][1] % 128, 1)
                post2[i, x - 1, pl.ds(row, 8), :] = value

    step(PAD - 1, (sub == 0) & (kz == 0))
    step(top - 7, (sub == 7) & (kz == nz - 1))

    def body(t, carry):
        step(pl.multiple_of(t * 8 + PAD, 8), None)
        return carry

    lax.fori_loop(0, rows // 8 - 2, body, 0)

    flow_own[...] = dot3(linear[0:3].reshape(3 * rows, 128), wy[0:128, :])
    flow_own[0:rows, :] += linear[3]
    for c in range(3):
        ghost_own[8 * c : 8 * c + 8, 0:rows] = dot3(wg[:, 0:128], linear[c], NT)
        ghost_own[8 * c : 8 * c + 8, rows:128] = jnp.zeros((8, 128 - rows), jnp.float32)
    assemble(tall, sa, sb, ya, yb, y_even)
    own_right[0:128, :] = jnp.transpose(tall[0])
    own_left[0:128, :] = jnp.transpose(tall[1])


def final_kernel(
    nz, post, solidp, post2, flow_own, ghost_own, own_right, own_left, meanrow, sa, sb, ya, yb, wy, wg,
    inflow, state_out,
    lhs, flow, inlet2, strip_left, strip_right, moving, still, ghost_moving, ghost_still,
    state, flow_out, tall, sems,
):
    height = state.shape[2]
    rows = height + 2 * PAD
    top = PAD + height
    kz = lax.axis_index("gz")
    ky = lax.axis_index("gy") * lax.axis_size("col") + lax.axis_index("col")
    y_even = lax.rem(ky, 2) == 0
    lane = lax.broadcasted_iota(jnp.int32, (8, 128), 1)
    sub = lax.broadcasted_iota(jnp.int32, (8, 128), 0)

    assemble(tall, sa, sb, ya, yb, jnp.logical_not(y_even))
    strip_left[0:128, :] = jnp.transpose(tall[0])
    strip_right[0:128, :] = jnp.transpose(tall[1])

    lane_h = lax.broadcasted_iota(jnp.int32, (Y_HALF, 128), 1)
    for c in range(3):
        at = slice(Y_FILTER + Y_HALF * c, Y_FILTER + Y_HALF * (c + 1))
        a, b = ya[at, :], yb[at, :]
        left, right = jnp.where(y_even, b, a), jnp.where(y_even, a, b)
        middle = rows * c + FIRST + Y_HALF
        lo, hi = slice(middle - Y_HALF, middle), slice(middle, middle + Y_HALF)
        lhs[lo, 0:128] = jnp.where(lane_h < 64, left, 0.0)
        lhs[hi, 0:128] = jnp.where(lane_h < 64, 0.0, left)
        lhs[lo, 128:256] = jnp.where(lane_h < 64, right, 0.0)
        lhs[hi, 128:256] = jnp.where(lane_h < 64, 0.0, right)
    flow[...] = flow_own[...] + dot3(lhs[...], wy[128:384, :])
    for c in range(3):
        flow_out[c] = flow[rows * c + PAD : rows * c + top, :]
    flow_copy = pltpu.make_async_copy(flow_out, inflow, sems.at[height // 8])
    flow_copy.start()
    b_end = float(taps()[0])
    column_flow = []
    for c in range(3):
        g = dot3(wg[:, 128:384], lhs[rows * c : rows * (c + 1), :], NT)
        g = jnp.concatenate([g, jnp.zeros((8, 128 - rows), jnp.float32)], axis=1)
        g = g + ghost_own[8 * c : 8 * c + 8, :]
        far = slice(Y_FAR + c, Y_FAR + c + 1)
        at = [g[n : n + 1, :] for n in range(4)]
        at[0] = at[0] + b_end * jnp.where(y_even, yb[far, :], ya[far, :])
        at[3] = at[3] + b_end * jnp.where(y_even, ya[far, :], yb[far, :])
        if c == 0:
            at = [v + meanrow[0:1, :] for v in at]
        column_flow.append(at)

    outside = ((lane < PAD) & (kz == 0)) | ((lane >= top) & (kz == nz - 1))
    sources = (
        ((strip_left, 0), (strip_left, 0), (own_left, 0)),
        ((own_left, 1), (strip_left, 1), (own_left, 1)),
        ((own_right, 0), (own_right, 0), (strip_right, 0)),
        ((strip_right, 1), (own_right, 1), (strip_right, 1)),
    )
    for column in range(4):
        def rows_of(start):
            return pl.ds(start, 8, stride=2)

        src, odd = sources[column][0]
        solid = src[rows_of(2 * FLAG_PLANE + odd), :] > 0.5
        g = [None] * 19
        for i in range(19):
            cx, cy, cz = DIRS[i]
            src, odd = sources[column][cy % 3]
            if cy == 0:
                start = 8 * Y_FLAT.index(i) + odd
            else:
                start = LANE_PLUS + 8 * Y_PLUS.index(i if cy == 1 else MIRROR_Y[i]) + odd
            v = src[rows_of(start - 2 * cx), :]
            if cx == 1:
                v = jnp.where(sub == 0, 0.0, v)
            elif cx == -1:
                v = jnp.where(sub == 3, src[rows_of(start), :], v)
            g[i] = v if cz == 0 else pltpu.roll(v, cz % 128, 1)
        us = [INLET * jnp.broadcast_to(column_flow[c][column], (8, 128)) for c in range(3)]
        eq = inlet_state(*us)
        put = (sub == 0) & jnp.logical_not(solid)
        moves = 1 if column < 2 else -1
        keep = [i for i in range(19) if DIRS[i][1] == moves or (DIRS[i][1] == 0 and column in (1, 2))]
        p = collide(g, solid, keep)
        for i in keep:
            value = jnp.where(outside, 0.0, jnp.where(put, eq[i], p[i]))[0:4, :]
            if DIRS[i][1]:
                n = Y_PLUS.index(i if moves == 1 else MIRROR_Y[i])
                moving[pl.ds(16 * n + (column + 2) % 4, 4, stride=4), :] = value
            else:
                still[pl.ds(8 * Y_FLAT.index(i) + 2 - column, 4, stride=2), :] = value
    ghost_moving[...] = jnp.transpose(moving[...])
    ghost_still[...] = jnp.transpose(still[...])

    def inlet(row, outside_rows):
        us = [INLET * flow[pl.ds(rows * c + row, 8), :] for c in range(3)]
        eq = inlet_state(*us)
        solid = solidp[0, pl.ds(row, 8), :] > 0.5
        for i in range(19):
            j = OPP[i]
            source = streamed(j, 0)
            if source is None:
                value = jnp.where(solid, 0.0, eq[i])
            else:
                value = jnp.where(solid, post[j, source, pl.ds(row - DIRS[j][2], 8), :], eq[i])
            if outside_rows is not None:
                value = jnp.where(outside_rows, 0.0, value)
            if DIRS[i][1]:
                value = pltpu.roll(value, DIRS[i][1] % 128, 1)
            inlet2[i, pl.ds(row, 8), :] = value

    def out_copy(t):
        at = pl.ds(pl.multiple_of(t * 8, 8), 8)
        return pltpu.make_async_copy(state.at[:, :, at, :], state_out.at[:, :, at, :], sems.at[t])

    def last(t):
        row = pl.multiple_of(t * 8 + PAD, 8)
        us = [INLET * flow[pl.ds(rows * c + row, 8), :] for c in range(3)]
        eq = inlet_state(*us)
        solid = solidp[0, pl.ds(row, 8), :] > 0.5
        ends = (lane == 0) | (lane == 127)

        def read(i, source, ghost):
            at = pl.ds(row - DIRS[i][2], 8)
            v = inlet2[i, at, :] if source == 0 else post2[i, source - 1, at, :]
            where = ends if DIRS[i][1] == 0 else (lane < 2 if DIRS[i][1] == 1 else lane >= 126)
            return jnp.where(where, ghost, v)

        def write(i, x, value):
            if x == 0:
                value = jnp.where(solid, value, eq[i])
            state[i, x, pl.ds(row - PAD, 8), :] = value

        for i in Y_FLAT + Y_PLUS:
            both = [i] if DIRS[i][1] == 0 else [i, MIRROR_Y[i]]
            at = pl.ds(row - DIRS[i][2], 8)
            for source in range(4):
                targets = [x for x in range(4) if streamed(i, x) == source]
                if not targets:
                    continue
                if DIRS[i][1] == 0:
                    slot = 2 * (4 * Y_FLAT.index(i) + source)
                    ghost = pltpu.roll(ghost_still[at, :], (127 - slot) % 128, 1)
                else:
                    slot = 4 * (4 * Y_PLUS.index(i) + source)
                    ghost = pltpu.roll(ghost_moving[at, :], (126 - slot) % 128, 1)
                for j in both:
                    value = read(j, source, ghost)
                    for x in targets:
                        write(j, x, value)
            for j in both:
                if streamed(j, 0) is None:
                    write(j, 0, jnp.zeros((8, 128), jnp.float32))
        out_copy(t).start()

    inlet(PAD - 1, (sub == 0) & (kz == 0))
    inlet(top - 7, (sub == 7) & (kz == nz - 1))
    inlet(PAD, None)

    def main(t, carry):
        inlet(pl.multiple_of(t * 8 + PAD, 8), None)
        last(t - 1)
        return carry

    tiles = height // 8
    lax.fori_loop(1, tiles, main, 0)
    last(tiles - 1)
    for t in range(tiles):
        out_copy(t).wait()
    flow_copy.wait()


def swap_pairs(count, phase, distance=1):
    pairs = []
    for i in range(count):
        block = (i + phase * distance) // distance
        j = i + distance if block % 2 == 0 else i - distance
        if 0 <= j < count:
            pairs.append((i, j))
    return pairs


def ring_pairs(count, phase):
    if phase == 0:
        return [(i, i ^ 1) for i in range(count)]
    return [(i, (((i + 1) % count ^ 1) - 1) % count) for i in range(count)]


def vm(n):
    return [pl.BlockSpec(memory_space=pltpu.VMEM)] * n


def hbm(n):
    return [pl.BlockSpec(memory_space=pltpu.HBM)] * n


def f32(*shape):
    return jax.ShapeDtypeStruct(shape, jnp.float32)


def scratch(*shape):
    return pltpu.VMEM(shape, jnp.float32)


def flags(*shape):
    return pltpu.VMEM(shape, jnp.int32)


def params(mib):
    return pltpu.CompilerParams(vmem_limit_bytes=mib * 1024 * 1024)


def cost(flops, size):
    return pl.CostEstimate(flops=flops, bytes_accessed=size, transcendentals=0)


def shards(nz, ny, noise, mean_profile, lund_diag, lund_off, populations, mask):
    height, span = noise.shape[1], noise.shape[2]
    rows = height + 2 * PAD
    message = ROW_NOISE + 3 * height
    dma = pltpu.SemaphoreType.DMA
    here = lambda value: pltpu.with_memory_space_constraint(value, pltpu.HBM)
    mean_profile = mean_profile.reshape(1, height)
    operands = populations, mask, noise, mean_profile, lund_diag, lund_off

    za, zb = pl.pallas_call(
        lambda *refs: edge_kernel(nz, *refs),
        out_shape=(f32(message, 128), f32(message, 128)),
        in_specs=hbm(6),
        out_specs=vm(2),
        scratch_shapes=[
            scratch(19, 4, 16, 128), flags(4, 16, 128), scratch(1, height), scratch(3, height),
            scratch(3, height), scratch(20, 4, 16, 128), dma((13,)),
        ],
        compiler_params=params(8),
        name="edge_rows",
    )(*map(here, operands))

    z2 = pl.pallas_call(
        lambda *refs: far_kernel(height, *refs),
        out_shape=f32(16, 128),
        in_specs=vm(1),
        out_specs=pl.BlockSpec(memory_space=pltpu.VMEM),
        compiler_params=params(1),
        name="far_rows",
    )(za)

    ra = lax.ppermute(za, "gz", swap_pairs(nz, 0))
    rb = lax.ppermute(zb, "gz", swap_pairs(nz, 1))
    rc = lax.ppermute(z2, "gz", swap_pairs(nz, 0, 2))
    far = swap_pairs(nz, 1, 2)
    rd = lax.ppermute(z2, "gz", far) if far else jnp.zeros_like(z2)

    post, solidp, sa, sb = pl.pallas_call(
        lambda *refs: bulk_kernel(nz, *refs),
        out_shape=(f32(19, 4, rows, 128), f32(4, rows, 128), f32(height, 128), f32(height, 128)),
        in_specs=vm(2),
        out_specs=vm(4),
        compiler_params=params(4),
        cost_estimate=cost(4_000_000_000, 8_000_000),
        name="bulk",
    )(populations, mask)

    pa = lax.ppermute(sa, ("gy", "col"), ring_pairs(ny, 0))
    pb = lax.ppermute(sb, ("gy", "col"), ring_pairs(ny, 1))
    pick = np.zeros((8, 128), np.float32)
    pick[0, span - HW - 1] = pick[1, HW] = 1.0

    line = np.arange(rows) - PAD
    used = (line >= -1) & (line <= height)
    bandz = np.where(used[:, None], band(np.arange(-height, 2 * height), line).T, 0.0)
    post, solidp, ya, yb, linear, meanrow = pl.pallas_call(
        lambda *refs: column_kernel(nz, *refs),
        out_shape=(
            f32(19, 4, rows, 128), f32(4, rows, 128), f32(Y_MESSAGE, 128), f32(Y_MESSAGE, 128),
            f32(4, rows, 128), f32(8, 128),
        ),
        in_specs=vm(9),
        out_specs=vm(6),
        scratch_shapes=[
            scratch(3 * height, 384), scratch(rows, 384), scratch(3, 2, ROW_PARAM, 128),
        ],
        input_output_aliases={0: 0, 1: 1},
        compiler_params=params(4),
        name="columns",
    )(post, solidp, za, ra, rb, rc, rd, jnp.asarray(bandz, jnp.float32), jnp.asarray(pick))

    qa = lax.ppermute(ya, ("gy", "col"), ring_pairs(ny, 0))
    qb = lax.ppermute(yb, ("gy", "col"), ring_pairs(ny, 1))

    own = np.arange(span)
    left = np.arange(128) % 64 - 64
    right = np.arange(128) % 64 + span
    source = np.concatenate([own, left, right])
    wy = jnp.asarray(band(source, own))
    wg = np.zeros((8, 384), np.float32)
    wg[0:4] = band(source, np.array([-1, 0, span - 1, span])).T
    wg = jnp.asarray(wg)
    post2, flow_own, ghost_own, own_right, own_left = pl.pallas_call(
        lambda *refs: interior_kernel(nz, *refs),
        out_shape=(
            f32(19, 3, rows, 128), f32(3 * rows, 128), f32(24, 128), f32(144, 128), f32(144, 128),
        ),
        in_specs=vm(9),
        out_specs=vm(5),
        scratch_shapes=[scratch(2, 128, 128)],
        compiler_params=params(4),
        cost_estimate=cost(4_000_000_000, 8_000_000),
        name="interior",
    )(post, solidp, linear, sa, sb, ya, yb, wy, wg)
    inflow, state = pl.pallas_call(
        lambda *refs: final_kernel(nz, *refs),
        out_shape=(f32(3, height, span), f32(19, 4, height, span)),
        in_specs=vm(14),
        out_specs=hbm(2),
        scratch_shapes=[
            scratch(3 * rows, 256), scratch(3 * rows, 128), scratch(19, rows, 128),
            scratch(144, 128), scratch(144, 128), scratch(128, 128), scratch(128, 128),
            scratch(128, 128), scratch(128, 128), scratch(19, 4, height, span),
            scratch(3, height, span), scratch(2, 128, 128), dma((height // 8 + 1,)),
        ],
        compiler_params=params(8),
        name="stream",
    )(post, solidp, post2, flow_own, ghost_own, own_right, own_left, meanrow, pa, pb, qa, qb, wy, wg)
    return inflow, state


def solution(mesh):
    nz = mesh.shape["gz"]
    ny = mesh.shape["gy"] * mesh.shape["col"]
    in_specs = (
        P(None, "gz", ("gy", "col")),
        P("gz"),
        P(None, "gz"),
        P(None, "gz"),
        P(None, None, "gz", ("gy", "col")),
        P(None, "gz", ("gy", "col")),
    )
    out_specs = (P(None, "gz", ("gy", "col")), P(None, None, "gz", ("gy", "col")))

    def body(*args):
        return shards(nz, ny, *args)

    return jax.shard_map(body, mesh=mesh, in_specs=in_specs, out_specs=out_specs, check_vma=False)
```

```python
import math

import jax
import jax.numpy as jnp
import numpy as np
from jax import lax
from jax.experimental import pallas as pl
from jax.experimental.pallas import tpu as pltpu
from jax.sharding import PartitionSpec as P

HW = 64
DIRS = [
    (0, 0, 0),
    (1, 0, 0), (-1, 0, 0), (0, 1, 0), (0, -1, 0), (0, 0, 1), (0, 0, -1),
    (1, 1, 0), (-1, -1, 0), (1, -1, 0), (-1, 1, 0),
    (1, 0, 1), (-1, 0, -1), (1, 0, -1), (-1, 0, 1),
    (0, 1, 1), (0, -1, -1), (0, 1, -1), (0, -1, 1),
]
OPP = [DIRS.index((-a, -b, -c)) for a, b, c in DIRS]
MIRROR_Y = [DIRS.index((a, -b, c)) for a, b, c in DIRS]
MIRROR_Z = [DIRS.index((a, b, -c)) for a, b, c in DIRS]
INLET = 0.05

Z_EDGE = [i for i in range(19) if DIRS[i][2] == 0] + [i for i in range(19) if DIRS[i][2] == 1]
Z_SECOND = [i for i in range(19) if DIRS[i][2] == 1]
Y_FLAT = [i for i in range(19) if DIRS[i][1] == 0]
Y_PLUS = [i for i in range(19) if DIRS[i][1] == 1]
FLAG_PLANE = 4 * len(Y_FLAT)
LANE_PLUS = 2 * FLAG_PLANE + 8

ROW_SOLID = 76
ROW_PARAM = 80
ROW_NOISE = 88
PAD = 8
FIRST = PAD - 2
Y_HALF = 34
Y_FAR = 2
Y_FILTER = 8
Y_MESSAGE = 112


def taps():
    k = np.arange(-HW, HW + 1).astype(np.float64)
    raw = np.exp(-math.pi * k * k / (2.0 * (HW // 2) ** 2))
    return raw / np.sqrt(np.sum(raw * raw))


def band(source, target):
    values = taps()
    offset = np.asarray(source)[:, None] - np.asarray(target)[None, :]
    inside = np.abs(offset) <= HW
    return np.where(inside, values[np.clip(offset + HW, 0, 2 * HW)], 0.0).astype(np.float32)


def moments(g):
    s = {a: g[a] + g[a + 1] for a in range(1, 19, 2)}
    d = {a: g[a] - g[a + 1] for a in range(1, 19, 2)}
    w1, w2 = 1.0 / 18.0, 1.0 / 36.0
    rho = (
        g[0] * (1.0 / 3.0)
        + (s[1] + s[3] + s[5]) * w1
        + ((s[7] + s[9]) + (s[11] + s[13]) + (s[15] + s[17])) * w2
    )
    mx = d[1] * w1 + ((d[7] + d[9]) + (d[11] + d[13])) * w2
    my = d[3] * w1 + ((d[7] - d[9]) + (d[15] + d[17])) * w2
    mz = d[5] * w1 + ((d[11] - d[13]) + (d[15] - d[17])) * w2
    return rho, mx, my, mz


def pair_vector(a, vx, vy, vz):
    total = None
    for c, v in zip(DIRS[a], (vx, vy, vz)):
        if c:
            term = v if c > 0 else -v
            total = term if total is None else (total + v if c > 0 else total - v)
    return total


def collide(g, solid, keep=range(19)):
    rho, mx, my, mz = moments(g)
    inv = 1.0 / rho
    ux, uy, uz = mx * inv, my * inv, mz * inv
    square = mx * ux + my * uy + mz * uz
    base = 1.25 * rho - 1.875 * square
    post = [None] * 19
    if 0 in keep:
        post[0] = jnp.where(solid, g[0], base - 0.25 * g[0])
    for a in range(1, 19, 2):
        if a not in keep and a + 1 not in keep:
            continue
        m = pair_vector(a, mx, my, mz)
        p = pair_vector(a, ux, uy, uz)
        even = base + 5.625 * (m * p)
        odd = 3.75 * m
        if a in keep:
            post[a] = jnp.where(solid, g[a + 1], (even + odd) - 0.25 * g[a])
        if a + 1 in keep:
            post[a + 1] = jnp.where(solid, g[a], (even - odd) - 0.25 * g[a + 1])
    return post


def inlet_state(ux, uy, uz):
    base = 1.0 - 1.5 * (ux * ux + uy * uy + uz * uz)
    out = [base] * 19
    for a in range(1, 19, 2):
        p = pair_vector(a, ux, uy, uz)
        even = base + 4.5 * (p * p)
        odd = 3.0 * p
        out[a] = even + odd
        out[a + 1] = even - odd
    return out


def wall_rows(first_row, height, kz, nz):
    rows = lax.broadcasted_iota(jnp.int32, (8, 128), 0) + first_row
    return ((rows == 0) & (kz == 0)) | ((rows == height - 1) & (kz == nz - 1))


def edge_kernel(
    nz, pops, mask, noise, mean, diag, off, za, zb, raw, flags, mean_v, diag_v, off_v, edge, sems
):
    height = pops.shape[2]
    kz = lax.axis_index("gz")
    upward = lax.rem(kz, 2) == 0
    upper = pl.ds(height - 8, 8)
    copies = [
        (pops.at[:, :, 0:8, :], raw.at[:, :, 0:8, :]),
        (pops.at[:, :, upper, :], raw.at[:, :, 8:16, :]),
        (mask.at[:, 0:8, :], flags.at[:, 0:8, :]),
        (mask.at[:, upper, :], flags.at[:, 8:16, :]),
        (mean, mean_v),
        (diag, diag_v),
        (off, off_v),
    ]
    for c in range(3):
        at = slice(ROW_NOISE + height * c, ROW_NOISE + height * (c + 1))
        copies.append((noise.at[c], za.at[at, :]))
        copies.append((noise.at[c], zb.at[at, :]))
    copies = [pltpu.make_async_copy(src, dst, sems.at[n]) for n, (src, dst) in enumerate(copies)]
    for copy in copies:
        copy.start()
    for part, row in ((0, 0), (1, height - 8)):
        copies[part].wait()
        copies[2 + part].wait()
        wall = wall_rows(row, height, kz, nz)
        at = slice(8 * part, 8 * part + 8)
        for x in range(4):
            solid = (flags[x, at, :] == 1) | wall
            post = collide([raw[i, x, at, :] for i in range(19)], solid)
            post.append(solid.astype(jnp.float32))
            for i in range(20):
                edge[64 * i + 16 * x + 8 * part : 64 * i + 16 * x + 8 * part + 8, :] = post[i]

    def put(q, i, depth):
        up = edge[pl.ds(64 * i + 15 - depth, 4, stride=16), :]
        down = edge[pl.ds(64 * (i if i == 19 else MIRROR_Z[i]) + depth, 4, stride=16), :]
        za[4 * q : 4 * q + 4, :] = jnp.where(upward, up, down)
        zb[4 * q : 4 * q + 4, :] = jnp.where(upward, down, up)

    for q, i in enumerate(Z_EDGE + Z_SECOND + [19]):
        put(q, i, 1 if len(Z_EDGE) <= q < 19 else 0)
    for copy in copies[4:]:
        copy.wait()
    for ref in (za, zb):
        ref[ROW_PARAM : ROW_PARAM + 8, :] = jnp.zeros((8, 128), jnp.float32)
        ref[ROW_PARAM : ROW_PARAM + 1, 0:height] = mean_v[...]
        ref[ROW_PARAM + 1 : ROW_PARAM + 4, 0:height] = diag_v[...]
        ref[ROW_PARAM + 4 : ROW_PARAM + 7, 0:height] = off_v[...]


def far_kernel(height, za, z2):
    kz = lax.axis_index("gz")
    low_half = lax.rem(kz, 4) < 2
    z2[...] = jnp.zeros((16, 128), jnp.float32)
    for c in range(3):
        base = ROW_NOISE + height * c
        last = za[base + height - 1 : base + height, :]
        first = za[base : base + 1, :]
        z2[c : c + 1, :] = jnp.where(low_half, last, first)
        z2[8 + c : 9 + c, :] = jnp.where(low_half, first, last)


def dot3(a, b, dims=(((1,), (0,)), ((), ()))):
    a_hi, b_hi = a.astype(jnp.bfloat16), b.astype(jnp.bfloat16)
    a_lo = (a - a_hi.astype(jnp.float32)).astype(jnp.bfloat16)
    b_lo = (b - b_hi.astype(jnp.float32)).astype(jnp.bfloat16)

    def dot(u, v):
        return lax.dot_general(u, v, dims, preferred_element_type=jnp.float32)

    return dot(a_hi, b_hi) + (dot(a_lo, b_hi) + dot(a_hi, b_lo))


NT = (((1,), (1,)), ((), ()))


def put_pair(pair, slot, value, first_column, into):
    return jnp.where(pair == slot, pltpu.roll(value, (2 * slot - first_column) % 128, 1), into)


def bulk_kernel(nz, pops, mask, post, solidp, ya, yb):
    height = pops.shape[2]
    kz = lax.axis_index("gz")
    ky = lax.axis_index("gy") * lax.axis_size("col") + lax.axis_index("col")
    y_even = lax.rem(ky, 2) == 0
    pair = lax.broadcasted_iota(jnp.int32, (8, 128), 1) // 2

    def body(t, carry):
        row = pl.multiple_of(t * 8, 8)
        out = pl.ds(row + PAD, 8)
        wall = wall_rows(row, height, kz, nz)
        flat = right = left = jnp.zeros((8, 128), jnp.float32)
        for x in range(4):
            solid = (mask[x, pl.ds(row, 8), :] == 1) | wall
            p = collide([pops[i, x, pl.ds(row, 8), :] for i in range(19)], solid)
            flag = solid.astype(jnp.float32)
            solidp[x, out, :] = flag
            flat = put_pair(pair, FLAG_PLANE + x, flag, 127, flat)
            for q, i in enumerate(Y_FLAT):
                post[i, x, out, :] = p[i]
                flat = put_pair(pair, 4 * q + x, p[i], 127, flat)
            for n, i in enumerate(Y_PLUS):
                j = MIRROR_Y[i]
                slot = LANE_PLUS // 2 + 4 * n + x
                post[i, x, out, :] = pltpu.roll(p[i], 1, 1)
                post[j, x, out, :] = pltpu.roll(p[j], 127, 1)
                right = put_pair(pair, slot, p[i], 126, right)
                left = put_pair(pair, slot, p[j], 0, left)
        right = jnp.where(pair < LANE_PLUS // 2, flat, right)
        left = jnp.where(pair < LANE_PLUS // 2, flat, left)
        ya[pl.ds(row, 8), :] = jnp.where(y_even, right, left)
        yb[pl.ds(row, 8), :] = jnp.where(y_even, left, right)
        return carry

    lax.fori_loop(0, height // 8, body, 0)


def column_kernel(
    nz, post_in, solid_in, sent, za, zb, z2c, z2d, bandz, pick,
    post, solidp, ya, yb, linear, meanrow,
    wide, filt, moved,
):
    height = post.shape[2] - 2 * PAD
    rows = height + 2 * PAD
    kz = lax.axis_index("gz")
    ky = lax.axis_index("gy") * lax.axis_size("col") + lax.axis_index("col")
    z_even = lax.rem(kz, 2) == 0
    y_even = lax.rem(ky, 2) == 0
    low_half = lax.rem(kz, 4) < 2

    def below(row, n=1):
        return jnp.where(z_even, zb[row : row + n, :], za[row : row + n, :])

    def above(row, n=1):
        return jnp.where(z_even, za[row : row + n, :], zb[row : row + n, :])

    top = PAD + height
    low, high = below(0, ROW_PARAM), above(0, ROW_PARAM)
    for n, shift in enumerate((0, 1, 127)):
        moved[n, 0] = low if shift == 0 else pltpu.roll(low, shift, 1)
        moved[n, 1] = high if shift == 0 else pltpu.roll(high, shift, 1)
    for items, first, depth in ((Z_EDGE, 0, 0), (Z_SECOND, len(Z_EDGE), 1)):
        for q, i in enumerate(items):
            n = DIRS[i][1] % 3
            for x in range(4):
                at = slice(4 * (first + q) + x, 4 * (first + q) + x + 1)
                post[i, x, PAD - 1 - depth : PAD - depth, :] = moved[n, 0, at, :]
                post[MIRROR_Z[i], x, top + depth : top + depth + 1, :] = moved[n, 1, at, :]
    for x in range(4):
        solidp[x, PAD - 1 : PAD, :] = moved[0, 0, ROW_SOLID + x : ROW_SOLID + x + 1, :]
        solidp[x, top : top + 1, :] = moved[0, 1, ROW_SOLID + x : ROW_SOLID + x + 1, :]

    lane = lax.broadcasted_iota(jnp.int32, (8, 128), 1)
    own_par = pltpu.roll(sent[ROW_PARAM : ROW_PARAM + 8, :], PAD, 1)
    low_par = pltpu.roll(below(ROW_PARAM, 8), 128 - height + PAD, 1)
    high_par = pltpu.roll(above(ROW_PARAM, 8), height + PAD, 1)
    par = jnp.where(lane < PAD, low_par, jnp.where(lane < top, own_par, high_par))
    par = jnp.where(lane < rows, par, 0.0)
    meanrow[...] = par
    cols = jnp.transpose(jnp.concatenate([par] * 16, axis=0))[0:rows]

    for c in range(3):
        lanes = slice(128 * c, 128 * c + 128)
        at = slice(ROW_NOISE + height * c, ROW_NOISE + height * (c + 1))
        wide[0:height, lanes] = below(ROW_NOISE + height * c, height)
        wide[height : 2 * height, lanes] = sent[at, :]
        wide[2 * height : 3 * height, lanes] = above(ROW_NOISE + height * c, height)
    filt[...] = dot3(bandz[...], wide[...])
    b_end = float(taps()[0])
    far_low = jnp.where(low_half, z2d[8:16, :], z2c[0:8, :])
    far_high = jnp.where(low_half, z2c[0:8, :], z2d[8:16, :])
    for c in range(3):
        lanes = slice(128 * c, 128 * c + 128)
        filt[PAD - 1 : PAD, lanes] += b_end * far_low[c : c + 1, :]
        filt[top : top + 1, lanes] += b_end * far_high[c : c + 1, :]
    f0, f1, f2 = (filt[:, 128 * c : 128 * c + 128] for c in range(3))
    linear[0] = cols[:, 1:2] * f0
    linear[1] = cols[:, 4:5] * f0 + cols[:, 2:3] * f1
    linear[2] = cols[:, 5:6] * f0 + cols[:, 6:7] * f1 + cols[:, 3:4] * f2
    linear[3] = jnp.broadcast_to(cols[:, 0:1], (rows, 128))

    pair = lane // 2
    for row in (0, rows - 8):
        out = slice(row, row + 8)
        flat = right = left = jnp.zeros((8, 128), jnp.float32)
        for x in range(4):
            flat = put_pair(pair, FLAG_PLANE + x, solidp[x, out, :], 127, flat)
            for q, i in enumerate(Y_FLAT):
                flat = put_pair(pair, 4 * q + x, post[i, x, out, :], 127, flat)
            for n, i in enumerate(Y_PLUS):
                slot = LANE_PLUS // 2 + 4 * n + x
                right = put_pair(pair, slot, post[i, x, out, :], 127, right)
                left = put_pair(pair, slot, post[MIRROR_Y[i], x, out, :], 127, left)
        right = jnp.where(pair < LANE_PLUS // 2, flat, right)
        left = jnp.where(pair < LANE_PLUS // 2, flat, left)
        at = slice(0, 2) if row else slice(6, 8)
        ya[at, :] = jnp.where(y_even, right, left)[at, :]
        yb[at, :] = jnp.where(y_even, left, right)[at, :]
    spare = jnp.zeros((1, 128), jnp.float32)
    for c in range(3):
        far = dot3(pick[...], linear[c], NT)
        far = jnp.concatenate([far, jnp.zeros((8, 128 - rows), jnp.float32)], axis=1)
        ya[Y_FAR + c : Y_FAR + c + 1, :] = jnp.where(y_even, far[0:1, :], far[1:2, :])
        yb[Y_FAR + c : Y_FAR + c + 1, :] = jnp.where(y_even, far[1:2, :], far[0:1, :])
    for ref in (ya, yb):
        ref[5:6, :] = spare
        ref[Y_FILTER + 3 * Y_HALF : Y_MESSAGE, :] = jnp.zeros((2, 128), jnp.float32)
    middle = FIRST + Y_HALF
    lane_h = lax.broadcasted_iota(jnp.int32, (Y_HALF, 128), 1)
    for c in range(3):
        first, second = linear[c, FIRST:middle, :], linear[c, middle : middle + Y_HALF, :]
        left = jnp.where(lane_h < 64, first, pltpu.roll(second, 64, 1))
        right = jnp.where(lane_h < 64, pltpu.roll(first, 64, 1), second)
        at = slice(Y_FILTER + Y_HALF * c, Y_FILTER + Y_HALF * (c + 1))
        ya[at, :] = jnp.where(y_even, right, left)
        yb[at, :] = jnp.where(y_even, left, right)


def streamed(i, x):
    source = x - DIRS[i][0]
    return None if source < 0 else min(source, 3)


INWARD = [i for i in range(19) if DIRS[i][2]]


def both_ghosts(sub, low, high):
    return jnp.where(sub < 4, low, high)


def assemble(tall, sa, sb, ya, yb, a_first):
    end = PAD + sa.shape[0]
    for out, source, a, b in (
        (slice(PAD, end), slice(0, sa.shape[0]), sa, sb),
        (slice(PAD - 2, PAD), slice(6, 8), ya, yb),
        (slice(end, end + 2), slice(0, 2), ya, yb),
    ):
        tall[0, out, :] = jnp.where(a_first, a[source, :], b[source, :])
        tall[1, out, :] = jnp.where(a_first, b[source, :], a[source, :])


def interior_kernel(
    nz, post, solidp, linear, sa, sb, ya, yb, wy, wg, post2, flow_own, ghost_own, own_right, own_left, tall
):
    rows = post.shape[2]
    top = rows - PAD
    kz = lax.axis_index("gz")
    ky = lax.axis_index("gy") * lax.axis_size("col") + lax.axis_index("col")
    y_even = lax.rem(ky, 2) == 0
    sub = lax.broadcasted_iota(jnp.int32, (8, 128), 0)

    def moved(i, value):
        return pltpu.roll(value, DIRS[i][1] % 128, 1) if DIRS[i][1] else value

    outside = ((sub < 4) & (kz == 0)) | ((sub >= 4) & (kz == nz - 1))
    for x in range(1, 4):
        solid = both_ghosts(sub, solidp[x, PAD - 1 : PAD + 7, :], solidp[x, top - 7 : top + 1, :]) > 0.5
        g = []
        for i in range(19):
            low, high, source = PAD - 1 - DIRS[i][2], top - 7 - DIRS[i][2], streamed(i, x)
            g.append(both_ghosts(sub, post[i, source, low : low + 8, :], post[i, source, high : high + 8, :]))
        p = collide(g, solid, INWARD)
        for i in INWARD:
            row, at = (PAD - 1, 0) if DIRS[i][2] == 1 else (top, 7)
            value = moved(i, jnp.where(outside, 0.0, p[i]))
            post2[i, x - 1, row : row + 1, :] = value[at : at + 1, :]

    def body(t, carry):
        row = pl.multiple_of(t * 8 + PAD, 8)
        for x in range(1, 4):
            solid = solidp[x, pl.ds(row, 8), :] > 0.5
            g = [post[i, streamed(i, x), pl.ds(row - DIRS[i][2], 8), :] for i in range(19)]
            p = collide(g, solid)
            for i in range(19):
                post2[i, x - 1, pl.ds(row, 8), :] = moved(i, p[i])
        return carry

    lax.fori_loop(0, rows // 8 - 2, body, 0)

    flow_own[...] = dot3(linear[0:3].reshape(3 * rows, 128), wy[0:128, :])
    flow_own[0:rows, :] += linear[3]
    for c in range(3):
        ghost_own[8 * c : 8 * c + 8, 0:rows] = dot3(wg[:, 0:128], linear[c], NT)
        ghost_own[8 * c : 8 * c + 8, rows:128] = jnp.zeros((8, 128 - rows), jnp.float32)
    assemble(tall, sa, sb, ya, yb, y_even)
    own_right[0:128, :] = jnp.transpose(tall[0])
    own_left[0:128, :] = jnp.transpose(tall[1])


def final_kernel(
    nz, post, solidp, post2, flow_own, ghost_own, own_right, own_left, meanrow, sa, sb, ya, yb, wy, wg,
    inflow, state_out,
    lhs, flow, inlet2, strip_left, strip_right, moving, still, ghost_moving, ghost_still,
    state, flow_out, tall, sems,
):
    height = state.shape[2]
    rows = height + 2 * PAD
    top = PAD + height
    kz = lax.axis_index("gz")
    ky = lax.axis_index("gy") * lax.axis_size("col") + lax.axis_index("col")
    y_even = lax.rem(ky, 2) == 0
    lane = lax.broadcasted_iota(jnp.int32, (8, 128), 1)
    sub = lax.broadcasted_iota(jnp.int32, (8, 128), 0)

    assemble(tall, sa, sb, ya, yb, jnp.logical_not(y_even))
    strip_left[0:128, 0:rows] = jnp.transpose(tall[0, 0:rows, :])
    strip_right[0:128, 0:rows] = jnp.transpose(tall[1, 0:rows, :])

    lane_h = lax.broadcasted_iota(jnp.int32, (Y_HALF, 128), 1)
    for c in range(3):
        at = slice(Y_FILTER + Y_HALF * c, Y_FILTER + Y_HALF * (c + 1))
        a, b = ya[at, :], yb[at, :]
        left, right = jnp.where(y_even, b, a), jnp.where(y_even, a, b)
        middle = rows * c + FIRST + Y_HALF
        lo, hi = slice(middle - Y_HALF, middle), slice(middle, middle + Y_HALF)
        lhs[lo, 0:128] = jnp.where(lane_h < 64, left, 0.0)
        lhs[hi, 0:128] = jnp.where(lane_h < 64, 0.0, left)
        lhs[lo, 128:256] = jnp.where(lane_h < 64, right, 0.0)
        lhs[hi, 128:256] = jnp.where(lane_h < 64, 0.0, right)
    flow[...] = flow_own[...] + dot3(lhs[...], wy[128:384, :])
    for c in range(3):
        flow_out[c] = flow[rows * c + PAD : rows * c + top, :]
    flow_copy = pltpu.make_async_copy(flow_out, inflow, sems.at[height // 8])
    flow_copy.start()
    b_end = float(taps()[0])
    column_flow = []
    for c in range(3):
        g = dot3(wg[:, 128:384], lhs[rows * c : rows * (c + 1), :], NT)
        g = jnp.concatenate([g, jnp.zeros((8, 128 - rows), jnp.float32)], axis=1)
        g = g + ghost_own[8 * c : 8 * c + 8, :]
        far = slice(Y_FAR + c, Y_FAR + c + 1)
        at = [g[n : n + 1, :] for n in range(4)]
        at[0] = at[0] + b_end * jnp.where(y_even, yb[far, :], ya[far, :])
        at[3] = at[3] + b_end * jnp.where(y_even, ya[far, :], yb[far, :])
        if c == 0:
            at = [v + meanrow[0:1, :] for v in at]
        column_flow.append(at)

    outside = ((lane < PAD) & (kz == 0)) | ((lane >= top) & (kz == nz - 1))
    sources = (
        ((strip_left, 0), (strip_left, 0), (own_left, 0)),
        ((own_left, 1), (strip_left, 1), (own_left, 1)),
        ((own_right, 0), (own_right, 0), (strip_right, 0)),
        ((strip_right, 1), (own_right, 1), (strip_right, 1)),
    )
    for column in range(4):
        def rows_of(start):
            return pl.ds(start, 8, stride=2)

        src, odd = sources[column][0]
        solid = src[rows_of(2 * FLAG_PLANE + odd), :] > 0.5
        g = [None] * 19
        for i in range(19):
            cx, cy, cz = DIRS[i]
            src, odd = sources[column][cy % 3]
            if cy == 0:
                start = 8 * Y_FLAT.index(i) + odd
            else:
                start = LANE_PLUS + 8 * Y_PLUS.index(i if cy == 1 else MIRROR_Y[i]) + odd
            v = src[rows_of(start - 2 * cx), :]
            if cx == 1:
                v = jnp.where(sub == 0, 0.0, v)
            elif cx == -1:
                v = jnp.where(sub == 3, src[rows_of(start), :], v)
            g[i] = v if cz == 0 else pltpu.roll(v, cz % 128, 1)
        us = [INLET * jnp.broadcast_to(column_flow[c][column], (8, 128)) for c in range(3)]
        eq = inlet_state(*us)
        put = (sub == 0) & jnp.logical_not(solid)
        moves = 1 if column < 2 else -1
        keep = [i for i in range(19) if DIRS[i][1] == moves or (DIRS[i][1] == 0 and column in (1, 2))]
        p = collide(g, solid, keep)
        for i in keep:
            value = jnp.where(outside, 0.0, jnp.where(put, eq[i], p[i]))[0:4, :]
            if DIRS[i][1]:
                n = Y_PLUS.index(i if moves == 1 else MIRROR_Y[i])
                moving[pl.ds(16 * n + (column + 2) % 4, 4, stride=4), :] = value
            else:
                still[pl.ds(8 * Y_FLAT.index(i) + 2 - column, 4, stride=2), :] = value
    ghost_moving[:, 0:80] = jnp.transpose(moving[0:80, :])
    ghost_still[:, 0:72] = jnp.transpose(still[0:72, :])

    def inlet_values(us, solid, planes, load):
        eq = inlet_state(*[INLET * u for u in us])
        for i in planes:
            j = OPP[i]
            source = streamed(j, 0)
            bounced = 0.0 if source is None else load(j, source)
            yield i, jnp.where(solid, bounced, eq[i])

    def moved(i, value):
        return pltpu.roll(value, DIRS[i][1] % 128, 1) if DIRS[i][1] else value

    def inlet(row):
        us = [flow[pl.ds(rows * c + row, 8), :] for c in range(3)]
        solid = solidp[0, pl.ds(row, 8), :] > 0.5
        load = lambda j, source: post[j, source, pl.ds(row - DIRS[j][2], 8), :]
        for i, value in inlet_values(us, solid, range(19), load):
            inlet2[i, pl.ds(row, 8), :] = moved(i, value)

    def inlet_ghosts():
        low, high = PAD - 1, top - 7

        def both(ref, shift, *lead):
            low_at, high_at = slice(low + shift, low + shift + 8), slice(high + shift, high + shift + 8)
            return both_ghosts(sub, ref[(*lead, low_at)], ref[(*lead, high_at)])

        us = [both(flow, rows * c) for c in range(3)]
        solid = both(solidp, 0, 0) > 0.5
        load = lambda j, source: both(post, -DIRS[j][2], j, source)
        beyond = ((sub < 4) & (kz == 0)) | ((sub >= 4) & (kz == nz - 1))
        for i, value in inlet_values(us, solid, INWARD, load):
            row, at = (PAD - 1, 0) if DIRS[i][2] == 1 else (top, 7)
            value = moved(i, jnp.where(beyond, 0.0, value))
            inlet2[i, row : row + 1, :] = value[at : at + 1, :]

    def out_copy(t):
        at = pl.ds(pl.multiple_of(t * 8, 8), 8)
        return pltpu.make_async_copy(state.at[:, :, at, :], state_out.at[:, :, at, :], sems.at[t])

    def last(t):
        row = pl.multiple_of(t * 8 + PAD, 8)
        us = [INLET * flow[pl.ds(rows * c + row, 8), :] for c in range(3)]
        eq = inlet_state(*us)
        solid = solidp[0, pl.ds(row, 8), :] > 0.5
        ends = (lane == 0) | (lane == 127)

        def read(i, source, ghost):
            at = pl.ds(row - DIRS[i][2], 8)
            v = inlet2[i, at, :] if source == 0 else post2[i, source - 1, at, :]
            where = ends if DIRS[i][1] == 0 else (lane < 2 if DIRS[i][1] == 1 else lane >= 126)
            return jnp.where(where, ghost, v)

        def write(i, x, value):
            if x == 0:
                value = jnp.where(solid, value, eq[i])
            state[i, x, pl.ds(row - PAD, 8), :] = value

        for i in Y_FLAT + Y_PLUS:
            both = [i] if DIRS[i][1] == 0 else [i, MIRROR_Y[i]]
            at = pl.ds(row - DIRS[i][2], 8)
            for source in range(4):
                targets = [x for x in range(4) if streamed(i, x) == source]
                if not targets:
                    continue
                if DIRS[i][1] == 0:
                    slot = 2 * (4 * Y_FLAT.index(i) + source)
                    ghost = pltpu.roll(ghost_still[at, :], (127 - slot) % 128, 1)
                else:
                    slot = 4 * (4 * Y_PLUS.index(i) + source)
                    ghost = pltpu.roll(ghost_moving[at, :], (126 - slot) % 128, 1)
                for j in both:
                    value = read(j, source, ghost)
                    for x in targets:
                        write(j, x, value)
            for j in both:
                if streamed(j, 0) is None:
                    write(j, 0, jnp.zeros((8, 128), jnp.float32))
        out_copy(t).start()

    inlet_ghosts()
    inlet(PAD)

    def main(t, carry):
        inlet(pl.multiple_of(t * 8 + PAD, 8))
        last(t - 1)
        return carry

    tiles = height // 8
    lax.fori_loop(1, tiles, main, 0)
    last(tiles - 1)
    for t in range(tiles):
        out_copy(t).wait()
    flow_copy.wait()


def swap_pairs(count, phase, distance=1):
    pairs = []
    for i in range(count):
        block = (i + phase * distance) // distance
        j = i + distance if block % 2 == 0 else i - distance
        if 0 <= j < count:
            pairs.append((i, j))
    return pairs


def ring_pairs(count, phase):
    if phase == 0:
        return [(i, i ^ 1) for i in range(count)]
    return [(i, (((i + 1) % count ^ 1) - 1) % count) for i in range(count)]


def vm(n):
    return [pl.BlockSpec(memory_space=pltpu.VMEM)] * n


def hbm(n):
    return [pl.BlockSpec(memory_space=pltpu.HBM)] * n


def f32(*shape):
    return jax.ShapeDtypeStruct(shape, jnp.float32)


def scratch(*shape):
    return pltpu.VMEM(shape, jnp.float32)


def flags(*shape):
    return pltpu.VMEM(shape, jnp.int32)


def params(mib):
    return pltpu.CompilerParams(vmem_limit_bytes=mib * 1024 * 1024)


def cost(flops, size):
    return pl.CostEstimate(flops=flops, bytes_accessed=size, transcendentals=0)


def shards(nz, ny, noise, mean_profile, lund_diag, lund_off, populations, mask):
    height, span = noise.shape[1], noise.shape[2]
    rows = height + 2 * PAD
    message = ROW_NOISE + 3 * height
    dma = pltpu.SemaphoreType.DMA
    here = lambda value: pltpu.with_memory_space_constraint(value, pltpu.HBM)
    mean_profile = mean_profile.reshape(1, height)
    operands = populations, mask, noise, mean_profile, lund_diag, lund_off

    za, zb = pl.pallas_call(
        lambda *refs: edge_kernel(nz, *refs),
        out_shape=(f32(message, 128), f32(message, 128)),
        in_specs=hbm(6),
        out_specs=vm(2),
        scratch_shapes=[
            scratch(19, 4, 16, 128), flags(4, 16, 128), scratch(1, height), scratch(3, height),
            scratch(3, height), scratch(20 * 4 * 16, 128), dma((13,)),
        ],
        compiler_params=params(8),
        name="edge_rows",
    )(*map(here, operands))

    z2 = pl.pallas_call(
        lambda *refs: far_kernel(height, *refs),
        out_shape=f32(16, 128),
        in_specs=vm(1),
        out_specs=pl.BlockSpec(memory_space=pltpu.VMEM),
        compiler_params=params(1),
        name="far_rows",
    )(za)

    ra = lax.ppermute(za, "gz", swap_pairs(nz, 0))
    rb = lax.ppermute(zb, "gz", swap_pairs(nz, 1))
    rc = lax.ppermute(z2, "gz", swap_pairs(nz, 0, 2))
    far = swap_pairs(nz, 1, 2)
    rd = lax.ppermute(z2, "gz", far) if far else jnp.zeros_like(z2)

    post, solidp, sa, sb = pl.pallas_call(
        lambda *refs: bulk_kernel(nz, *refs),
        out_shape=(f32(19, 4, rows, 128), f32(4, rows, 128), f32(height, 128), f32(height, 128)),
        in_specs=vm(2),
        out_specs=vm(4),
        compiler_params=params(4),
        cost_estimate=cost(4_000_000_000, 8_000_000),
        name="bulk",
    )(populations, mask)

    pa = lax.ppermute(sa, ("gy", "col"), ring_pairs(ny, 0))
    pb = lax.ppermute(sb, ("gy", "col"), ring_pairs(ny, 1))
    pick = np.zeros((8, 128), np.float32)
    pick[0, span - HW - 1] = pick[1, HW] = 1.0

    line = np.arange(rows) - PAD
    used = (line >= -1) & (line <= height)
    bandz = np.where(used[:, None], band(np.arange(-height, 2 * height), line).T, 0.0)
    post, solidp, ya, yb, linear, meanrow = pl.pallas_call(
        lambda *refs: column_kernel(nz, *refs),
        out_shape=(
            f32(19, 4, rows, 128), f32(4, rows, 128), f32(Y_MESSAGE, 128), f32(Y_MESSAGE, 128),
            f32(4, rows, 128), f32(8, 128),
        ),
        in_specs=vm(9),
        out_specs=vm(6),
        scratch_shapes=[
            scratch(3 * height, 384), scratch(rows, 384), scratch(3, 2, ROW_PARAM, 128),
        ],
        input_output_aliases={0: 0, 1: 1},
        compiler_params=params(4),
        name="columns",
    )(post, solidp, za, ra, rb, rc, rd, jnp.asarray(bandz, jnp.float32), jnp.asarray(pick))

    qa = lax.ppermute(ya, ("gy", "col"), ring_pairs(ny, 0))
    qb = lax.ppermute(yb, ("gy", "col"), ring_pairs(ny, 1))

    own = np.arange(span)
    left = np.arange(128) % 64 - 64
    right = np.arange(128) % 64 + span
    source = np.concatenate([own, left, right])
    wy = jnp.asarray(band(source, own))
    wg = np.zeros((8, 384), np.float32)
    wg[0:4] = band(source, np.array([-1, 0, span - 1, span])).T
    wg = jnp.asarray(wg)
    post2, flow_own, ghost_own, own_right, own_left = pl.pallas_call(
        lambda *refs: interior_kernel(nz, *refs),
        out_shape=(
            f32(19, 3, rows, 128), f32(3 * rows, 128), f32(24, 128), f32(144, 128), f32(144, 128),
        ),
        in_specs=vm(9),
        out_specs=vm(5),
        scratch_shapes=[scratch(2, 128, 128)],
        compiler_params=params(4),
        cost_estimate=cost(4_000_000_000, 8_000_000),
        name="interior",
    )(post, solidp, linear, sa, sb, ya, yb, wy, wg)
    inflow, state = pl.pallas_call(
        lambda *refs: final_kernel(nz, *refs),
        out_shape=(f32(3, height, span), f32(19, 4, height, span)),
        in_specs=vm(14),
        out_specs=hbm(2),
        scratch_shapes=[
            scratch(3 * rows, 256), scratch(3 * rows, 128), scratch(19, rows, 128),
            scratch(144, 128), scratch(144, 128), scratch(128, 128), scratch(128, 128),
            scratch(128, 128), scratch(128, 128), scratch(19, 4, height, span),
            scratch(3, height, span), scratch(2, 128, 128), dma((height // 8 + 1,)),
        ],
        compiler_params=params(8),
        name="stream",
    )(post, solidp, post2, flow_own, ghost_own, own_right, own_left, meanrow, pa, pb, qa, qb, wy, wg)
    return inflow, state


def solution(mesh):
    nz = mesh.shape["gz"]
    ny = mesh.shape["gy"] * mesh.shape["col"]
    in_specs = (
        P(None, "gz", ("gy", "col")),
        P("gz"),
        P(None, "gz"),
        P(None, "gz"),
        P(None, None, "gz", ("gy", "col")),
        P(None, "gz", ("gy", "col")),
    )
    out_specs = (P(None, "gz", ("gy", "col")), P(None, None, "gz", ("gy", "col")))

    def body(*args):
        return shards(nz, ny, *args)

    return jax.shard_map(body, mesh=mesh, in_specs=in_specs, out_specs=out_specs, check_vma=False)
```

```python
import math

import jax
import jax.numpy as jnp
import numpy as np
from jax import lax
from jax.experimental import pallas as pl
from jax.experimental.pallas import tpu as pltpu
from jax.sharding import PartitionSpec as P

HW = 64
DIRS = [
    (0, 0, 0),
    (1, 0, 0), (-1, 0, 0), (0, 1, 0), (0, -1, 0), (0, 0, 1), (0, 0, -1),
    (1, 1, 0), (-1, -1, 0), (1, -1, 0), (-1, 1, 0),
    (1, 0, 1), (-1, 0, -1), (1, 0, -1), (-1, 0, 1),
    (0, 1, 1), (0, -1, -1), (0, 1, -1), (0, -1, 1),
]
OPP = [DIRS.index((-a, -b, -c)) for a, b, c in DIRS]
MIRROR_Y = [DIRS.index((a, -b, c)) for a, b, c in DIRS]
MIRROR_Z = [DIRS.index((a, b, -c)) for a, b, c in DIRS]
INLET = 0.05

Z_EDGE = [i for i in range(19) if DIRS[i][2] == 0] + [i for i in range(19) if DIRS[i][2] == 1]
Z_SECOND = [i for i in range(19) if DIRS[i][2] == 1]
Y_FLAT = [i for i in range(19) if DIRS[i][1] == 0]
Y_PLUS = [i for i in range(19) if DIRS[i][1] == 1]
FLAG_PLANE = 4 * len(Y_FLAT)
LANE_PLUS = 2 * FLAG_PLANE + 8

ROW_SOLID = 76
ROW_PARAM = 80
ROW_NOISE = 88
PAD = 8
FIRST = PAD - 2
Y_HALF = 34
Y_FAR = 2
Y_FILTER = 8
Y_MESSAGE = 112


def taps():
    k = np.arange(-HW, HW + 1).astype(np.float64)
    raw = np.exp(-math.pi * k * k / (2.0 * (HW // 2) ** 2))
    return raw / np.sqrt(np.sum(raw * raw))


def band(source, target):
    values = taps()
    offset = np.asarray(source)[:, None] - np.asarray(target)[None, :]
    inside = np.abs(offset) <= HW
    return np.where(inside, values[np.clip(offset + HW, 0, 2 * HW)], 0.0).astype(np.float32)


def moments(g):
    s = {a: g[a] + g[a + 1] for a in range(1, 19, 2)}
    d = {a: g[a] - g[a + 1] for a in range(1, 19, 2)}
    w1, w2 = 1.0 / 18.0, 1.0 / 36.0
    rho = (
        g[0] * (1.0 / 3.0)
        + (s[1] + s[3] + s[5]) * w1
        + ((s[7] + s[9]) + (s[11] + s[13]) + (s[15] + s[17])) * w2
    )
    mx = d[1] * w1 + ((d[7] + d[9]) + (d[11] + d[13])) * w2
    my = d[3] * w1 + ((d[7] - d[9]) + (d[15] + d[17])) * w2
    mz = d[5] * w1 + ((d[11] - d[13]) + (d[15] - d[17])) * w2
    return rho, mx, my, mz


def pair_vector(a, vx, vy, vz):
    total = None
    for c, v in zip(DIRS[a], (vx, vy, vz)):
        if c:
            term = v if c > 0 else -v
            total = term if total is None else (total + v if c > 0 else total - v)
    return total


def collide(g, solid, keep=range(19)):
    rho, mx, my, mz = moments(g)
    inv = 1.0 / rho
    ux, uy, uz = mx * inv, my * inv, mz * inv
    square = mx * ux + my * uy + mz * uz
    base = 1.25 * rho - 1.875 * square
    post = [None] * 19
    if 0 in keep:
        post[0] = jnp.where(solid, g[0], base - 0.25 * g[0])
    for a in range(1, 19, 2):
        if a not in keep and a + 1 not in keep:
            continue
        m = pair_vector(a, mx, my, mz)
        p = pair_vector(a, ux, uy, uz)
        even = base + 5.625 * (m * p)
        odd = 3.75 * m
        if a in keep:
            post[a] = jnp.where(solid, g[a + 1], (even + odd) - 0.25 * g[a])
        if a + 1 in keep:
            post[a + 1] = jnp.where(solid, g[a], (even - odd) - 0.25 * g[a + 1])
    return post


def inlet_state(ux, uy, uz):
    base = 1.0 - 1.5 * (ux * ux + uy * uy + uz * uz)
    out = [base] * 19
    for a in range(1, 19, 2):
        p = pair_vector(a, ux, uy, uz)
        even = base + 4.5 * (p * p)
        odd = 3.0 * p
        out[a] = even + odd
        out[a + 1] = even - odd
    return out


def wall_rows(first_row, height, kz, nz):
    rows = lax.broadcasted_iota(jnp.int32, (8, 128), 0) + first_row
    return ((rows == 0) & (kz == 0)) | ((rows == height - 1) & (kz == nz - 1))


def edge_kernel(
    nz, pops, mask, noise, mean, diag, off, za, zb, raw, flags, mean_v, diag_v, off_v, edge, sems
):
    height = pops.shape[2]
    kz = lax.axis_index("gz")
    upward = lax.rem(kz, 2) == 0
    upper = pl.ds(height - 8, 8)
    copies = [
        (pops.at[:, :, 0:8, :], raw.at[:, :, 0:8, :]),
        (pops.at[:, :, upper, :], raw.at[:, :, 8:16, :]),
        (mask.at[:, 0:8, :], flags.at[:, 0:8, :]),
        (mask.at[:, upper, :], flags.at[:, 8:16, :]),
        (mean, mean_v),
        (diag, diag_v),
        (off, off_v),
    ]
    for c in range(3):
        at = slice(ROW_NOISE + height * c, ROW_NOISE + height * (c + 1))
        copies.append((noise.at[c], za.at[at, :]))
        copies.append((noise.at[c], zb.at[at, :]))
    copies = [pltpu.make_async_copy(src, dst, sems.at[n]) for n, (src, dst) in enumerate(copies)]
    for copy in copies:
        copy.start()
    for part, row in ((0, 0), (1, height - 8)):
        copies[part].wait()
        copies[2 + part].wait()
        wall = wall_rows(row, height, kz, nz)
        at = slice(8 * part, 8 * part + 8)
        for x in range(4):
            solid = (flags[x, at, :] == 1) | wall
            post = collide([raw[i, x, at, :] for i in range(19)], solid)
            post.append(solid.astype(jnp.float32))
            for i in range(20):
                edge[64 * i + 16 * x + 8 * part : 64 * i + 16 * x + 8 * part + 8, :] = post[i]

    def put(q, i, depth):
        up = edge[pl.ds(64 * i + 15 - depth, 4, stride=16), :]
        down = edge[pl.ds(64 * (i if i == 19 else MIRROR_Z[i]) + depth, 4, stride=16), :]
        za[4 * q : 4 * q + 4, :] = jnp.where(upward, up, down)
        zb[4 * q : 4 * q + 4, :] = jnp.where(upward, down, up)

    for q, i in enumerate(Z_EDGE + Z_SECOND + [19]):
        put(q, i, 1 if len(Z_EDGE) <= q < 19 else 0)
    for copy in copies[4:]:
        copy.wait()
    for ref in (za, zb):
        ref[ROW_PARAM : ROW_PARAM + 8, :] = jnp.zeros((8, 128), jnp.float32)
        ref[ROW_PARAM : ROW_PARAM + 1, 0:height] = mean_v[...]
        ref[ROW_PARAM + 1 : ROW_PARAM + 4, 0:height] = diag_v[...]
        ref[ROW_PARAM + 4 : ROW_PARAM + 7, 0:height] = off_v[...]


def far_kernel(height, za, z2):
    kz = lax.axis_index("gz")
    low_half = lax.rem(kz, 4) < 2
    z2[...] = jnp.zeros((16, 128), jnp.float32)
    for c in range(3):
        base = ROW_NOISE + height * c
        last = za[base + height - 1 : base + height, :]
        first = za[base : base + 1, :]
        z2[c : c + 1, :] = jnp.where(low_half, last, first)
        z2[8 + c : 9 + c, :] = jnp.where(low_half, first, last)


def dot3(a, b, dims=(((1,), (0,)), ((), ()))):
    a_hi, b_hi = a.astype(jnp.bfloat16), b.astype(jnp.bfloat16)
    a_lo = (a - a_hi.astype(jnp.float32)).astype(jnp.bfloat16)
    b_lo = (b - b_hi.astype(jnp.float32)).astype(jnp.bfloat16)

    def dot(u, v):
        return lax.dot_general(u, v, dims, preferred_element_type=jnp.float32)

    return dot(a_hi, b_hi) + (dot(a_lo, b_hi) + dot(a_hi, b_lo))


NT = (((1,), (1,)), ((), ()))


def put_pair(pair, slot, value, first_column, into):
    return jnp.where(pair == slot, pltpu.roll(value, (2 * slot - first_column) % 128, 1), into)


def bulk_kernel(nz, pops, mask, post, solidp, ya, yb):
    height = pops.shape[2]
    kz = lax.axis_index("gz")
    ky = lax.axis_index("gy") * lax.axis_size("col") + lax.axis_index("col")
    y_even = lax.rem(ky, 2) == 0
    pair = lax.broadcasted_iota(jnp.int32, (8, 128), 1) // 2

    def body(t, carry):
        row = pl.multiple_of(t * 8, 8)
        out = pl.ds(row + PAD, 8)
        wall = wall_rows(row, height, kz, nz)
        flat = right = left = jnp.zeros((8, 128), jnp.float32)
        for x in range(4):
            solid = (mask[x, pl.ds(row, 8), :] == 1) | wall
            p = collide([pops[i, x, pl.ds(row, 8), :] for i in range(19)], solid)
            flag = solid.astype(jnp.float32)
            solidp[x, out, :] = flag
            flat = put_pair(pair, FLAG_PLANE + x, flag, 127, flat)
            for q, i in enumerate(Y_FLAT):
                post[i, x, out, :] = p[i]
                flat = put_pair(pair, 4 * q + x, p[i], 127, flat)
            for n, i in enumerate(Y_PLUS):
                j = MIRROR_Y[i]
                slot = LANE_PLUS // 2 + 4 * n + x
                post[i, x, out, :], post[j, x, out, :] = p[i], p[j]
                right = put_pair(pair, slot, p[i], 126, right)
                left = put_pair(pair, slot, p[j], 0, left)
        right = jnp.where(pair < LANE_PLUS // 2, flat, right)
        left = jnp.where(pair < LANE_PLUS // 2, flat, left)
        ya[pl.ds(row, 8), :] = jnp.where(y_even, right, left)
        yb[pl.ds(row, 8), :] = jnp.where(y_even, left, right)
        return carry

    lax.fori_loop(0, height // 8, body, 0)


def column_kernel(
    nz, post_in, solid_in, sent, za, zb, z2c, z2d, bandz, pick,
    post, solidp, ya, yb, linear, meanrow,
    wide, filt, edges,
):
    height = post.shape[2] - 2 * PAD
    rows = height + 2 * PAD
    kz = lax.axis_index("gz")
    ky = lax.axis_index("gy") * lax.axis_size("col") + lax.axis_index("col")
    z_even = lax.rem(kz, 2) == 0
    y_even = lax.rem(ky, 2) == 0
    low_half = lax.rem(kz, 4) < 2

    def below(row, n=1):
        return jnp.where(z_even, zb[row : row + n, :], za[row : row + n, :])

    def above(row, n=1):
        return jnp.where(z_even, za[row : row + n, :], zb[row : row + n, :])

    top = PAD + height
    edges[0], edges[1] = below(0, ROW_PARAM), above(0, ROW_PARAM)
    for items, first, depth in ((Z_EDGE, 0, 0), (Z_SECOND, len(Z_EDGE), 1)):
        for q, i in enumerate(items):
            for x in range(4):
                at = slice(4 * (first + q) + x, 4 * (first + q) + x + 1)
                post[i, x, PAD - 1 - depth : PAD - depth, :] = edges[0, at, :]
                post[MIRROR_Z[i], x, top + depth : top + depth + 1, :] = edges[1, at, :]
    for x in range(4):
        solidp[x, PAD - 1 : PAD, :] = edges[0, ROW_SOLID + x : ROW_SOLID + x + 1, :]
        solidp[x, top : top + 1, :] = edges[1, ROW_SOLID + x : ROW_SOLID + x + 1, :]

    lane = lax.broadcasted_iota(jnp.int32, (8, 128), 1)
    own_par = pltpu.roll(sent[ROW_PARAM : ROW_PARAM + 8, :], PAD, 1)
    low_par = pltpu.roll(below(ROW_PARAM, 8), 128 - height + PAD, 1)
    high_par = pltpu.roll(above(ROW_PARAM, 8), height + PAD, 1)
    par = jnp.where(lane < PAD, low_par, jnp.where(lane < top, own_par, high_par))
    par = jnp.where(lane < rows, par, 0.0)
    meanrow[...] = par
    cols = jnp.transpose(jnp.concatenate([par] * 16, axis=0))[0:rows]

    for c in range(3):
        lanes = slice(128 * c, 128 * c + 128)
        at = slice(ROW_NOISE + height * c, ROW_NOISE + height * (c + 1))
        wide[0:height, lanes] = below(ROW_NOISE + height * c, height)
        wide[height : 2 * height, lanes] = sent[at, :]
        wide[2 * height : 3 * height, lanes] = above(ROW_NOISE + height * c, height)
    filt[...] = dot3(bandz[...], wide[...])
    b_end = float(taps()[0])
    far_low = jnp.where(low_half, z2d[8:16, :], z2c[0:8, :])
    far_high = jnp.where(low_half, z2c[0:8, :], z2d[8:16, :])
    for c in range(3):
        lanes = slice(128 * c, 128 * c + 128)
        filt[PAD - 1 : PAD, lanes] += b_end * far_low[c : c + 1, :]
        filt[top : top + 1, lanes] += b_end * far_high[c : c + 1, :]
    f0, f1, f2 = (filt[:, 128 * c : 128 * c + 128] for c in range(3))
    linear[0] = cols[:, 1:2] * f0
    linear[1] = cols[:, 4:5] * f0 + cols[:, 2:3] * f1
    linear[2] = cols[:, 5:6] * f0 + cols[:, 6:7] * f1 + cols[:, 3:4] * f2
    linear[3] = jnp.broadcast_to(cols[:, 0:1], (rows, 128))

    pair = lane // 2
    for row in (0, rows - 8):
        out = slice(row, row + 8)
        flat = right = left = jnp.zeros((8, 128), jnp.float32)
        for x in range(4):
            flat = put_pair(pair, FLAG_PLANE + x, solidp[x, out, :], 127, flat)
            for q, i in enumerate(Y_FLAT):
                flat = put_pair(pair, 4 * q + x, post[i, x, out, :], 127, flat)
            for n, i in enumerate(Y_PLUS):
                slot = LANE_PLUS // 2 + 4 * n + x
                right = put_pair(pair, slot, post[i, x, out, :], 126, right)
                left = put_pair(pair, slot, post[MIRROR_Y[i], x, out, :], 0, left)
        right = jnp.where(pair < LANE_PLUS // 2, flat, right)
        left = jnp.where(pair < LANE_PLUS // 2, flat, left)
        at = slice(0, 2) if row else slice(6, 8)
        ya[at, :] = jnp.where(y_even, right, left)[at, :]
        yb[at, :] = jnp.where(y_even, left, right)[at, :]
    spare = jnp.zeros((1, 128), jnp.float32)
    for c in range(3):
        far = dot3(pick[...], linear[c], NT)
        far = jnp.concatenate([far, jnp.zeros((8, 128 - rows), jnp.float32)], axis=1)
        ya[Y_FAR + c : Y_FAR + c + 1, :] = jnp.where(y_even, far[0:1, :], far[1:2, :])
        yb[Y_FAR + c : Y_FAR + c + 1, :] = jnp.where(y_even, far[1:2, :], far[0:1, :])
    for ref in (ya, yb):
        ref[5:6, :] = spare
        ref[Y_FILTER + 3 * Y_HALF : Y_MESSAGE, :] = jnp.zeros((2, 128), jnp.float32)
    middle = FIRST + Y_HALF
    lane_h = lax.broadcasted_iota(jnp.int32, (Y_HALF, 128), 1)
    for c in range(3):
        first, second = linear[c, FIRST:middle, :], linear[c, middle : middle + Y_HALF, :]
        left = jnp.where(lane_h < 64, first, pltpu.roll(second, 64, 1))
        right = jnp.where(lane_h < 64, pltpu.roll(first, 64, 1), second)
        at = slice(Y_FILTER + Y_HALF * c, Y_FILTER + Y_HALF * (c + 1))
        ya[at, :] = jnp.where(y_even, right, left)
        yb[at, :] = jnp.where(y_even, left, right)


def streamed(i, x):
    source = x - DIRS[i][0]
    return None if source < 0 else min(source, 3)


INWARD = [i for i in range(19) if DIRS[i][2]]


def both_ghosts(sub, low, high):
    return jnp.where(sub < 4, low, high)


def assemble(tall, sa, sb, ya, yb, a_first):
    end = PAD + sa.shape[0]
    for out, source, a, b in (
        (slice(PAD, end), slice(0, sa.shape[0]), sa, sb),
        (slice(PAD - 2, PAD), slice(6, 8), ya, yb),
        (slice(end, end + 2), slice(0, 2), ya, yb),
    ):
        tall[0, out, :] = jnp.where(a_first, a[source, :], b[source, :])
        tall[1, out, :] = jnp.where(a_first, b[source, :], a[source, :])


def interior_kernel(
    nz, post, solidp, linear, sa, sb, ya, yb, wy, wg, post2, flow_own, ghost_own, own_right, own_left, tall
):
    rows = post.shape[2]
    top = rows - PAD
    kz = lax.axis_index("gz")
    ky = lax.axis_index("gy") * lax.axis_size("col") + lax.axis_index("col")
    y_even = lax.rem(ky, 2) == 0
    sub = lax.broadcasted_iota(jnp.int32, (8, 128), 0)

    def moved(i, value):
        return pltpu.roll(value, DIRS[i][1] % 128, 1) if DIRS[i][1] else value

    outside = ((sub < 4) & (kz == 0)) | ((sub >= 4) & (kz == nz - 1))
    for x in range(1, 4):
        solid = both_ghosts(sub, solidp[x, PAD - 1 : PAD + 7, :], solidp[x, top - 7 : top + 1, :]) > 0.5
        g = []
        for i in range(19):
            low, high, source = PAD - 1 - DIRS[i][2], top - 7 - DIRS[i][2], streamed(i, x)
            value = both_ghosts(sub, post[i, source, low : low + 8, :], post[i, source, high : high + 8, :])
            g.append(moved(i, value))
        p = collide(g, solid, INWARD)
        for i in INWARD:
            row, at = (PAD - 1, 0) if DIRS[i][2] == 1 else (top, 7)
            value = moved(i, jnp.where(outside, 0.0, p[i]))
            post2[i, x - 1, row : row + 1, :] = value[at : at + 1, :]

    def body(t, carry):
        row = pl.multiple_of(t * 8 + PAD, 8)
        for x in range(1, 4):
            solid = solidp[x, pl.ds(row, 8), :] > 0.5
            g = [moved(i, post[i, streamed(i, x), pl.ds(row - DIRS[i][2], 8), :]) for i in range(19)]
            p = collide(g, solid)
            for i in range(19):
                post2[i, x - 1, pl.ds(row, 8), :] = moved(i, p[i])
        return carry

    lax.fori_loop(0, rows // 8 - 2, body, 0)

    flow_own[...] = dot3(linear[0:3].reshape(3 * rows, 128), wy[0:128, :])
    flow_own[0:rows, :] += linear[3]
    for c in range(3):
        ghost_own[8 * c : 8 * c + 8, 0:rows] = dot3(wg[:, 0:128], linear[c], NT)
        ghost_own[8 * c : 8 * c + 8, rows:128] = jnp.zeros((8, 128 - rows), jnp.float32)
    assemble(tall, sa, sb, ya, yb, y_even)
    own_right[0:128, :] = jnp.transpose(tall[0])
    own_left[0:128, :] = jnp.transpose(tall[1])


def final_kernel(
    nz, post, solidp, post2, flow_own, ghost_own, own_right, own_left, meanrow, sa, sb, ya, yb, wy, wg,
    inflow, state_out,
    lhs, flow, inlet2, strip_left, strip_right, moving, still, ghost_moving, ghost_still,
    state, flow_out, tall, sems,
):
    height = state.shape[2]
    rows = height + 2 * PAD
    top = PAD + height
    kz = lax.axis_index("gz")
    ky = lax.axis_index("gy") * lax.axis_size("col") + lax.axis_index("col")
    y_even = lax.rem(ky, 2) == 0
    lane = lax.broadcasted_iota(jnp.int32, (8, 128), 1)
    sub = lax.broadcasted_iota(jnp.int32, (8, 128), 0)

    assemble(tall, sa, sb, ya, yb, jnp.logical_not(y_even))
    strip_left[0:128, 0:rows] = jnp.transpose(tall[0, 0:rows, :])
    strip_right[0:128, 0:rows] = jnp.transpose(tall[1, 0:rows, :])

    lane_h = lax.broadcasted_iota(jnp.int32, (Y_HALF, 128), 1)
    for c in range(3):
        at = slice(Y_FILTER + Y_HALF * c, Y_FILTER + Y_HALF * (c + 1))
        a, b = ya[at, :], yb[at, :]
        left, right = jnp.where(y_even, b, a), jnp.where(y_even, a, b)
        middle = rows * c + FIRST + Y_HALF
        lo, hi = slice(middle - Y_HALF, middle), slice(middle, middle + Y_HALF)
        lhs[lo, 0:128] = jnp.where(lane_h < 64, left, 0.0)
        lhs[hi, 0:128] = jnp.where(lane_h < 64, 0.0, left)
        lhs[lo, 128:256] = jnp.where(lane_h < 64, right, 0.0)
        lhs[hi, 128:256] = jnp.where(lane_h < 64, 0.0, right)
    flow[...] = flow_own[...] + dot3(lhs[...], wy[128:384, :])
    for c in range(3):
        flow_out[c] = flow[rows * c + PAD : rows * c + top, :]
    flow_copy = pltpu.make_async_copy(flow_out, inflow, sems.at[height // 8])
    flow_copy.start()
    b_end = float(taps()[0])
    column_flow = []
    for c in range(3):
        g = dot3(wg[:, 128:384], lhs[rows * c : rows * (c + 1), :], NT)
        g = jnp.concatenate([g, jnp.zeros((8, 128 - rows), jnp.float32)], axis=1)
        g = g + ghost_own[8 * c : 8 * c + 8, :]
        far = slice(Y_FAR + c, Y_FAR + c + 1)
        at = [g[n : n + 1, :] for n in range(4)]
        at[0] = at[0] + b_end * jnp.where(y_even, yb[far, :], ya[far, :])
        at[3] = at[3] + b_end * jnp.where(y_even, ya[far, :], yb[far, :])
        if c == 0:
            at = [v + meanrow[0:1, :] for v in at]
        column_flow.append(at)

    outside = ((lane < PAD) & (kz == 0)) | ((lane >= top) & (kz == nz - 1))
    sources = (
        ((strip_left, 0), (strip_left, 0), (own_left, 0)),
        ((own_left, 1), (strip_left, 1), (own_left, 1)),
        ((own_right, 0), (own_right, 0), (strip_right, 0)),
        ((strip_right, 1), (own_right, 1), (strip_right, 1)),
    )
    for column in range(4):
        def rows_of(start):
            return pl.ds(start, 8, stride=2)

        src, odd = sources[column][0]
        solid = src[rows_of(2 * FLAG_PLANE + odd), :] > 0.5
        g = [None] * 19
        for i in range(19):
            cx, cy, cz = DIRS[i]
            src, odd = sources[column][cy % 3]
            if cy == 0:
                start = 8 * Y_FLAT.index(i) + odd
            else:
                start = LANE_PLUS + 8 * Y_PLUS.index(i if cy == 1 else MIRROR_Y[i]) + odd
            v = src[rows_of(start - 2 * cx), :]
            if cx == 1:
                v = jnp.where(sub == 0, 0.0, v)
            elif cx == -1:
                v = jnp.where(sub == 3, src[rows_of(start), :], v)
            g[i] = v if cz == 0 else pltpu.roll(v, cz % 128, 1)
        us = [INLET * jnp.broadcast_to(column_flow[c][column], (8, 128)) for c in range(3)]
        eq = inlet_state(*us)
        put = (sub == 0) & jnp.logical_not(solid)
        moves = 1 if column < 2 else -1
        keep = [i for i in range(19) if DIRS[i][1] == moves or (DIRS[i][1] == 0 and column in (1, 2))]
        p = collide(g, solid, keep)
        for i in keep:
            value = jnp.where(outside, 0.0, jnp.where(put, eq[i], p[i]))[0:4, :]
            if DIRS[i][1]:
                n = Y_PLUS.index(i if moves == 1 else MIRROR_Y[i])
                moving[pl.ds(16 * n + (column + 2) % 4, 4, stride=4), :] = value
            else:
                still[pl.ds(8 * Y_FLAT.index(i) + 2 - column, 4, stride=2), :] = value
    ghost_moving[:, 0:80] = jnp.transpose(moving[0:80, :])
    ghost_still[:, 0:72] = jnp.transpose(still[0:72, :])

    def inlet_values(us, solid, planes, load):
        eq = inlet_state(*[INLET * u for u in us])
        for i in planes:
            j = OPP[i]
            source = streamed(j, 0)
            bounced = 0.0 if source is None else moved(j, load(j, source))
            yield i, jnp.where(solid, bounced, eq[i])

    def moved(i, value):
        return pltpu.roll(value, DIRS[i][1] % 128, 1) if DIRS[i][1] else value

    def inlet(row):
        us = [flow[pl.ds(rows * c + row, 8), :] for c in range(3)]
        solid = solidp[0, pl.ds(row, 8), :] > 0.5
        load = lambda j, source: post[j, source, pl.ds(row - DIRS[j][2], 8), :]
        for i, value in inlet_values(us, solid, range(19), load):
            inlet2[i, pl.ds(row, 8), :] = moved(i, value)

    def inlet_ghosts():
        low, high = PAD - 1, top - 7

        def both(ref, shift, *lead):
            low_at, high_at = slice(low + shift, low + shift + 8), slice(high + shift, high + shift + 8)
            return both_ghosts(sub, ref[(*lead, low_at)], ref[(*lead, high_at)])

        us = [both(flow, rows * c) for c in range(3)]
        solid = both(solidp, 0, 0) > 0.5
        load = lambda j, source: both(post, -DIRS[j][2], j, source)
        beyond = ((sub < 4) & (kz == 0)) | ((sub >= 4) & (kz == nz - 1))
        for i, value in inlet_values(us, solid, INWARD, load):
            row, at = (PAD - 1, 0) if DIRS[i][2] == 1 else (top, 7)
            value = moved(i, jnp.where(beyond, 0.0, value))
            inlet2[i, row : row + 1, :] = value[at : at + 1, :]

    def out_copy(t):
        at = pl.ds(pl.multiple_of(t * 8, 8), 8)
        return pltpu.make_async_copy(state.at[:, :, at, :], state_out.at[:, :, at, :], sems.at[t])

    def last(t):
        row = pl.multiple_of(t * 8 + PAD, 8)
        us = [INLET * flow[pl.ds(rows * c + row, 8), :] for c in range(3)]
        eq = inlet_state(*us)
        solid = solidp[0, pl.ds(row, 8), :] > 0.5
        ends = (lane == 0) | (lane == 127)

        def read(i, source, ghost):
            at = pl.ds(row - DIRS[i][2], 8)
            v = inlet2[i, at, :] if source == 0 else post2[i, source - 1, at, :]
            where = ends if DIRS[i][1] == 0 else (lane < 2 if DIRS[i][1] == 1 else lane >= 126)
            return jnp.where(where, ghost, v)

        def write(i, x, value):
            if x == 0:
                value = jnp.where(solid, value, eq[i])
            state[i, x, pl.ds(row - PAD, 8), :] = value

        for i in Y_FLAT + Y_PLUS:
            both = [i] if DIRS[i][1] == 0 else [i, MIRROR_Y[i]]
            at = pl.ds(row - DIRS[i][2], 8)
            for source in range(4):
                targets = [x for x in range(4) if streamed(i, x) == source]
                if not targets:
                    continue
                if DIRS[i][1] == 0:
                    slot = 2 * (4 * Y_FLAT.index(i) + source)
                    ghost = pltpu.roll(ghost_still[at, :], (127 - slot) % 128, 1)
                else:
                    slot = 4 * (4 * Y_PLUS.index(i) + source)
                    ghost = pltpu.roll(ghost_moving[at, :], (126 - slot) % 128, 1)
                for j in both:
                    value = read(j, source, ghost)
                    for x in targets:
                        write(j, x, value)
            for j in both:
                if streamed(j, 0) is None:
                    write(j, 0, jnp.zeros((8, 128), jnp.float32))
        out_copy(t).start()

    inlet_ghosts()
    inlet(PAD)

    def main(t, carry):
        inlet(pl.multiple_of(t * 8 + PAD, 8))
        last(t - 1)
        return carry

    tiles = height // 8
    lax.fori_loop(1, tiles, main, 0)
    last(tiles - 1)
    for t in range(tiles):
        out_copy(t).wait()
    flow_copy.wait()


def swap_pairs(count, phase, distance=1):
    pairs = []
    for i in range(count):
        block = (i + phase * distance) // distance
        j = i + distance if block % 2 == 0 else i - distance
        if 0 <= j < count:
            pairs.append((i, j))
    return pairs


def ring_pairs(count, phase):
    if phase == 0:
        return [(i, i ^ 1) for i in range(count)]
    return [(i, (((i + 1) % count ^ 1) - 1) % count) for i in range(count)]


def vm(n):
    return [pl.BlockSpec(memory_space=pltpu.VMEM)] * n


def hbm(n):
    return [pl.BlockSpec(memory_space=pltpu.HBM)] * n


def f32(*shape):
    return jax.ShapeDtypeStruct(shape, jnp.float32)


def scratch(*shape):
    return pltpu.VMEM(shape, jnp.float32)


def flags(*shape):
    return pltpu.VMEM(shape, jnp.int32)


def params(mib):
    return pltpu.CompilerParams(vmem_limit_bytes=mib * 1024 * 1024)


def cost(flops, size):
    return pl.CostEstimate(flops=flops, bytes_accessed=size, transcendentals=0)


def shards(nz, ny, noise, mean_profile, lund_diag, lund_off, populations, mask):
    height, span = noise.shape[1], noise.shape[2]
    rows = height + 2 * PAD
    message = ROW_NOISE + 3 * height
    dma = pltpu.SemaphoreType.DMA
    here = lambda value: pltpu.with_memory_space_constraint(value, pltpu.HBM)
    mean_profile = mean_profile.reshape(1, height)
    operands = populations, mask, noise, mean_profile, lund_diag, lund_off

    za, zb = pl.pallas_call(
        lambda *refs: edge_kernel(nz, *refs),
        out_shape=(f32(message, 128), f32(message, 128)),
        in_specs=hbm(6),
        out_specs=vm(2),
        scratch_shapes=[
            scratch(19, 4, 16, 128), flags(4, 16, 128), scratch(1, height), scratch(3, height),
            scratch(3, height), scratch(20 * 4 * 16, 128), dma((13,)),
        ],
        compiler_params=params(8),
        name="edge_rows",
    )(*map(here, operands))

    z2 = pl.pallas_call(
        lambda *refs: far_kernel(height, *refs),
        out_shape=f32(16, 128),
        in_specs=vm(1),
        out_specs=pl.BlockSpec(memory_space=pltpu.VMEM),
        compiler_params=params(1),
        name="far_rows",
    )(za)

    ra = lax.ppermute(za, "gz", swap_pairs(nz, 0))
    rb = lax.ppermute(zb, "gz", swap_pairs(nz, 1))
    rc = lax.ppermute(z2, "gz", swap_pairs(nz, 0, 2))
    far = swap_pairs(nz, 1, 2)
    rd = lax.ppermute(z2, "gz", far) if far else jnp.zeros_like(z2)

    post, solidp, sa, sb = pl.pallas_call(
        lambda *refs: bulk_kernel(nz, *refs),
        out_shape=(f32(19, 4, rows, 128), f32(4, rows, 128), f32(height, 128), f32(height, 128)),
        in_specs=vm(2),
        out_specs=vm(4),
        compiler_params=params(4),
        cost_estimate=cost(4_000_000_000, 8_000_000),
        name="bulk",
    )(populations, mask)

    pa = lax.ppermute(sa, ("gy", "col"), ring_pairs(ny, 0))
    pb = lax.ppermute(sb, ("gy", "col"), ring_pairs(ny, 1))
    pick = np.zeros((8, 128), np.float32)
    pick[0, span - HW - 1] = pick[1, HW] = 1.0

    line = np.arange(rows) - PAD
    used = (line >= -1) & (line <= height)
    bandz = np.where(used[:, None], band(np.arange(-height, 2 * height), line).T, 0.0)
    post, solidp, ya, yb, linear, meanrow = pl.pallas_call(
        lambda *refs: column_kernel(nz, *refs),
        out_shape=(
            f32(19, 4, rows, 128), f32(4, rows, 128), f32(Y_MESSAGE, 128), f32(Y_MESSAGE, 128),
            f32(4, rows, 128), f32(8, 128),
        ),
        in_specs=vm(9),
        out_specs=vm(6),
        scratch_shapes=[
            scratch(3 * height, 384), scratch(rows, 384), scratch(2, ROW_PARAM, 128),
        ],
        input_output_aliases={0: 0, 1: 1},
        compiler_params=params(4),
        name="columns",
    )(post, solidp, za, ra, rb, rc, rd, jnp.asarray(bandz, jnp.float32), jnp.asarray(pick))

    qa = lax.ppermute(ya, ("gy", "col"), ring_pairs(ny, 0))
    qb = lax.ppermute(yb, ("gy", "col"), ring_pairs(ny, 1))

    own = np.arange(span)
    left = np.arange(128) % 64 - 64
    right = np.arange(128) % 64 + span
    source = np.concatenate([own, left, right])
    wy = jnp.asarray(band(source, own))
    wg = np.zeros((8, 384), np.float32)
    wg[0:4] = band(source, np.array([-1, 0, span - 1, span])).T
    wg = jnp.asarray(wg)
    post2, flow_own, ghost_own, own_right, own_left = pl.pallas_call(
        lambda *refs: interior_kernel(nz, *refs),
        out_shape=(
            f32(19, 3, rows, 128), f32(3 * rows, 128), f32(24, 128), f32(144, 128), f32(144, 128),
        ),
        in_specs=vm(9),
        out_specs=vm(5),
        scratch_shapes=[scratch(2, 128, 128)],
        compiler_params=params(4),
        cost_estimate=cost(4_000_000_000, 8_000_000),
        name="interior",
    )(post, solidp, linear, sa, sb, ya, yb, wy, wg)
    inflow, state = pl.pallas_call(
        lambda *refs: final_kernel(nz, *refs),
        out_shape=(f32(3, height, span), f32(19, 4, height, span)),
        in_specs=vm(14),
        out_specs=hbm(2),
        scratch_shapes=[
            scratch(3 * rows, 256), scratch(3 * rows, 128), scratch(19, rows, 128),
            scratch(144, 128), scratch(144, 128), scratch(128, 128), scratch(128, 128),
            scratch(128, 128), scratch(128, 128), scratch(19, 4, height, span),
            scratch(3, height, span), scratch(2, 128, 128), dma((height // 8 + 1,)),
        ],
        compiler_params=params(8),
        name="stream",
    )(post, solidp, post2, flow_own, ghost_own, own_right, own_left, meanrow, pa, pb, qa, qb, wy, wg)
    return inflow, state


def solution(mesh):
    nz = mesh.shape["gz"]
    ny = mesh.shape["gy"] * mesh.shape["col"]
    in_specs = (
        P(None, "gz", ("gy", "col")),
        P("gz"),
        P(None, "gz"),
        P(None, "gz"),
        P(None, None, "gz", ("gy", "col")),
        P(None, "gz", ("gy", "col")),
    )
    out_specs = (P(None, "gz", ("gy", "col")), P(None, None, "gz", ("gy", "col")))

    def body(*args):
        return shards(nz, ny, *args)

    return jax.shard_map(body, mesh=mesh, in_specs=in_specs, out_specs=out_specs, check_vma=False)
```

```python
import math

import jax
import jax.numpy as jnp
import numpy as np
from jax import lax
from jax.experimental import pallas as pl
from jax.experimental.pallas import tpu as pltpu
from jax.sharding import PartitionSpec as P

HW = 64
DIRS = [
    (0, 0, 0),
    (1, 0, 0), (-1, 0, 0), (0, 1, 0), (0, -1, 0), (0, 0, 1), (0, 0, -1),
    (1, 1, 0), (-1, -1, 0), (1, -1, 0), (-1, 1, 0),
    (1, 0, 1), (-1, 0, -1), (1, 0, -1), (-1, 0, 1),
    (0, 1, 1), (0, -1, -1), (0, 1, -1), (0, -1, 1),
]
OPP = [DIRS.index((-a, -b, -c)) for a, b, c in DIRS]
MIRROR_Y = [DIRS.index((a, -b, c)) for a, b, c in DIRS]
MIRROR_Z = [DIRS.index((a, b, -c)) for a, b, c in DIRS]
INLET = 0.05

Z_EDGE = [i for i in range(19) if DIRS[i][2] == 0] + [i for i in range(19) if DIRS[i][2] == 1]
Z_SECOND = [i for i in range(19) if DIRS[i][2] == 1]
Y_FLAT = [i for i in range(19) if DIRS[i][1] == 0]
Y_PLUS = [i for i in range(19) if DIRS[i][1] == 1]
FLAG_PLANE = 4 * len(Y_FLAT)
LANE_PLUS = 2 * FLAG_PLANE + 8

ROW_SOLID = 76
ROW_PARAM = 80
ROW_NOISE = 88
PAD = 8
FIRST = PAD - 2
Y_HALF = 34
Y_FAR = 2
Y_FILTER = 8
Y_MESSAGE = 112


def taps():
    k = np.arange(-HW, HW + 1).astype(np.float64)
    raw = np.exp(-math.pi * k * k / (2.0 * (HW // 2) ** 2))
    return raw / np.sqrt(np.sum(raw * raw))


def band(source, target):
    values = taps()
    offset = np.asarray(source)[:, None] - np.asarray(target)[None, :]
    inside = np.abs(offset) <= HW
    return np.where(inside, values[np.clip(offset + HW, 0, 2 * HW)], 0.0).astype(np.float32)


def moments(g):
    s = {a: g[a] + g[a + 1] for a in range(1, 19, 2)}
    d = {a: g[a] - g[a + 1] for a in range(1, 19, 2)}
    w1, w2 = 1.0 / 18.0, 1.0 / 36.0
    rho = (
        g[0] * (1.0 / 3.0)
        + (s[1] + s[3] + s[5]) * w1
        + ((s[7] + s[9]) + (s[11] + s[13]) + (s[15] + s[17])) * w2
    )
    mx = d[1] * w1 + ((d[7] + d[9]) + (d[11] + d[13])) * w2
    my = d[3] * w1 + ((d[7] - d[9]) + (d[15] + d[17])) * w2
    mz = d[5] * w1 + ((d[11] - d[13]) + (d[15] - d[17])) * w2
    return rho, mx, my, mz


def pair_vector(a, vx, vy, vz):
    total = None
    for c, v in zip(DIRS[a], (vx, vy, vz)):
        if c:
            term = v if c > 0 else -v
            total = term if total is None else (total + v if c > 0 else total - v)
    return total


def collide(g, solid, keep=range(19)):
    rho, mx, my, mz = moments(g)
    inv = 1.0 / rho
    ux, uy, uz = mx * inv, my * inv, mz * inv
    square = mx * ux + my * uy + mz * uz
    base = 1.25 * rho - 1.875 * square
    post = [None] * 19
    if 0 in keep:
        post[0] = jnp.where(solid, g[0], base - 0.25 * g[0])
    for a in range(1, 19, 2):
        if a not in keep and a + 1 not in keep:
            continue
        m = pair_vector(a, mx, my, mz)
        p = pair_vector(a, ux, uy, uz)
        even = base + 5.625 * (m * p)
        odd = 3.75 * m
        if a in keep:
            post[a] = jnp.where(solid, g[a + 1], (even + odd) - 0.25 * g[a])
        if a + 1 in keep:
            post[a + 1] = jnp.where(solid, g[a], (even - odd) - 0.25 * g[a + 1])
    return post


def inlet_state(ux, uy, uz):
    base = 1.0 - 1.5 * (ux * ux + uy * uy + uz * uz)
    out = [base] * 19
    for a in range(1, 19, 2):
        p = pair_vector(a, ux, uy, uz)
        even = base + 4.5 * (p * p)
        odd = 3.0 * p
        out[a] = even + odd
        out[a + 1] = even - odd
    return out


def wall_rows(first_row, height, kz, nz):
    rows = lax.broadcasted_iota(jnp.int32, (8, 128), 0) + first_row
    return ((rows == 0) & (kz == 0)) | ((rows == height - 1) & (kz == nz - 1))


def edge_kernel(
    nz, pops, mask, noise, mean, diag, off, za, zb, raw, flags, mean_v, diag_v, off_v, edge, sems
):
    height = pops.shape[2]
    kz = lax.axis_index("gz")
    upward = lax.rem(kz, 2) == 0
    upper = pl.ds(height - 8, 8)
    copies = [
        (pops.at[:, :, 0:8, :], raw.at[:, :, 0:8, :]),
        (pops.at[:, :, upper, :], raw.at[:, :, 8:16, :]),
        (mask.at[:, 0:8, :], flags.at[:, 0:8, :]),
        (mask.at[:, upper, :], flags.at[:, 8:16, :]),
        (mean, mean_v),
        (diag, diag_v),
        (off, off_v),
    ]
    for c in range(3):
        at = slice(ROW_NOISE + height * c, ROW_NOISE + height * (c + 1))
        copies.append((noise.at[c], za.at[at, :]))
        copies.append((noise.at[c], zb.at[at, :]))
    copies = [pltpu.make_async_copy(src, dst, sems.at[n]) for n, (src, dst) in enumerate(copies)]
    for copy in copies:
        copy.start()
    for part, row in ((0, 0), (1, height - 8)):
        copies[part].wait()
        copies[2 + part].wait()
        wall = wall_rows(row, height, kz, nz)
        at = slice(8 * part, 8 * part + 8)
        for x in range(4):
            solid = (flags[x, at, :] == 1) | wall
            post = collide([raw[i, x, at, :] for i in range(19)], solid)
            post.append(solid.astype(jnp.float32))
            for i in range(20):
                edge[64 * i + 16 * x + 8 * part : 64 * i + 16 * x + 8 * part + 8, :] = post[i]

    def put(q, i, depth):
        up = edge[pl.ds(64 * i + 15 - depth, 4, stride=16), :]
        down = edge[pl.ds(64 * (i if i == 19 else MIRROR_Z[i]) + depth, 4, stride=16), :]
        za[4 * q : 4 * q + 4, :] = jnp.where(upward, up, down)
        zb[4 * q : 4 * q + 4, :] = jnp.where(upward, down, up)

    for q, i in enumerate(Z_EDGE + Z_SECOND + [19]):
        put(q, i, 1 if len(Z_EDGE) <= q < 19 else 0)
    for copy in copies[4:]:
        copy.wait()
    for ref in (za, zb):
        ref[ROW_PARAM : ROW_PARAM + 8, :] = jnp.zeros((8, 128), jnp.float32)
        ref[ROW_PARAM : ROW_PARAM + 1, 0:height] = mean_v[...]
        ref[ROW_PARAM + 1 : ROW_PARAM + 4, 0:height] = diag_v[...]
        ref[ROW_PARAM + 4 : ROW_PARAM + 7, 0:height] = off_v[...]


def far_kernel(height, za, z2):
    kz = lax.axis_index("gz")
    low_half = lax.rem(kz, 4) < 2
    z2[...] = jnp.zeros((16, 128), jnp.float32)
    for c in range(3):
        base = ROW_NOISE + height * c
        last = za[base + height - 1 : base + height, :]
        first = za[base : base + 1, :]
        z2[c : c + 1, :] = jnp.where(low_half, last, first)
        z2[8 + c : 9 + c, :] = jnp.where(low_half, first, last)


def dot3(a, b, dims=(((1,), (0,)), ((), ()))):
    a_hi, b_hi = a.astype(jnp.bfloat16), b.astype(jnp.bfloat16)
    a_lo = (a - a_hi.astype(jnp.float32)).astype(jnp.bfloat16)
    b_lo = (b - b_hi.astype(jnp.float32)).astype(jnp.bfloat16)

    def dot(u, v):
        return lax.dot_general(u, v, dims, preferred_element_type=jnp.float32)

    return dot(a_hi, b_hi) + (dot(a_lo, b_hi) + dot(a_hi, b_lo))


NT = (((1,), (1,)), ((), ()))


def put_pair(pair, slot, value, first_column, into):
    return jnp.where(pair == slot, pltpu.roll(value, (2 * slot - first_column) % 128, 1), into)


def bulk_kernel(nz, pops, mask, post, solidp, ya, yb):
    height = pops.shape[2]
    kz = lax.axis_index("gz")
    ky = lax.axis_index("gy") * lax.axis_size("col") + lax.axis_index("col")
    y_even = lax.rem(ky, 2) == 0
    pair = lax.broadcasted_iota(jnp.int32, (8, 128), 1) // 2

    def body(t, carry):
        row = pl.multiple_of(t * 8, 8)
        out = pl.ds(row + PAD, 8)
        wall = wall_rows(row, height, kz, nz)
        flat = right = left = jnp.zeros((8, 128), jnp.float32)
        for x in range(4):
            solid = (mask[x, pl.ds(row, 8), :] == 1) | wall
            p = collide([pops[i, x, pl.ds(row, 8), :] for i in range(19)], solid)
            flag = solid.astype(jnp.float32)
            solidp[x, out, :] = flag
            flat = put_pair(pair, FLAG_PLANE + x, flag, 127, flat)
            for q, i in enumerate(Y_FLAT):
                post[i, x, out, :] = p[i]
                flat = put_pair(pair, 4 * q + x, p[i], 127, flat)
            for n, i in enumerate(Y_PLUS):
                j = MIRROR_Y[i]
                slot = LANE_PLUS // 2 + 4 * n + x
                post[i, x, out, :], post[j, x, out, :] = p[i], p[j]
                right = put_pair(pair, slot, p[i], 126, right)
                left = put_pair(pair, slot, p[j], 0, left)
        right = jnp.where(pair < LANE_PLUS // 2, flat, right)
        left = jnp.where(pair < LANE_PLUS // 2, flat, left)
        ya[pl.ds(row, 8), :] = jnp.where(y_even, right, left)
        yb[pl.ds(row, 8), :] = jnp.where(y_even, left, right)
        return carry

    lax.fori_loop(0, height // 8, body, 0, unroll=2)


def column_kernel(
    nz, post_in, solid_in, sent, za, zb, z2c, z2d, bandz, pick,
    post, solidp, ya, yb, linear, meanrow,
    wide, filt, edges,
):
    height = post.shape[2] - 2 * PAD
    rows = height + 2 * PAD
    kz = lax.axis_index("gz")
    ky = lax.axis_index("gy") * lax.axis_size("col") + lax.axis_index("col")
    z_even = lax.rem(kz, 2) == 0
    y_even = lax.rem(ky, 2) == 0
    low_half = lax.rem(kz, 4) < 2

    def below(row, n=1):
        return jnp.where(z_even, zb[row : row + n, :], za[row : row + n, :])

    def above(row, n=1):
        return jnp.where(z_even, za[row : row + n, :], zb[row : row + n, :])

    top = PAD + height
    edges[0], edges[1] = below(0, ROW_PARAM), above(0, ROW_PARAM)
    for items, first, depth in ((Z_EDGE, 0, 0), (Z_SECOND, len(Z_EDGE), 1)):
        for q, i in enumerate(items):
            for x in range(4):
                at = slice(4 * (first + q) + x, 4 * (first + q) + x + 1)
                post[i, x, PAD - 1 - depth : PAD - depth, :] = edges[0, at, :]
                post[MIRROR_Z[i], x, top + depth : top + depth + 1, :] = edges[1, at, :]
    for x in range(4):
        solidp[x, PAD - 1 : PAD, :] = edges[0, ROW_SOLID + x : ROW_SOLID + x + 1, :]
        solidp[x, top : top + 1, :] = edges[1, ROW_SOLID + x : ROW_SOLID + x + 1, :]

    lane = lax.broadcasted_iota(jnp.int32, (8, 128), 1)
    own_par = pltpu.roll(sent[ROW_PARAM : ROW_PARAM + 8, :], PAD, 1)
    low_par = pltpu.roll(below(ROW_PARAM, 8), 128 - height + PAD, 1)
    high_par = pltpu.roll(above(ROW_PARAM, 8), height + PAD, 1)
    par = jnp.where(lane < PAD, low_par, jnp.where(lane < top, own_par, high_par))
    par = jnp.where(lane < rows, par, 0.0)
    meanrow[...] = par
    cols = jnp.transpose(jnp.concatenate([par] * 16, axis=0))[0:rows]

    for c in range(3):
        lanes = slice(128 * c, 128 * c + 128)
        at = slice(ROW_NOISE + height * c, ROW_NOISE + height * (c + 1))
        wide[0:height, lanes] = below(ROW_NOISE + height * c, height)
        wide[height : 2 * height, lanes] = sent[at, :]
        wide[2 * height : 3 * height, lanes] = above(ROW_NOISE + height * c, height)
    filt[...] = dot3(bandz[...], wide[...])
    b_end = float(taps()[0])
    far_low = jnp.where(low_half, z2d[8:16, :], z2c[0:8, :])
    far_high = jnp.where(low_half, z2c[0:8, :], z2d[8:16, :])
    for c in range(3):
        lanes = slice(128 * c, 128 * c + 128)
        filt[PAD - 1 : PAD, lanes] += b_end * far_low[c : c + 1, :]
        filt[top : top + 1, lanes] += b_end * far_high[c : c + 1, :]
    f0, f1, f2 = (filt[:, 128 * c : 128 * c + 128] for c in range(3))
    linear[0] = cols[:, 1:2] * f0
    linear[1] = cols[:, 4:5] * f0 + cols[:, 2:3] * f1
    linear[2] = cols[:, 5:6] * f0 + cols[:, 6:7] * f1 + cols[:, 3:4] * f2
    linear[3] = jnp.broadcast_to(cols[:, 0:1], (rows, 128))

    pair = lane // 2
    for row in (0, rows - 8):
        out = slice(row, row + 8)
        flat = right = left = jnp.zeros((8, 128), jnp.float32)
        for x in range(4):
            flat = put_pair(pair, FLAG_PLANE + x, solidp[x, out, :], 127, flat)
            for q, i in enumerate(Y_FLAT):
                flat = put_pair(pair, 4 * q + x, post[i, x, out, :], 127, flat)
            for n, i in enumerate(Y_PLUS):
                slot = LANE_PLUS // 2 + 4 * n + x
                right = put_pair(pair, slot, post[i, x, out, :], 126, right)
                left = put_pair(pair, slot, post[MIRROR_Y[i], x, out, :], 0, left)
        right = jnp.where(pair < LANE_PLUS // 2, flat, right)
        left = jnp.where(pair < LANE_PLUS // 2, flat, left)
        at = slice(0, 2) if row else slice(6, 8)
        ya[at, :] = jnp.where(y_even, right, left)[at, :]
        yb[at, :] = jnp.where(y_even, left, right)[at, :]
    spare = jnp.zeros((1, 128), jnp.float32)
    for c in range(3):
        far = dot3(pick[...], linear[c], NT)
        far = jnp.concatenate([far, jnp.zeros((8, 128 - rows), jnp.float32)], axis=1)
        ya[Y_FAR + c : Y_FAR + c + 1, :] = jnp.where(y_even, far[0:1, :], far[1:2, :])
        yb[Y_FAR + c : Y_FAR + c + 1, :] = jnp.where(y_even, far[1:2, :], far[0:1, :])
    for ref in (ya, yb):
        ref[5:6, :] = spare
        ref[Y_FILTER + 3 * Y_HALF : Y_MESSAGE, :] = jnp.zeros((2, 128), jnp.float32)
    middle = FIRST + Y_HALF
    lane_h = lax.broadcasted_iota(jnp.int32, (Y_HALF, 128), 1)
    for c in range(3):
        first, second = linear[c, FIRST:middle, :], linear[c, middle : middle + Y_HALF, :]
        left = jnp.where(lane_h < 64, first, pltpu.roll(second, 64, 1))
        right = jnp.where(lane_h < 64, pltpu.roll(first, 64, 1), second)
        at = slice(Y_FILTER + Y_HALF * c, Y_FILTER + Y_HALF * (c + 1))
        ya[at, :] = jnp.where(y_even, right, left)
        yb[at, :] = jnp.where(y_even, left, right)


def streamed(i, x):
    source = x - DIRS[i][0]
    return None if source < 0 else min(source, 3)


INWARD = [i for i in range(19) if DIRS[i][2]]


def both_ghosts(sub, low, high):
    return jnp.where(sub < 4, low, high)


def assemble(tall, sa, sb, ya, yb, a_first):
    end = PAD + sa.shape[0]
    for out, source, a, b in (
        (slice(PAD, end), slice(0, sa.shape[0]), sa, sb),
        (slice(PAD - 2, PAD), slice(6, 8), ya, yb),
        (slice(end, end + 2), slice(0, 2), ya, yb),
    ):
        tall[0, out, :] = jnp.where(a_first, a[source, :], b[source, :])
        tall[1, out, :] = jnp.where(a_first, b[source, :], a[source, :])


def interior_kernel(
    nz, post, solidp, linear, sa, sb, ya, yb, wy, wg, post2, flow_own, ghost_own, own_right, own_left, tall
):
    rows = post.shape[2]
    top = rows - PAD
    kz = lax.axis_index("gz")
    ky = lax.axis_index("gy") * lax.axis_size("col") + lax.axis_index("col")
    y_even = lax.rem(ky, 2) == 0
    sub = lax.broadcasted_iota(jnp.int32, (8, 128), 0)

    def moved(i, value):
        return pltpu.roll(value, DIRS[i][1] % 128, 1) if DIRS[i][1] else value

    outside = ((sub < 4) & (kz == 0)) | ((sub >= 4) & (kz == nz - 1))
    for x in range(1, 4):
        solid = both_ghosts(sub, solidp[x, PAD - 1 : PAD + 7, :], solidp[x, top - 7 : top + 1, :]) > 0.5
        g = []
        for i in range(19):
            low, high, source = PAD - 1 - DIRS[i][2], top - 7 - DIRS[i][2], streamed(i, x)
            value = both_ghosts(sub, post[i, source, low : low + 8, :], post[i, source, high : high + 8, :])
            g.append(moved(i, value))
        p = collide(g, solid, INWARD)
        for i in INWARD:
            row, at = (PAD - 1, 0) if DIRS[i][2] == 1 else (top, 7)
            value = moved(i, jnp.where(outside, 0.0, p[i]))
            post2[i, x - 1, row : row + 1, :] = value[at : at + 1, :]

    def body(t, carry):
        row = pl.multiple_of(t * 8 + PAD, 8)
        for x in range(1, 4):
            solid = solidp[x, pl.ds(row, 8), :] > 0.5
            g = [moved(i, post[i, streamed(i, x), pl.ds(row - DIRS[i][2], 8), :]) for i in range(19)]
            p = collide(g, solid)
            for i in range(19):
                post2[i, x - 1, pl.ds(row, 8), :] = moved(i, p[i])
        return carry

    lax.fori_loop(0, rows // 8 - 2, body, 0, unroll=2)

    flow_own[...] = dot3(linear[0:3].reshape(3 * rows, 128), wy[0:128, :])
    flow_own[0:rows, :] += linear[3]
    for c in range(3):
        ghost_own[8 * c : 8 * c + 8, 0:rows] = dot3(wg[:, 0:128], linear[c], NT)
        ghost_own[8 * c : 8 * c + 8, rows:128] = jnp.zeros((8, 128 - rows), jnp.float32)
    assemble(tall, sa, sb, ya, yb, y_even)
    own_right[0:128, :] = jnp.transpose(tall[0])
    own_left[0:128, :] = jnp.transpose(tall[1])


def final_kernel(
    nz, post, solidp, post2, flow_own, ghost_own, own_right, own_left, meanrow, sa, sb, ya, yb, wy, wg,
    inflow, state_out,
    lhs, flow, inlet2, strip_left, strip_right, moving, still, ghost_moving, ghost_still,
    state, flow_out, tall, sems,
):
    height = state.shape[2]
    rows = height + 2 * PAD
    top = PAD + height
    kz = lax.axis_index("gz")
    ky = lax.axis_index("gy") * lax.axis_size("col") + lax.axis_index("col")
    y_even = lax.rem(ky, 2) == 0
    lane = lax.broadcasted_iota(jnp.int32, (8, 128), 1)
    sub = lax.broadcasted_iota(jnp.int32, (8, 128), 0)

    assemble(tall, sa, sb, ya, yb, jnp.logical_not(y_even))
    strip_left[0:128, 0:rows] = jnp.transpose(tall[0, 0:rows, :])
    strip_right[0:128, 0:rows] = jnp.transpose(tall[1, 0:rows, :])

    lane_h = lax.broadcasted_iota(jnp.int32, (Y_HALF, 128), 1)
    for c in range(3):
        at = slice(Y_FILTER + Y_HALF * c, Y_FILTER + Y_HALF * (c + 1))
        a, b = ya[at, :], yb[at, :]
        left, right = jnp.where(y_even, b, a), jnp.where(y_even, a, b)
        middle = rows * c + FIRST + Y_HALF
        lo, hi = slice(middle - Y_HALF, middle), slice(middle, middle + Y_HALF)
        lhs[lo, 0:128] = jnp.where(lane_h < 64, left, 0.0)
        lhs[hi, 0:128] = jnp.where(lane_h < 64, 0.0, left)
        lhs[lo, 128:256] = jnp.where(lane_h < 64, right, 0.0)
        lhs[hi, 128:256] = jnp.where(lane_h < 64, 0.0, right)
    flow[...] = flow_own[...] + dot3(lhs[...], wy[128:384, :])
    for c in range(3):
        flow_out[c] = flow[rows * c + PAD : rows * c + top, :]
    flow_copy = pltpu.make_async_copy(flow_out, inflow, sems.at[height // 8])
    flow_copy.start()
    b_end = float(taps()[0])
    column_flow = []
    for c in range(3):
        g = dot3(wg[:, 128:384], lhs[rows * c : rows * (c + 1), :], NT)
        g = jnp.concatenate([g, jnp.zeros((8, 128 - rows), jnp.float32)], axis=1)
        g = g + ghost_own[8 * c : 8 * c + 8, :]
        far = slice(Y_FAR + c, Y_FAR + c + 1)
        at = [g[n : n + 1, :] for n in range(4)]
        at[0] = at[0] + b_end * jnp.where(y_even, yb[far, :], ya[far, :])
        at[3] = at[3] + b_end * jnp.where(y_even, ya[far, :], yb[far, :])
        if c == 0:
            at = [v + meanrow[0:1, :] for v in at]
        column_flow.append(at)

    outside = ((lane < PAD) & (kz == 0)) | ((lane >= top) & (kz == nz - 1))
    sources = (
        ((strip_left, 0), (strip_left, 0), (own_left, 0)),
        ((own_left, 1), (strip_left, 1), (own_left, 1)),
        ((own_right, 0), (own_right, 0), (strip_right, 0)),
        ((strip_right, 1), (own_right, 1), (strip_right, 1)),
    )
    for column in range(4):
        def rows_of(start):
            return pl.ds(start, 8, stride=2)

        src, odd = sources[column][0]
        solid = src[rows_of(2 * FLAG_PLANE + odd), :] > 0.5
        g = [None] * 19
        for i in range(19):
            cx, cy, cz = DIRS[i]
            src, odd = sources[column][cy % 3]
            if cy == 0:
                start = 8 * Y_FLAT.index(i) + odd
            else:
                start = LANE_PLUS + 8 * Y_PLUS.index(i if cy == 1 else MIRROR_Y[i]) + odd
            v = src[rows_of(start - 2 * cx), :]
            if cx == 1:
                v = jnp.where(sub == 0, 0.0, v)
            elif cx == -1:
                v = jnp.where(sub == 3, src[rows_of(start), :], v)
            g[i] = v if cz == 0 else pltpu.roll(v, cz % 128, 1)
        us = [INLET * jnp.broadcast_to(column_flow[c][column], (8, 128)) for c in range(3)]
        eq = inlet_state(*us)
        put = (sub == 0) & jnp.logical_not(solid)
        moves = 1 if column < 2 else -1
        keep = [i for i in range(19) if DIRS[i][1] == moves or (DIRS[i][1] == 0 and column in (1, 2))]
        p = collide(g, solid, keep)
        for i in keep:
            value = jnp.where(outside, 0.0, jnp.where(put, eq[i], p[i]))[0:4, :]
            if DIRS[i][1]:
                n = Y_PLUS.index(i if moves == 1 else MIRROR_Y[i])
                moving[pl.ds(16 * n + (column + 2) % 4, 4, stride=4), :] = value
            else:
                still[pl.ds(8 * Y_FLAT.index(i) + 2 - column, 4, stride=2), :] = value
    ghost_moving[:, 0:80] = jnp.transpose(moving[0:80, :])
    ghost_still[:, 0:72] = jnp.transpose(still[0:72, :])

    def inlet_values(us, solid, planes, load):
        eq = inlet_state(*[INLET * u for u in us])
        for i in planes:
            j = OPP[i]
            source = streamed(j, 0)
            bounced = 0.0 if source is None else moved(j, load(j, source))
            yield i, jnp.where(solid, bounced, eq[i])

    def moved(i, value):
        return pltpu.roll(value, DIRS[i][1] % 128, 1) if DIRS[i][1] else value

    def inlet(row):
        us = [flow[pl.ds(rows * c + row, 8), :] for c in range(3)]
        solid = solidp[0, pl.ds(row, 8), :] > 0.5
        load = lambda j, source: post[j, source, pl.ds(row - DIRS[j][2], 8), :]
        for i, value in inlet_values(us, solid, range(19), load):
            inlet2[i, pl.ds(row, 8), :] = moved(i, value)

    def inlet_ghosts():
        low, high = PAD - 1, top - 7

        def both(ref, shift, *lead):
            low_at, high_at = slice(low + shift, low + shift + 8), slice(high + shift, high + shift + 8)
            return both_ghosts(sub, ref[(*lead, low_at)], ref[(*lead, high_at)])

        us = [both(flow, rows * c) for c in range(3)]
        solid = both(solidp, 0, 0) > 0.5
        load = lambda j, source: both(post, -DIRS[j][2], j, source)
        beyond = ((sub < 4) & (kz == 0)) | ((sub >= 4) & (kz == nz - 1))
        for i, value in inlet_values(us, solid, INWARD, load):
            row, at = (PAD - 1, 0) if DIRS[i][2] == 1 else (top, 7)
            value = moved(i, jnp.where(beyond, 0.0, value))
            inlet2[i, row : row + 1, :] = value[at : at + 1, :]

    def out_copy(t):
        at = pl.ds(pl.multiple_of(t * 8, 8), 8)
        return pltpu.make_async_copy(state.at[:, :, at, :], state_out.at[:, :, at, :], sems.at[t])

    def last(t):
        row = pl.multiple_of(t * 8 + PAD, 8)
        us = [INLET * flow[pl.ds(rows * c + row, 8), :] for c in range(3)]
        eq = inlet_state(*us)
        solid = solidp[0, pl.ds(row, 8), :] > 0.5
        ends = (lane == 0) | (lane == 127)

        def read(i, source, ghost):
            at = pl.ds(row - DIRS[i][2], 8)
            v = inlet2[i, at, :] if source == 0 else post2[i, source - 1, at, :]
            where = ends if DIRS[i][1] == 0 else (lane < 2 if DIRS[i][1] == 1 else lane >= 126)
            return jnp.where(where, ghost, v)

        def write(i, x, value):
            if x == 0:
                value = jnp.where(solid, value, eq[i])
            state[i, x, pl.ds(row - PAD, 8), :] = value

        for i in Y_FLAT + Y_PLUS:
            both = [i] if DIRS[i][1] == 0 else [i, MIRROR_Y[i]]
            at = pl.ds(row - DIRS[i][2], 8)
            for source in range(4):
                targets = [x for x in range(4) if streamed(i, x) == source]
                if not targets:
                    continue
                if DIRS[i][1] == 0:
                    slot = 2 * (4 * Y_FLAT.index(i) + source)
                    ghost = pltpu.roll(ghost_still[at, :], (127 - slot) % 128, 1)
                else:
                    slot = 4 * (4 * Y_PLUS.index(i) + source)
                    ghost = pltpu.roll(ghost_moving[at, :], (126 - slot) % 128, 1)
                for j in both:
                    value = read(j, source, ghost)
                    for x in targets:
                        write(j, x, value)
            for j in both:
                if streamed(j, 0) is None:
                    write(j, 0, jnp.zeros((8, 128), jnp.float32))
        out_copy(t).start()

    inlet_ghosts()
    inlet(PAD)

    def main(t, carry):
        inlet(pl.multiple_of(t * 8 + PAD, 8))
        last(t - 1)
        return carry

    tiles = height // 8
    lax.fori_loop(1, tiles, main, 0)
    last(tiles - 1)
    for t in range(tiles):
        out_copy(t).wait()
    flow_copy.wait()


def swap_pairs(count, phase, distance=1):
    pairs = []
    for i in range(count):
        block = (i + phase * distance) // distance
        j = i + distance if block % 2 == 0 else i - distance
        if 0 <= j < count:
            pairs.append((i, j))
    return pairs


def ring_pairs(count, phase):
    if phase == 0:
        return [(i, i ^ 1) for i in range(count)]
    return [(i, (((i + 1) % count ^ 1) - 1) % count) for i in range(count)]


def vm(n):
    return [pl.BlockSpec(memory_space=pltpu.VMEM)] * n


def hbm(n):
    return [pl.BlockSpec(memory_space=pltpu.HBM)] * n


def f32(*shape):
    return jax.ShapeDtypeStruct(shape, jnp.float32)


def scratch(*shape):
    return pltpu.VMEM(shape, jnp.float32)


def flags(*shape):
    return pltpu.VMEM(shape, jnp.int32)


def params(mib):
    return pltpu.CompilerParams(vmem_limit_bytes=mib * 1024 * 1024)


def cost(flops, size):
    return pl.CostEstimate(flops=flops, bytes_accessed=size, transcendentals=0)


def shards(nz, ny, noise, mean_profile, lund_diag, lund_off, populations, mask):
    height, span = noise.shape[1], noise.shape[2]
    rows = height + 2 * PAD
    message = ROW_NOISE + 3 * height
    dma = pltpu.SemaphoreType.DMA
    here = lambda value: pltpu.with_memory_space_constraint(value, pltpu.HBM)
    mean_profile = mean_profile.reshape(1, height)
    operands = populations, mask, noise, mean_profile, lund_diag, lund_off

    za, zb = pl.pallas_call(
        lambda *refs: edge_kernel(nz, *refs),
        out_shape=(f32(message, 128), f32(message, 128)),
        in_specs=hbm(6),
        out_specs=vm(2),
        scratch_shapes=[
            scratch(19, 4, 16, 128), flags(4, 16, 128), scratch(1, height), scratch(3, height),
            scratch(3, height), scratch(20 * 4 * 16, 128), dma((13,)),
        ],
        compiler_params=params(8),
        name="edge_rows",
    )(*map(here, operands))

    z2 = pl.pallas_call(
        lambda *refs: far_kernel(height, *refs),
        out_shape=f32(16, 128),
        in_specs=vm(1),
        out_specs=pl.BlockSpec(memory_space=pltpu.VMEM),
        compiler_params=params(1),
        name="far_rows",
    )(za)

    ra = lax.ppermute(za, "gz", swap_pairs(nz, 0))
    rb = lax.ppermute(zb, "gz", swap_pairs(nz, 1))
    rc = lax.ppermute(z2, "gz", swap_pairs(nz, 0, 2))
    far = swap_pairs(nz, 1, 2)
    rd = lax.ppermute(z2, "gz", far) if far else jnp.zeros_like(z2)

    post, solidp, sa, sb = pl.pallas_call(
        lambda *refs: bulk_kernel(nz, *refs),
        out_shape=(f32(19, 4, rows, 128), f32(4, rows, 128), f32(height, 128), f32(height, 128)),
        in_specs=vm(2),
        out_specs=vm(4),
        compiler_params=params(4),
        cost_estimate=cost(4_000_000_000, 8_000_000),
        name="bulk",
    )(populations, mask)

    pa = lax.ppermute(sa, ("gy", "col"), ring_pairs(ny, 0))
    pb = lax.ppermute(sb, ("gy", "col"), ring_pairs(ny, 1))
    pick = np.zeros((8, 128), np.float32)
    pick[0, span - HW - 1] = pick[1, HW] = 1.0

    line = np.arange(rows) - PAD
    used = (line >= -1) & (line <= height)
    bandz = np.where(used[:, None], band(np.arange(-height, 2 * height), line).T, 0.0)
    post, solidp, ya, yb, linear, meanrow = pl.pallas_call(
        lambda *refs: column_kernel(nz, *refs),
        out_shape=(
            f32(19, 4, rows, 128), f32(4, rows, 128), f32(Y_MESSAGE, 128), f32(Y_MESSAGE, 128),
            f32(4, rows, 128), f32(8, 128),
        ),
        in_specs=vm(9),
        out_specs=vm(6),
        scratch_shapes=[
            scratch(3 * height, 384), scratch(rows, 384), scratch(2, ROW_PARAM, 128),
        ],
        input_output_aliases={0: 0, 1: 1},
        compiler_params=params(4),
        name="columns",
    )(post, solidp, za, ra, rb, rc, rd, jnp.asarray(bandz, jnp.float32), jnp.asarray(pick))

    qa = lax.ppermute(ya, ("gy", "col"), ring_pairs(ny, 0))
    qb = lax.ppermute(yb, ("gy", "col"), ring_pairs(ny, 1))

    own = np.arange(span)
    left = np.arange(128) % 64 - 64
    right = np.arange(128) % 64 + span
    source = np.concatenate([own, left, right])
    wy = jnp.asarray(band(source, own))
    wg = np.zeros((8, 384), np.float32)
    wg[0:4] = band(source, np.array([-1, 0, span - 1, span])).T
    wg = jnp.asarray(wg)
    post2, flow_own, ghost_own, own_right, own_left = pl.pallas_call(
        lambda *refs: interior_kernel(nz, *refs),
        out_shape=(
            f32(19, 3, rows, 128), f32(3 * rows, 128), f32(24, 128), f32(144, 128), f32(144, 128),
        ),
        in_specs=vm(9),
        out_specs=vm(5),
        scratch_shapes=[scratch(2, 128, 128)],
        compiler_params=params(4),
        cost_estimate=cost(4_000_000_000, 8_000_000),
        name="interior",
    )(post, solidp, linear, sa, sb, ya, yb, wy, wg)
    inflow, state = pl.pallas_call(
        lambda *refs: final_kernel(nz, *refs),
        out_shape=(f32(3, height, span), f32(19, 4, height, span)),
        in_specs=vm(14),
        out_specs=hbm(2),
        scratch_shapes=[
            scratch(3 * rows, 256), scratch(3 * rows, 128), scratch(19, rows, 128),
            scratch(144, 128), scratch(144, 128), scratch(128, 128), scratch(128, 128),
            scratch(128, 128), scratch(128, 128), scratch(19, 4, height, span),
            scratch(3, height, span), scratch(2, 128, 128), dma((height // 8 + 1,)),
        ],
        compiler_params=params(8),
        name="stream",
    )(post, solidp, post2, flow_own, ghost_own, own_right, own_left, meanrow, pa, pb, qa, qb, wy, wg)
    return inflow, state


def solution(mesh):
    nz = mesh.shape["gz"]
    ny = mesh.shape["gy"] * mesh.shape["col"]
    in_specs = (
        P(None, "gz", ("gy", "col")),
        P("gz"),
        P(None, "gz"),
        P(None, "gz"),
        P(None, None, "gz", ("gy", "col")),
        P(None, "gz", ("gy", "col")),
    )
    out_specs = (P(None, "gz", ("gy", "col")), P(None, None, "gz", ("gy", "col")))

    def body(*args):
        return shards(nz, ny, *args)

    return jax.shard_map(body, mesh=mesh, in_specs=in_specs, out_specs=out_specs, check_vma=False)
```

```python
import math

import jax
import jax.numpy as jnp
import numpy as np
from jax import lax
from jax.experimental import pallas as pl
from jax.experimental.pallas import tpu as pltpu
from jax.sharding import PartitionSpec as P

HW = 64
DIRS = [
    (0, 0, 0),
    (1, 0, 0), (-1, 0, 0), (0, 1, 0), (0, -1, 0), (0, 0, 1), (0, 0, -1),
    (1, 1, 0), (-1, -1, 0), (1, -1, 0), (-1, 1, 0),
    (1, 0, 1), (-1, 0, -1), (1, 0, -1), (-1, 0, 1),
    (0, 1, 1), (0, -1, -1), (0, 1, -1), (0, -1, 1),
]
OPP = [DIRS.index((-a, -b, -c)) for a, b, c in DIRS]
MIRROR_Y = [DIRS.index((a, -b, c)) for a, b, c in DIRS]
MIRROR_Z = [DIRS.index((a, b, -c)) for a, b, c in DIRS]
INLET = 0.05

Z_EDGE = [i for i in range(19) if DIRS[i][2] == 0] + [i for i in range(19) if DIRS[i][2] == 1]
Z_SECOND = [i for i in range(19) if DIRS[i][2] == 1]
Y_FLAT = [i for i in range(19) if DIRS[i][1] == 0]
Y_PLUS = [i for i in range(19) if DIRS[i][1] == 1]
FLAG_PLANE = 4 * len(Y_FLAT)
LANE_PLUS = 2 * FLAG_PLANE + 8

ROW_SOLID = 76
ROW_PARAM = 80
ROW_NOISE = 88
PAD = 8
FIRST = PAD - 2
Y_HALF = 34
Y_FAR = 2
Y_FILTER = 8
Y_MESSAGE = 112


def taps():
    k = np.arange(-HW, HW + 1).astype(np.float64)
    raw = np.exp(-math.pi * k * k / (2.0 * (HW // 2) ** 2))
    return raw / np.sqrt(np.sum(raw * raw))


def band(source, target):
    values = taps()
    offset = np.asarray(source)[:, None] - np.asarray(target)[None, :]
    inside = np.abs(offset) <= HW
    return np.where(inside, values[np.clip(offset + HW, 0, 2 * HW)], 0.0).astype(np.float32)


def moments(g):
    s = {a: g[a] + g[a + 1] for a in range(1, 19, 2)}
    d = {a: g[a] - g[a + 1] for a in range(1, 19, 2)}
    w1, w2 = 1.0 / 18.0, 1.0 / 36.0
    rho = (
        g[0] * (1.0 / 3.0)
        + (s[1] + s[3] + s[5]) * w1
        + ((s[7] + s[9]) + (s[11] + s[13]) + (s[15] + s[17])) * w2
    )
    mx = d[1] * w1 + ((d[7] + d[9]) + (d[11] + d[13])) * w2
    my = d[3] * w1 + ((d[7] - d[9]) + (d[15] + d[17])) * w2
    mz = d[5] * w1 + ((d[11] - d[13]) + (d[15] - d[17])) * w2
    return rho, mx, my, mz


def pair_vector(a, vx, vy, vz):
    total = None
    for c, v in zip(DIRS[a], (vx, vy, vz)):
        if c:
            term = v if c > 0 else -v
            total = term if total is None else (total + v if c > 0 else total - v)
    return total


def collide(g, solid, keep=range(19)):
    rho, mx, my, mz = moments(g)
    inv = 1.0 / rho
    ux, uy, uz = mx * inv, my * inv, mz * inv
    square = mx * ux + my * uy + mz * uz
    base = 1.25 * rho - 1.875 * square
    post = [None] * 19
    if 0 in keep:
        post[0] = jnp.where(solid, g[0], base - 0.25 * g[0])
    for a in range(1, 19, 2):
        if a not in keep and a + 1 not in keep:
            continue
        m = pair_vector(a, mx, my, mz)
        p = pair_vector(a, ux, uy, uz)
        even = base + 5.625 * (m * p)
        odd = 3.75 * m
        if a in keep:
            post[a] = jnp.where(solid, g[a + 1], (even + odd) - 0.25 * g[a])
        if a + 1 in keep:
            post[a + 1] = jnp.where(solid, g[a], (even - odd) - 0.25 * g[a + 1])
    return post


def inlet_state(ux, uy, uz):
    base = 1.0 - 1.5 * (ux * ux + uy * uy + uz * uz)
    out = [base] * 19
    for a in range(1, 19, 2):
        p = pair_vector(a, ux, uy, uz)
        even = base + 4.5 * (p * p)
        odd = 3.0 * p
        out[a] = even + odd
        out[a + 1] = even - odd
    return out


def wall_rows(first_row, height, kz, nz):
    rows = lax.broadcasted_iota(jnp.int32, (8, 128), 0) + first_row
    return ((rows == 0) & (kz == 0)) | ((rows == height - 1) & (kz == nz - 1))


def edge_kernel(
    nz, pops, mask, noise, mean, diag, off, za, zb, raw, flags, mean_v, diag_v, off_v, edge, sems
):
    height = pops.shape[2]
    kz = lax.axis_index("gz")
    upward = lax.rem(kz, 2) == 0
    upper = pl.ds(height - 8, 8)
    copies = [
        (pops.at[:, :, 0:8, :], raw.at[:, :, 0:8, :]),
        (pops.at[:, :, upper, :], raw.at[:, :, 8:16, :]),
        (mask.at[:, 0:8, :], flags.at[:, 0:8, :]),
        (mask.at[:, upper, :], flags.at[:, 8:16, :]),
        (mean, mean_v),
        (diag, diag_v),
        (off, off_v),
    ]
    for c in range(3):
        at = slice(ROW_NOISE + height * c, ROW_NOISE + height * (c + 1))
        copies.append((noise.at[c], za.at[at, :]))
        copies.append((noise.at[c], zb.at[at, :]))
    copies = [pltpu.make_async_copy(src, dst, sems.at[n]) for n, (src, dst) in enumerate(copies)]
    for copy in copies:
        copy.start()
    for part, row in ((0, 0), (1, height - 8)):
        copies[part].wait()
        copies[2 + part].wait()
        wall = wall_rows(row, height, kz, nz)
        at = slice(8 * part, 8 * part + 8)
        for x in range(4):
            solid = (flags[x, at, :] == 1) | wall
            post = collide([raw[i, x, at, :] for i in range(19)], solid)
            post.append(solid.astype(jnp.float32))
            for i in range(20):
                edge[64 * i + 16 * x + 8 * part : 64 * i + 16 * x + 8 * part + 8, :] = post[i]

    def put(q, i, depth):
        up = edge[pl.ds(64 * i + 15 - depth, 4, stride=16), :]
        down = edge[pl.ds(64 * (i if i == 19 else MIRROR_Z[i]) + depth, 4, stride=16), :]
        za[4 * q : 4 * q + 4, :] = jnp.where(upward, up, down)
        zb[4 * q : 4 * q + 4, :] = jnp.where(upward, down, up)

    for q, i in enumerate(Z_EDGE + Z_SECOND + [19]):
        put(q, i, 1 if len(Z_EDGE) <= q < 19 else 0)
    for copy in copies[4:]:
        copy.wait()
    for ref in (za, zb):
        ref[ROW_PARAM : ROW_PARAM + 8, :] = jnp.zeros((8, 128), jnp.float32)
        ref[ROW_PARAM : ROW_PARAM + 1, 0:height] = mean_v[...]
        ref[ROW_PARAM + 1 : ROW_PARAM + 4, 0:height] = diag_v[...]
        ref[ROW_PARAM + 4 : ROW_PARAM + 7, 0:height] = off_v[...]


def far_kernel(height, za, z2):
    kz = lax.axis_index("gz")
    low_half = lax.rem(kz, 4) < 2
    z2[...] = jnp.zeros((16, 128), jnp.float32)
    for c in range(3):
        base = ROW_NOISE + height * c
        last = za[base + height - 1 : base + height, :]
        first = za[base : base + 1, :]
        z2[c : c + 1, :] = jnp.where(low_half, last, first)
        z2[8 + c : 9 + c, :] = jnp.where(low_half, first, last)


def dot3(a, b, dims=(((1,), (0,)), ((), ()))):
    a_hi, b_hi = a.astype(jnp.bfloat16), b.astype(jnp.bfloat16)
    a_lo = (a - a_hi.astype(jnp.float32)).astype(jnp.bfloat16)
    b_lo = (b - b_hi.astype(jnp.float32)).astype(jnp.bfloat16)

    def dot(u, v):
        return lax.dot_general(u, v, dims, preferred_element_type=jnp.float32)

    return dot(a_hi, b_hi) + (dot(a_lo, b_hi) + dot(a_hi, b_lo))


NT = (((1,), (1,)), ((), ()))


def put_pair(pair, slot, value, first_column, into):
    return jnp.where(pair == slot, pltpu.roll(value, (2 * slot - first_column) % 128, 1), into)


def bulk_kernel(nz, pops, mask, post, solidp, ya, yb):
    height = pops.shape[2]
    kz = lax.axis_index("gz")
    ky = lax.axis_index("gy") * lax.axis_size("col") + lax.axis_index("col")
    y_even = lax.rem(ky, 2) == 0
    pair = lax.broadcasted_iota(jnp.int32, (8, 128), 1) // 2

    def body(t, carry):
        row = pl.multiple_of(t * 8, 8)
        out = pl.ds(row + PAD, 8)
        wall = wall_rows(row, height, kz, nz)
        flat = right = left = jnp.zeros((8, 128), jnp.float32)
        for x in range(4):
            solid = (mask[x, pl.ds(row, 8), :] == 1) | wall
            p = collide([pops[i, x, pl.ds(row, 8), :] for i in range(19)], solid)
            flag = solid.astype(jnp.float32)
            solidp[x, out, :] = flag
            flat = put_pair(pair, FLAG_PLANE + x, flag, 127, flat)
            for q, i in enumerate(Y_FLAT):
                post[i, x, out, :] = p[i]
                flat = put_pair(pair, 4 * q + x, p[i], 127, flat)
            for n, i in enumerate(Y_PLUS):
                j = MIRROR_Y[i]
                slot = LANE_PLUS // 2 + 4 * n + x
                post[i, x, out, :] = pltpu.roll(p[i], 1, 1)
                post[j, x, out, :] = pltpu.roll(p[j], 127, 1)
                right = put_pair(pair, slot, p[i], 126, right)
                left = put_pair(pair, slot, p[j], 0, left)
        right = jnp.where(pair < LANE_PLUS // 2, flat, right)
        left = jnp.where(pair < LANE_PLUS // 2, flat, left)
        ya[pl.ds(row, 8), :] = jnp.where(y_even, right, left)
        yb[pl.ds(row, 8), :] = jnp.where(y_even, left, right)
        return carry

    lax.fori_loop(0, height // 8, body, 0, unroll=2)


def column_kernel(
    nz, post_in, solid_in, sent, za, zb, z2c, z2d, bandz, pick,
    post, solidp, ya, yb, linear, meanrow,
    wide, filt, moved,
):
    height = post.shape[2] - 2 * PAD
    rows = height + 2 * PAD
    kz = lax.axis_index("gz")
    ky = lax.axis_index("gy") * lax.axis_size("col") + lax.axis_index("col")
    z_even = lax.rem(kz, 2) == 0
    y_even = lax.rem(ky, 2) == 0
    low_half = lax.rem(kz, 4) < 2

    def below(row, n=1):
        return jnp.where(z_even, zb[row : row + n, :], za[row : row + n, :])

    def above(row, n=1):
        return jnp.where(z_even, za[row : row + n, :], zb[row : row + n, :])

    top = PAD + height
    low, high = below(0, ROW_PARAM), above(0, ROW_PARAM)
    for n, shift in enumerate((0, 1, 127)):
        moved[n, 0] = low if shift == 0 else pltpu.roll(low, shift, 1)
        moved[n, 1] = high if shift == 0 else pltpu.roll(high, shift, 1)
    for items, first, depth in ((Z_EDGE, 0, 0), (Z_SECOND, len(Z_EDGE), 1)):
        for q, i in enumerate(items):
            n = DIRS[i][1] % 3
            for x in range(4):
                at = slice(4 * (first + q) + x, 4 * (first + q) + x + 1)
                post[i, x, PAD - 1 - depth : PAD - depth, :] = moved[n, 0, at, :]
                post[MIRROR_Z[i], x, top + depth : top + depth + 1, :] = moved[n, 1, at, :]
    for x in range(4):
        solidp[x, PAD - 1 : PAD, :] = moved[0, 0, ROW_SOLID + x : ROW_SOLID + x + 1, :]
        solidp[x, top : top + 1, :] = moved[0, 1, ROW_SOLID + x : ROW_SOLID + x + 1, :]

    lane = lax.broadcasted_iota(jnp.int32, (8, 128), 1)
    own_par = pltpu.roll(sent[ROW_PARAM : ROW_PARAM + 8, :], PAD, 1)
    low_par = pltpu.roll(below(ROW_PARAM, 8), 128 - height + PAD, 1)
    high_par = pltpu.roll(above(ROW_PARAM, 8), height + PAD, 1)
    par = jnp.where(lane < PAD, low_par, jnp.where(lane < top, own_par, high_par))
    par = jnp.where(lane < rows, par, 0.0)
    meanrow[...] = par
    cols = jnp.transpose(jnp.concatenate([par] * 16, axis=0))[0:rows]

    for c in range(3):
        lanes = slice(128 * c, 128 * c + 128)
        at = slice(ROW_NOISE + height * c, ROW_NOISE + height * (c + 1))
        wide[0:height, lanes] = below(ROW_NOISE + height * c, height)
        wide[height : 2 * height, lanes] = sent[at, :]
        wide[2 * height : 3 * height, lanes] = above(ROW_NOISE + height * c, height)
    filt[...] = dot3(bandz[...], wide[...])
    b_end = float(taps()[0])
    far_low = jnp.where(low_half, z2d[8:16, :], z2c[0:8, :])
    far_high = jnp.where(low_half, z2c[0:8, :], z2d[8:16, :])
    for c in range(3):
        lanes = slice(128 * c, 128 * c + 128)
        filt[PAD - 1 : PAD, lanes] += b_end * far_low[c : c + 1, :]
        filt[top : top + 1, lanes] += b_end * far_high[c : c + 1, :]
    f0, f1, f2 = (filt[:, 128 * c : 128 * c + 128] for c in range(3))
    linear[0] = cols[:, 1:2] * f0
    linear[1] = cols[:, 4:5] * f0 + cols[:, 2:3] * f1
    linear[2] = cols[:, 5:6] * f0 + cols[:, 6:7] * f1 + cols[:, 3:4] * f2
    linear[3] = jnp.broadcast_to(cols[:, 0:1], (rows, 128))

    pair = lane // 2
    for row in (0, rows - 8):
        out = slice(row, row + 8)
        flat = right = left = jnp.zeros((8, 128), jnp.float32)
        for x in range(4):
            flat = put_pair(pair, FLAG_PLANE + x, solidp[x, out, :], 127, flat)
            for q, i in enumerate(Y_FLAT):
                flat = put_pair(pair, 4 * q + x, post[i, x, out, :], 127, flat)
            for n, i in enumerate(Y_PLUS):
                slot = LANE_PLUS // 2 + 4 * n + x
                right = put_pair(pair, slot, post[i, x, out, :], 127, right)
                left = put_pair(pair, slot, post[MIRROR_Y[i], x, out, :], 127, left)
        right = jnp.where(pair < LANE_PLUS // 2, flat, right)
        left = jnp.where(pair < LANE_PLUS // 2, flat, left)
        at = slice(0, 2) if row else slice(6, 8)
        ya[at, :] = jnp.where(y_even, right, left)[at, :]
        yb[at, :] = jnp.where(y_even, left, right)[at, :]
    spare = jnp.zeros((1, 128), jnp.float32)
    for c in range(3):
        far = dot3(pick[...], linear[c], NT)
        far = jnp.concatenate([far, jnp.zeros((8, 128 - rows), jnp.float32)], axis=1)
        ya[Y_FAR + c : Y_FAR + c + 1, :] = jnp.where(y_even, far[0:1, :], far[1:2, :])
        yb[Y_FAR + c : Y_FAR + c + 1, :] = jnp.where(y_even, far[1:2, :], far[0:1, :])
    for ref in (ya, yb):
        ref[5:6, :] = spare
        ref[Y_FILTER + 3 * Y_HALF : Y_MESSAGE, :] = jnp.zeros((2, 128), jnp.float32)
    middle = FIRST + Y_HALF
    lane_h = lax.broadcasted_iota(jnp.int32, (Y_HALF, 128), 1)
    for c in range(3):
        first, second = linear[c, FIRST:middle, :], linear[c, middle : middle + Y_HALF, :]
        left = jnp.where(lane_h < 64, first, pltpu.roll(second, 64, 1))
        right = jnp.where(lane_h < 64, pltpu.roll(first, 64, 1), second)
        at = slice(Y_FILTER + Y_HALF * c, Y_FILTER + Y_HALF * (c + 1))
        ya[at, :] = jnp.where(y_even, right, left)
        yb[at, :] = jnp.where(y_even, left, right)


def streamed(i, x):
    source = x - DIRS[i][0]
    return None if source < 0 else min(source, 3)


INWARD = [i for i in range(19) if DIRS[i][2]]


def both_ghosts(sub, low, high):
    return jnp.where(sub < 4, low, high)


def assemble(tall, sa, sb, ya, yb, a_first):
    end = PAD + sa.shape[0]
    for out, source, a, b in (
        (slice(PAD, end), slice(0, sa.shape[0]), sa, sb),
        (slice(PAD - 2, PAD), slice(6, 8), ya, yb),
        (slice(end, end + 2), slice(0, 2), ya, yb),
    ):
        tall[0, out, :] = jnp.where(a_first, a[source, :], b[source, :])
        tall[1, out, :] = jnp.where(a_first, b[source, :], a[source, :])


def interior_kernel(
    nz, post, solidp, linear, sa, sb, ya, yb, wy, wg, post2, flow_own, ghost_own, own_right, own_left, tall
):
    rows = post.shape[2]
    top = rows - PAD
    kz = lax.axis_index("gz")
    ky = lax.axis_index("gy") * lax.axis_size("col") + lax.axis_index("col")
    y_even = lax.rem(ky, 2) == 0
    sub = lax.broadcasted_iota(jnp.int32, (8, 128), 0)

    def moved(i, value):
        return pltpu.roll(value, DIRS[i][1] % 128, 1) if DIRS[i][1] else value

    outside = ((sub < 4) & (kz == 0)) | ((sub >= 4) & (kz == nz - 1))
    for x in range(1, 4):
        solid = both_ghosts(sub, solidp[x, PAD - 1 : PAD + 7, :], solidp[x, top - 7 : top + 1, :]) > 0.5
        g = []
        for i in range(19):
            low, high, source = PAD - 1 - DIRS[i][2], top - 7 - DIRS[i][2], streamed(i, x)
            g.append(both_ghosts(sub, post[i, source, low : low + 8, :], post[i, source, high : high + 8, :]))
        p = collide(g, solid, INWARD)
        for i in INWARD:
            row, at = (PAD - 1, 0) if DIRS[i][2] == 1 else (top, 7)
            value = moved(i, jnp.where(outside, 0.0, p[i]))
            post2[i, x - 1, row : row + 1, :] = value[at : at + 1, :]

    def body(t, carry):
        row = pl.multiple_of(t * 8 + PAD, 8)
        for x in range(1, 4):
            solid = solidp[x, pl.ds(row, 8), :] > 0.5
            g = [post[i, streamed(i, x), pl.ds(row - DIRS[i][2], 8), :] for i in range(19)]
            p = collide(g, solid)
            for i in range(19):
                post2[i, x - 1, pl.ds(row, 8), :] = moved(i, p[i])
        return carry

    lax.fori_loop(0, rows // 8 - 2, body, 0, unroll=2)

    flow_own[...] = dot3(linear[0:3].reshape(3 * rows, 128), wy[0:128, :])
    flow_own[0:rows, :] += linear[3]
    for c in range(3):
        ghost_own[8 * c : 8 * c + 8, 0:rows] = dot3(wg[:, 0:128], linear[c], NT)
        ghost_own[8 * c : 8 * c + 8, rows:128] = jnp.zeros((8, 128 - rows), jnp.float32)
    assemble(tall, sa, sb, ya, yb, y_even)
    own_right[0:128, :] = jnp.transpose(tall[0])
    own_left[0:128, :] = jnp.transpose(tall[1])


def final_kernel(
    nz, post, solidp, post2, flow_own, ghost_own, own_right, own_left, meanrow, sa, sb, ya, yb, wy, wg,
    inflow, state_out,
    lhs, flow, inlet2, strip_left, strip_right, moving, still, ghost_moving, ghost_still,
    state, flow_out, tall, sems,
):
    height = state.shape[2]
    rows = height + 2 * PAD
    top = PAD + height
    kz = lax.axis_index("gz")
    ky = lax.axis_index("gy") * lax.axis_size("col") + lax.axis_index("col")
    y_even = lax.rem(ky, 2) == 0
    lane = lax.broadcasted_iota(jnp.int32, (8, 128), 1)
    sub = lax.broadcasted_iota(jnp.int32, (8, 128), 0)

    assemble(tall, sa, sb, ya, yb, jnp.logical_not(y_even))
    strip_left[0:128, 0:rows] = jnp.transpose(tall[0, 0:rows, :])
    strip_right[0:128, 0:rows] = jnp.transpose(tall[1, 0:rows, :])

    lane_h = lax.broadcasted_iota(jnp.int32, (Y_HALF, 128), 1)
    for c in range(3):
        at = slice(Y_FILTER + Y_HALF * c, Y_FILTER + Y_HALF * (c + 1))
        a, b = ya[at, :], yb[at, :]
        left, right = jnp.where(y_even, b, a), jnp.where(y_even, a, b)
        middle = rows * c + FIRST + Y_HALF
        lo, hi = slice(middle - Y_HALF, middle), slice(middle, middle + Y_HALF)
        lhs[lo, 0:128] = jnp.where(lane_h < 64, left, 0.0)
        lhs[hi, 0:128] = jnp.where(lane_h < 64, 0.0, left)
        lhs[lo, 128:256] = jnp.where(lane_h < 64, right, 0.0)
        lhs[hi, 128:256] = jnp.where(lane_h < 64, 0.0, right)
    flow[...] = flow_own[...] + dot3(lhs[...], wy[128:384, :])
    for c in range(3):
        flow_out[c] = flow[rows * c + PAD : rows * c + top, :]
    flow_copy = pltpu.make_async_copy(flow_out, inflow, sems.at[height // 8])
    flow_copy.start()
    b_end = float(taps()[0])
    column_flow = []
    for c in range(3):
        g = dot3(wg[:, 128:384], lhs[rows * c : rows * (c + 1), :], NT)
        g = jnp.concatenate([g, jnp.zeros((8, 128 - rows), jnp.float32)], axis=1)
        g = g + ghost_own[8 * c : 8 * c + 8, :]
        far = slice(Y_FAR + c, Y_FAR + c + 1)
        at = [g[n : n + 1, :] for n in range(4)]
        at[0] = at[0] + b_end * jnp.where(y_even, yb[far, :], ya[far, :])
        at[3] = at[3] + b_end * jnp.where(y_even, ya[far, :], yb[far, :])
        if c == 0:
            at = [v + meanrow[0:1, :] for v in at]
        column_flow.append(at)

    outside = ((lane < PAD) & (kz == 0)) | ((lane >= top) & (kz == nz - 1))
    sources = (
        ((strip_left, 0), (strip_left, 0), (own_left, 0)),
        ((own_left, 1), (strip_left, 1), (own_left, 1)),
        ((own_right, 0), (own_right, 0), (strip_right, 0)),
        ((strip_right, 1), (own_right, 1), (strip_right, 1)),
    )
    for column in range(4):
        def rows_of(start):
            return pl.ds(start, 8, stride=2)

        src, odd = sources[column][0]
        solid = src[rows_of(2 * FLAG_PLANE + odd), :] > 0.5
        g = [None] * 19
        for i in range(19):
            cx, cy, cz = DIRS[i]
            src, odd = sources[column][cy % 3]
            if cy == 0:
                start = 8 * Y_FLAT.index(i) + odd
            else:
                start = LANE_PLUS + 8 * Y_PLUS.index(i if cy == 1 else MIRROR_Y[i]) + odd
            v = src[rows_of(start - 2 * cx), :]
            if cx == 1:
                v = jnp.where(sub == 0, 0.0, v)
            elif cx == -1:
                v = jnp.where(sub == 3, src[rows_of(start), :], v)
            g[i] = v if cz == 0 else pltpu.roll(v, cz % 128, 1)
        us = [INLET * jnp.broadcast_to(column_flow[c][column], (8, 128)) for c in range(3)]
        eq = inlet_state(*us)
        put = (sub == 0) & jnp.logical_not(solid)
        moves = 1 if column < 2 else -1
        keep = [i for i in range(19) if DIRS[i][1] == moves or (DIRS[i][1] == 0 and column in (1, 2))]
        p = collide(g, solid, keep)
        for i in keep:
            value = jnp.where(outside, 0.0, jnp.where(put, eq[i], p[i]))[0:4, :]
            if DIRS[i][1]:
                n = Y_PLUS.index(i if moves == 1 else MIRROR_Y[i])
                moving[pl.ds(16 * n + (column + 2) % 4, 4, stride=4), :] = value
            else:
                still[pl.ds(8 * Y_FLAT.index(i) + 2 - column, 4, stride=2), :] = value
    ghost_moving[:, 0:80] = jnp.transpose(moving[0:80, :])
    ghost_still[:, 0:72] = jnp.transpose(still[0:72, :])

    def inlet_values(us, solid, planes, load):
        eq = inlet_state(*[INLET * u for u in us])
        for i in planes:
            j = OPP[i]
            source = streamed(j, 0)
            bounced = 0.0 if source is None else load(j, source)
            yield i, jnp.where(solid, bounced, eq[i])

    def moved(i, value):
        return pltpu.roll(value, DIRS[i][1] % 128, 1) if DIRS[i][1] else value

    def inlet(row):
        us = [flow[pl.ds(rows * c + row, 8), :] for c in range(3)]
        solid = solidp[0, pl.ds(row, 8), :] > 0.5
        load = lambda j, source: post[j, source, pl.ds(row - DIRS[j][2], 8), :]
        for i, value in inlet_values(us, solid, range(19), load):
            inlet2[i, pl.ds(row, 8), :] = moved(i, value)

    def inlet_ghosts():
        low, high = PAD - 1, top - 7

        def both(ref, shift, *lead):
            low_at, high_at = slice(low + shift, low + shift + 8), slice(high + shift, high + shift + 8)
            return both_ghosts(sub, ref[(*lead, low_at)], ref[(*lead, high_at)])

        us = [both(flow, rows * c) for c in range(3)]
        solid = both(solidp, 0, 0) > 0.5
        load = lambda j, source: both(post, -DIRS[j][2], j, source)
        beyond = ((sub < 4) & (kz == 0)) | ((sub >= 4) & (kz == nz - 1))
        for i, value in inlet_values(us, solid, INWARD, load):
            row, at = (PAD - 1, 0) if DIRS[i][2] == 1 else (top, 7)
            value = moved(i, jnp.where(beyond, 0.0, value))
            inlet2[i, row : row + 1, :] = value[at : at + 1, :]

    def out_copy(t):
        at = pl.ds(pl.multiple_of(t * 8, 8), 8)
        return pltpu.make_async_copy(state.at[:, :, at, :], state_out.at[:, :, at, :], sems.at[t])

    def last(t):
        row = pl.multiple_of(t * 8 + PAD, 8)
        us = [INLET * flow[pl.ds(rows * c + row, 8), :] for c in range(3)]
        eq = inlet_state(*us)
        solid = solidp[0, pl.ds(row, 8), :] > 0.5
        ends = (lane == 0) | (lane == 127)

        def read(i, source, ghost):
            at = pl.ds(row - DIRS[i][2], 8)
            v = inlet2[i, at, :] if source == 0 else post2[i, source - 1, at, :]
            where = ends if DIRS[i][1] == 0 else (lane < 2 if DIRS[i][1] == 1 else lane >= 126)
            return jnp.where(where, ghost, v)

        def write(i, x, value):
            if x == 0:
                value = jnp.where(solid, value, eq[i])
            state[i, x, pl.ds(row - PAD, 8), :] = value

        for i in Y_FLAT + Y_PLUS:
            both = [i] if DIRS[i][1] == 0 else [i, MIRROR_Y[i]]
            at = pl.ds(row - DIRS[i][2], 8)
            for source in range(4):
                targets = [x for x in range(4) if streamed(i, x) == source]
                if not targets:
                    continue
                if DIRS[i][1] == 0:
                    slot = 2 * (4 * Y_FLAT.index(i) + source)
                    ghost = pltpu.roll(ghost_still[at, :], (127 - slot) % 128, 1)
                else:
                    slot = 4 * (4 * Y_PLUS.index(i) + source)
                    ghost = pltpu.roll(ghost_moving[at, :], (126 - slot) % 128, 1)
                for j in both:
                    value = read(j, source, ghost)
                    for x in targets:
                        write(j, x, value)
            for j in both:
                if streamed(j, 0) is None:
                    write(j, 0, jnp.zeros((8, 128), jnp.float32))
        out_copy(t).start()

    inlet_ghosts()
    inlet(PAD)

    def main(t, carry):
        inlet(pl.multiple_of(t * 8 + PAD, 8))
        last(t - 1)
        return carry

    tiles = height // 8
    lax.fori_loop(1, tiles, main, 0)
    last(tiles - 1)
    for t in range(tiles):
        out_copy(t).wait()
    flow_copy.wait()


def swap_pairs(count, phase, distance=1):
    pairs = []
    for i in range(count):
        block = (i + phase * distance) // distance
        j = i + distance if block % 2 == 0 else i - distance
        if 0 <= j < count:
            pairs.append((i, j))
    return pairs


def ring_pairs(count, phase):
    if phase == 0:
        return [(i, i ^ 1) for i in range(count)]
    return [(i, (((i + 1) % count ^ 1) - 1) % count) for i in range(count)]


def vm(n):
    return [pl.BlockSpec(memory_space=pltpu.VMEM)] * n


def hbm(n):
    return [pl.BlockSpec(memory_space=pltpu.HBM)] * n


def f32(*shape):
    return jax.ShapeDtypeStruct(shape, jnp.float32)


def scratch(*shape):
    return pltpu.VMEM(shape, jnp.float32)


def flags(*shape):
    return pltpu.VMEM(shape, jnp.int32)


def params(mib):
    return pltpu.CompilerParams(vmem_limit_bytes=mib * 1024 * 1024)


def cost(flops, size):
    return pl.CostEstimate(flops=flops, bytes_accessed=size, transcendentals=0)


def shards(nz, ny, noise, mean_profile, lund_diag, lund_off, populations, mask):
    height, span = noise.shape[1], noise.shape[2]
    rows = height + 2 * PAD
    message = ROW_NOISE + 3 * height
    dma = pltpu.SemaphoreType.DMA
    here = lambda value: pltpu.with_memory_space_constraint(value, pltpu.HBM)
    mean_profile = mean_profile.reshape(1, height)
    operands = populations, mask, noise, mean_profile, lund_diag, lund_off

    za, zb = pl.pallas_call(
        lambda *refs: edge_kernel(nz, *refs),
        out_shape=(f32(message, 128), f32(message, 128)),
        in_specs=hbm(6),
        out_specs=vm(2),
        scratch_shapes=[
            scratch(19, 4, 16, 128), flags(4, 16, 128), scratch(1, height), scratch(3, height),
            scratch(3, height), scratch(20 * 4 * 16, 128), dma((13,)),
        ],
        compiler_params=params(8),
        name="edge_rows",
    )(*map(here, operands))

    z2 = pl.pallas_call(
        lambda *refs: far_kernel(height, *refs),
        out_shape=f32(16, 128),
        in_specs=vm(1),
        out_specs=pl.BlockSpec(memory_space=pltpu.VMEM),
        compiler_params=params(1),
        name="far_rows",
    )(za)

    ra = lax.ppermute(za, "gz", swap_pairs(nz, 0))
    rb = lax.ppermute(zb, "gz", swap_pairs(nz, 1))
    rc = lax.ppermute(z2, "gz", swap_pairs(nz, 0, 2))
    far = swap_pairs(nz, 1, 2)
    rd = lax.ppermute(z2, "gz", far) if far else jnp.zeros_like(z2)

    post, solidp, sa, sb = pl.pallas_call(
        lambda *refs: bulk_kernel(nz, *refs),
        out_shape=(f32(19, 4, rows, 128), f32(4, rows, 128), f32(height, 128), f32(height, 128)),
        in_specs=vm(2),
        out_specs=vm(4),
        compiler_params=params(4),
        cost_estimate=cost(4_000_000_000, 8_000_000),
        name="bulk",
    )(populations, mask)

    pa = lax.ppermute(sa, ("gy", "col"), ring_pairs(ny, 0))
    pb = lax.ppermute(sb, ("gy", "col"), ring_pairs(ny, 1))
    pick = np.zeros((8, 128), np.float32)
    pick[0, span - HW - 1] = pick[1, HW] = 1.0

    line = np.arange(rows) - PAD
    used = (line >= -1) & (line <= height)
    bandz = np.where(used[:, None], band(np.arange(-height, 2 * height), line).T, 0.0)
    post, solidp, ya, yb, linear, meanrow = pl.pallas_call(
        lambda *refs: column_kernel(nz, *refs),
        out_shape=(
            f32(19, 4, rows, 128), f32(4, rows, 128), f32(Y_MESSAGE, 128), f32(Y_MESSAGE, 128),
            f32(4, rows, 128), f32(8, 128),
        ),
        in_specs=vm(9),
        out_specs=vm(6),
        scratch_shapes=[
            scratch(3 * height, 384), scratch(rows, 384), scratch(3, 2, ROW_PARAM, 128),
        ],
        input_output_aliases={0: 0, 1: 1},
        compiler_params=params(4),
        name="columns",
    )(post, solidp, za, ra, rb, rc, rd, jnp.asarray(bandz, jnp.float32), jnp.asarray(pick))

    qa = lax.ppermute(ya, ("gy", "col"), ring_pairs(ny, 0))
    qb = lax.ppermute(yb, ("gy", "col"), ring_pairs(ny, 1))

    own = np.arange(span)
    left = np.arange(128) % 64 - 64
    right = np.arange(128) % 64 + span
    source = np.concatenate([own, left, right])
    wy = jnp.asarray(band(source, own))
    wg = np.zeros((8, 384), np.float32)
    wg[0:4] = band(source, np.array([-1, 0, span - 1, span])).T
    wg = jnp.asarray(wg)
    post2, flow_own, ghost_own, own_right, own_left = pl.pallas_call(
        lambda *refs: interior_kernel(nz, *refs),
        out_shape=(
            f32(19, 3, rows, 128), f32(3 * rows, 128), f32(24, 128), f32(144, 128), f32(144, 128),
        ),
        in_specs=vm(9),
        out_specs=vm(5),
        scratch_shapes=[scratch(2, 128, 128)],
        compiler_params=params(4),
        cost_estimate=cost(4_000_000_000, 8_000_000),
        name="interior",
    )(post, solidp, linear, sa, sb, ya, yb, wy, wg)
    inflow, state = pl.pallas_call(
        lambda *refs: final_kernel(nz, *refs),
        out_shape=(f32(3, height, span), f32(19, 4, height, span)),
        in_specs=vm(14),
        out_specs=hbm(2),
        scratch_shapes=[
            scratch(3 * rows, 256), scratch(3 * rows, 128), scratch(19, rows, 128),
            scratch(144, 128), scratch(144, 128), scratch(128, 128), scratch(128, 128),
            scratch(128, 128), scratch(128, 128), scratch(19, 4, height, span),
            scratch(3, height, span), scratch(2, 128, 128), dma((height // 8 + 1,)),
        ],
        compiler_params=params(8),
        name="stream",
    )(post, solidp, post2, flow_own, ghost_own, own_right, own_left, meanrow, pa, pb, qa, qb, wy, wg)
    return inflow, state


def solution(mesh):
    nz = mesh.shape["gz"]
    ny = mesh.shape["gy"] * mesh.shape["col"]
    in_specs = (
        P(None, "gz", ("gy", "col")),
        P("gz"),
        P(None, "gz"),
        P(None, "gz"),
        P(None, None, "gz", ("gy", "col")),
        P(None, "gz", ("gy", "col")),
    )
    out_specs = (P(None, "gz", ("gy", "col")), P(None, None, "gz", ("gy", "col")))

    def body(*args):
        return shards(nz, ny, *args)

    return jax.shard_map(body, mesh=mesh, in_specs=in_specs, out_specs=out_specs, check_vma=False)
```

```python
import math

import jax
import jax.numpy as jnp
import numpy as np
from jax import lax
from jax.experimental import pallas as pl
from jax.experimental.pallas import tpu as pltpu
from jax.sharding import PartitionSpec as P

HW = 64
DIRS = [
    (0, 0, 0),
    (1, 0, 0), (-1, 0, 0), (0, 1, 0), (0, -1, 0), (0, 0, 1), (0, 0, -1),
    (1, 1, 0), (-1, -1, 0), (1, -1, 0), (-1, 1, 0),
    (1, 0, 1), (-1, 0, -1), (1, 0, -1), (-1, 0, 1),
    (0, 1, 1), (0, -1, -1), (0, 1, -1), (0, -1, 1),
]
OPP = [DIRS.index((-a, -b, -c)) for a, b, c in DIRS]
MIRROR_Y = [DIRS.index((a, -b, c)) for a, b, c in DIRS]
MIRROR_Z = [DIRS.index((a, b, -c)) for a, b, c in DIRS]
INLET = 0.05

Z_EDGE = [i for i in range(19) if DIRS[i][2] == 0] + [i for i in range(19) if DIRS[i][2] == 1]
Z_SECOND = [i for i in range(19) if DIRS[i][2] == 1]
Y_FLAT = [i for i in range(19) if DIRS[i][1] == 0]
Y_PLUS = [i for i in range(19) if DIRS[i][1] == 1]
FLAG_PLANE = 4 * len(Y_FLAT)
LANE_PLUS = 2 * FLAG_PLANE + 8

ROW_SOLID = 76
ROW_PARAM = 80
ROW_NOISE = 88
PAD = 8
FIRST = PAD - 2
Y_HALF = 34
Y_FAR = 2
Y_FILTER = 8
Y_MESSAGE = 112


def taps():
    k = np.arange(-HW, HW + 1).astype(np.float64)
    raw = np.exp(-math.pi * k * k / (2.0 * (HW // 2) ** 2))
    return raw / np.sqrt(np.sum(raw * raw))


def band(source, target):
    values = taps()
    offset = np.asarray(source)[:, None] - np.asarray(target)[None, :]
    inside = np.abs(offset) <= HW
    return np.where(inside, values[np.clip(offset + HW, 0, 2 * HW)], 0.0).astype(np.float32)


def moments(g):
    s = {a: g[a] + g[a + 1] for a in range(1, 19, 2)}
    d = {a: g[a] - g[a + 1] for a in range(1, 19, 2)}
    w1, w2 = 1.0 / 18.0, 1.0 / 36.0
    rho = (
        g[0] * (1.0 / 3.0)
        + (s[1] + s[3] + s[5]) * w1
        + ((s[7] + s[9]) + (s[11] + s[13]) + (s[15] + s[17])) * w2
    )
    mx = d[1] * w1 + ((d[7] + d[9]) + (d[11] + d[13])) * w2
    my = d[3] * w1 + ((d[7] - d[9]) + (d[15] + d[17])) * w2
    mz = d[5] * w1 + ((d[11] - d[13]) + (d[15] - d[17])) * w2
    return rho, mx, my, mz


def pair_vector(a, vx, vy, vz):
    total = None
    for c, v in zip(DIRS[a], (vx, vy, vz)):
        if c:
            term = v if c > 0 else -v
            total = term if total is None else (total + v if c > 0 else total - v)
    return total


def collide(g, solid, keep=range(19)):
    rho, mx, my, mz = moments(g)
    inv = 1.0 / rho
    ux, uy, uz = mx * inv, my * inv, mz * inv
    square = mx * ux + my * uy + mz * uz
    base = 1.25 * rho - 1.875 * square
    post = [None] * 19
    if 0 in keep:
        post[0] = jnp.where(solid, g[0], base - 0.25 * g[0])
    for a in range(1, 19, 2):
        if a not in keep and a + 1 not in keep:
            continue
        m = pair_vector(a, mx, my, mz)
        p = pair_vector(a, ux, uy, uz)
        even = base + 5.625 * (m * p)
        odd = 3.75 * m
        if a in keep:
            post[a] = jnp.where(solid, g[a + 1], (even + odd) - 0.25 * g[a])
        if a + 1 in keep:
            post[a + 1] = jnp.where(solid, g[a], (even - odd) - 0.25 * g[a + 1])
    return post


def inlet_state(ux, uy, uz):
    base = 1.0 - 1.5 * (ux * ux + uy * uy + uz * uz)
    out = [base] * 19
    for a in range(1, 19, 2):
        p = pair_vector(a, ux, uy, uz)
        even = base + 4.5 * (p * p)
        odd = 3.0 * p
        out[a] = even + odd
        out[a + 1] = even - odd
    return out


def wall_rows(first_row, height, kz, nz):
    rows = lax.broadcasted_iota(jnp.int32, (8, 128), 0) + first_row
    return ((rows == 0) & (kz == 0)) | ((rows == height - 1) & (kz == nz - 1))


def edge_kernel(
    nz, pops, mask, noise, mean, diag, off, za, zb, raw, flags, mean_v, diag_v, off_v, edge, sems
):
    height = pops.shape[2]
    kz = lax.axis_index("gz")
    upward = lax.rem(kz, 2) == 0
    upper = pl.ds(height - 8, 8)
    copies = [
        (pops.at[:, :, 0:8, :], raw.at[:, :, 0:8, :]),
        (pops.at[:, :, upper, :], raw.at[:, :, 8:16, :]),
        (mask.at[:, 0:8, :], flags.at[:, 0:8, :]),
        (mask.at[:, upper, :], flags.at[:, 8:16, :]),
        (mean, mean_v),
        (diag, diag_v),
        (off, off_v),
    ]
    for c in range(3):
        at = slice(ROW_NOISE + height * c, ROW_NOISE + height * (c + 1))
        copies.append((noise.at[c], za.at[at, :]))
        copies.append((noise.at[c], zb.at[at, :]))
    copies = [pltpu.make_async_copy(src, dst, sems.at[n]) for n, (src, dst) in enumerate(copies)]
    for copy in copies:
        copy.start()
    for part, row in ((0, 0), (1, height - 8)):
        copies[part].wait()
        copies[2 + part].wait()
        wall = wall_rows(row, height, kz, nz)
        at = slice(8 * part, 8 * part + 8)
        for x in range(4):
            solid = (flags[x, at, :] == 1) | wall
            post = collide([raw[i, x, at, :] for i in range(19)], solid)
            post.append(solid.astype(jnp.float32))
            for i in range(20):
                edge[64 * i + 16 * x + 8 * part : 64 * i + 16 * x + 8 * part + 8, :] = post[i]

    def put(q, i, depth):
        up = edge[pl.ds(64 * i + 15 - depth, 4, stride=16), :]
        down = edge[pl.ds(64 * (i if i == 19 else MIRROR_Z[i]) + depth, 4, stride=16), :]
        za[4 * q : 4 * q + 4, :] = jnp.where(upward, up, down)
        zb[4 * q : 4 * q + 4, :] = jnp.where(upward, down, up)

    for q, i in enumerate(Z_EDGE + Z_SECOND + [19]):
        put(q, i, 1 if len(Z_EDGE) <= q < 19 else 0)
    for copy in copies[4:]:
        copy.wait()
    for ref in (za, zb):
        ref[ROW_PARAM : ROW_PARAM + 8, :] = jnp.zeros((8, 128), jnp.float32)
        ref[ROW_PARAM : ROW_PARAM + 1, 0:height] = mean_v[...]
        ref[ROW_PARAM + 1 : ROW_PARAM + 4, 0:height] = diag_v[...]
        ref[ROW_PARAM + 4 : ROW_PARAM + 7, 0:height] = off_v[...]


def far_kernel(height, za, z2):
    kz = lax.axis_index("gz")
    low_half = lax.rem(kz, 4) < 2
    z2[...] = jnp.zeros((16, 128), jnp.float32)
    for c in range(3):
        base = ROW_NOISE + height * c
        last = za[base + height - 1 : base + height, :]
        first = za[base : base + 1, :]
        z2[c : c + 1, :] = jnp.where(low_half, last, first)
        z2[8 + c : 9 + c, :] = jnp.where(low_half, first, last)


def dot3(a, b, dims=(((1,), (0,)), ((), ()))):
    a_hi, b_hi = a.astype(jnp.bfloat16), b.astype(jnp.bfloat16)
    a_lo = (a - a_hi.astype(jnp.float32)).astype(jnp.bfloat16)
    b_lo = (b - b_hi.astype(jnp.float32)).astype(jnp.bfloat16)

    def dot(u, v):
        return lax.dot_general(u, v, dims, preferred_element_type=jnp.float32)

    return dot(a_hi, b_hi) + (dot(a_lo, b_hi) + dot(a_hi, b_lo))


NT = (((1,), (1,)), ((), ()))


def put_pair(pair, slot, value, first_column, into):
    return jnp.where(pair == slot, pltpu.roll(value, (2 * slot - first_column) % 128, 1), into)


def bulk_kernel(nz, pops, mask, post, solidp, ya, yb):
    height = pops.shape[2]
    kz = lax.axis_index("gz")
    ky = lax.axis_index("gy") * lax.axis_size("col") + lax.axis_index("col")
    y_even = lax.rem(ky, 2) == 0
    pair = lax.broadcasted_iota(jnp.int32, (8, 128), 1) // 2

    def body(t, carry):
        row = pl.multiple_of(t * 8, 8)
        out = pl.ds(row + PAD, 8)
        wall = wall_rows(row, height, kz, nz)
        flat = right = left = jnp.zeros((8, 128), jnp.float32)
        for x in range(4):
            solid = (mask[x, pl.ds(row, 8), :] == 1) | wall
            p = collide([pops[i, x, pl.ds(row, 8), :] for i in range(19)], solid)
            flag = solid.astype(jnp.float32)
            solidp[x, out, :] = flag
            flat = put_pair(pair, FLAG_PLANE + x, flag, 127, flat)
            for q, i in enumerate(Y_FLAT):
                post[i, x, out, :] = p[i]
                flat = put_pair(pair, 4 * q + x, p[i], 127, flat)
            for n, i in enumerate(Y_PLUS):
                j = MIRROR_Y[i]
                slot = LANE_PLUS // 2 + 4 * n + x
                post[i, x, out, :] = pltpu.roll(p[i], 1, 1)
                post[j, x, out, :] = pltpu.roll(p[j], 127, 1)
                right = put_pair(pair, slot, p[i], 126, right)
                left = put_pair(pair, slot, p[j], 0, left)
        right = jnp.where(pair < LANE_PLUS // 2, flat, right)
        left = jnp.where(pair < LANE_PLUS // 2, flat, left)
        ya[pl.ds(row, 8), :] = jnp.where(y_even, right, left)
        yb[pl.ds(row, 8), :] = jnp.where(y_even, left, right)
        return carry

    lax.fori_loop(0, height // 8, body, 0, unroll=2)


def column_kernel(
    nz, post_in, solid_in, sent, za, zb, z2c, z2d, bandz, pick,
    post, solidp, ya, yb, linear, meanrow,
    wide, filt, moved,
):
    height = post.shape[2] - 2 * PAD
    rows = height + 2 * PAD
    kz = lax.axis_index("gz")
    ky = lax.axis_index("gy") * lax.axis_size("col") + lax.axis_index("col")
    z_even = lax.rem(kz, 2) == 0
    y_even = lax.rem(ky, 2) == 0
    low_half = lax.rem(kz, 4) < 2

    def below(row, n=1):
        return jnp.where(z_even, zb[row : row + n, :], za[row : row + n, :])

    def above(row, n=1):
        return jnp.where(z_even, za[row : row + n, :], zb[row : row + n, :])

    top = PAD + height
    low, high = below(0, ROW_PARAM), above(0, ROW_PARAM)
    for n, shift in enumerate((0, 1, 127)):
        moved[n, 0] = low if shift == 0 else pltpu.roll(low, shift, 1)
        moved[n, 1] = high if shift == 0 else pltpu.roll(high, shift, 1)
    for items, first, depth in ((Z_EDGE, 0, 0), (Z_SECOND, len(Z_EDGE), 1)):
        for q, i in enumerate(items):
            n = DIRS[i][1] % 3
            for x in range(4):
                at = slice(4 * (first + q) + x, 4 * (first + q) + x + 1)
                post[i, x, PAD - 1 - depth : PAD - depth, :] = moved[n, 0, at, :]
                post[MIRROR_Z[i], x, top + depth : top + depth + 1, :] = moved[n, 1, at, :]
    for x in range(4):
        solidp[x, PAD - 1 : PAD, :] = moved[0, 0, ROW_SOLID + x : ROW_SOLID + x + 1, :]
        solidp[x, top : top + 1, :] = moved[0, 1, ROW_SOLID + x : ROW_SOLID + x + 1, :]

    lane = lax.broadcasted_iota(jnp.int32, (8, 128), 1)
    own_par = pltpu.roll(sent[ROW_PARAM : ROW_PARAM + 8, :], PAD, 1)
    low_par = pltpu.roll(below(ROW_PARAM, 8), 128 - height + PAD, 1)
    high_par = pltpu.roll(above(ROW_PARAM, 8), height + PAD, 1)
    par = jnp.where(lane < PAD, low_par, jnp.where(lane < top, own_par, high_par))
    par = jnp.where(lane < rows, par, 0.0)
    meanrow[...] = par
    cols = jnp.transpose(jnp.concatenate([par] * 16, axis=0))[0:rows]

    for c in range(3):
        lanes = slice(128 * c, 128 * c + 128)
        at = slice(ROW_NOISE + height * c, ROW_NOISE + height * (c + 1))
        wide[0:height, lanes] = below(ROW_NOISE + height * c, height)
        wide[height : 2 * height, lanes] = sent[at, :]
        wide[2 * height : 3 * height, lanes] = above(ROW_NOISE + height * c, height)
    filt[...] = dot3(bandz[...], wide[...])
    b_end = float(taps()[0])
    far_low = jnp.where(low_half, z2d[8:16, :], z2c[0:8, :])
    far_high = jnp.where(low_half, z2c[0:8, :], z2d[8:16, :])
    for c in range(3):
        lanes = slice(128 * c, 128 * c + 128)
        filt[PAD - 1 : PAD, lanes] += b_end * far_low[c : c + 1, :]
        filt[top : top + 1, lanes] += b_end * far_high[c : c + 1, :]
    f0, f1, f2 = (filt[:, 128 * c : 128 * c + 128] for c in range(3))
    linear[0] = cols[:, 1:2] * f0
    linear[1] = cols[:, 4:5] * f0 + cols[:, 2:3] * f1
    linear[2] = cols[:, 5:6] * f0 + cols[:, 6:7] * f1 + cols[:, 3:4] * f2
    linear[3] = jnp.broadcast_to(cols[:, 0:1], (rows, 128))

    pair = lane // 2
    for row in (0, rows - 8):
        out = slice(row, row + 8)
        flat = right = left = jnp.zeros((8, 128), jnp.float32)
        for x in range(4):
            flat = put_pair(pair, FLAG_PLANE + x, solidp[x, out, :], 127, flat)
            for q, i in enumerate(Y_FLAT):
                flat = put_pair(pair, 4 * q + x, post[i, x, out, :], 127, flat)
            for n, i in enumerate(Y_PLUS):
                slot = LANE_PLUS // 2 + 4 * n + x
                right = put_pair(pair, slot, post[i, x, out, :], 127, right)
                left = put_pair(pair, slot, post[MIRROR_Y[i], x, out, :], 127, left)
        right = jnp.where(pair < LANE_PLUS // 2, flat, right)
        left = jnp.where(pair < LANE_PLUS // 2, flat, left)
        at = slice(0, 2) if row else slice(6, 8)
        ya[at, :] = jnp.where(y_even, right, left)[at, :]
        yb[at, :] = jnp.where(y_even, left, right)[at, :]
    spare = jnp.zeros((1, 128), jnp.float32)
    for c in range(3):
        far = dot3(pick[...], linear[c], NT)
        far = jnp.concatenate([far, jnp.zeros((8, 128 - rows), jnp.float32)], axis=1)
        ya[Y_FAR + c : Y_FAR + c + 1, :] = jnp.where(y_even, far[0:1, :], far[1:2, :])
        yb[Y_FAR + c : Y_FAR + c + 1, :] = jnp.where(y_even, far[1:2, :], far[0:1, :])
    for ref in (ya, yb):
        ref[5:6, :] = spare
        ref[Y_FILTER + 3 * Y_HALF : Y_MESSAGE, :] = jnp.zeros((2, 128), jnp.float32)
    middle = FIRST + Y_HALF
    lane_h = lax.broadcasted_iota(jnp.int32, (Y_HALF, 128), 1)
    for c in range(3):
        first, second = linear[c, FIRST:middle, :], linear[c, middle : middle + Y_HALF, :]
        left = jnp.where(lane_h < 64, first, pltpu.roll(second, 64, 1))
        right = jnp.where(lane_h < 64, pltpu.roll(first, 64, 1), second)
        at = slice(Y_FILTER + Y_HALF * c, Y_FILTER + Y_HALF * (c + 1))
        ya[at, :] = jnp.where(y_even, right, left)
        yb[at, :] = jnp.where(y_even, left, right)


def streamed(i, x):
    source = x - DIRS[i][0]
    return None if source < 0 else min(source, 3)


INWARD = [i for i in range(19) if DIRS[i][2]]


def both_ghosts(sub, low, high):
    return jnp.where(sub < 4, low, high)


def assemble(tall, sa, sb, ya, yb, a_first):
    end = PAD + sa.shape[0]
    for out, source, a, b in (
        (slice(PAD, end), slice(0, sa.shape[0]), sa, sb),
        (slice(PAD - 2, PAD), slice(6, 8), ya, yb),
        (slice(end, end + 2), slice(0, 2), ya, yb),
    ):
        tall[0, out, :] = jnp.where(a_first, a[source, :], b[source, :])
        tall[1, out, :] = jnp.where(a_first, b[source, :], a[source, :])


def interior_kernel(
    nz, post, solidp, linear, sa, sb, ya, yb, wy, wg, post2, flow_own, ghost_own, own_right, own_left, tall
):
    rows = post.shape[2]
    top = rows - PAD
    kz = lax.axis_index("gz")
    ky = lax.axis_index("gy") * lax.axis_size("col") + lax.axis_index("col")
    y_even = lax.rem(ky, 2) == 0
    sub = lax.broadcasted_iota(jnp.int32, (8, 128), 0)

    def moved(i, value):
        return pltpu.roll(value, DIRS[i][1] % 128, 1) if DIRS[i][1] else value

    outside = ((sub < 4) & (kz == 0)) | ((sub >= 4) & (kz == nz - 1))
    for x in range(1, 4):
        solid = both_ghosts(sub, solidp[x, PAD - 1 : PAD + 7, :], solidp[x, top - 7 : top + 1, :]) > 0.5
        g = []
        for i in range(19):
            low, high, source = PAD - 1 - DIRS[i][2], top - 7 - DIRS[i][2], streamed(i, x)
            g.append(both_ghosts(sub, post[i, source, low : low + 8, :], post[i, source, high : high + 8, :]))
        p = collide(g, solid, INWARD)
        for i in INWARD:
            row, at = (PAD - 1, 0) if DIRS[i][2] == 1 else (top, 7)
            value = moved(i, jnp.where(outside, 0.0, p[i]))
            post2[i, x - 1, row : row + 1, :] = value[at : at + 1, :]

    def body(t, carry):
        row = pl.multiple_of(t * 8 + PAD, 8)
        for x in range(1, 4):
            solid = solidp[x, pl.ds(row, 8), :] > 0.5
            g = [post[i, streamed(i, x), pl.ds(row - DIRS[i][2], 8), :] for i in range(19)]
            p = collide(g, solid)
            for i in range(19):
                post2[i, x - 1, pl.ds(row, 8), :] = moved(i, p[i])
        return carry

    lax.fori_loop(0, rows // 8 - 2, body, 0, unroll=2)

    flow_own[...] = dot3(linear[0:3].reshape(3 * rows, 128), wy[0:128, :])
    flow_own[0:rows, :] += linear[3]
    for c in range(3):
        ghost_own[8 * c : 8 * c + 8, 0:rows] = dot3(wg[:, 0:128], linear[c], NT)
        ghost_own[8 * c : 8 * c + 8, rows:128] = jnp.zeros((8, 128 - rows), jnp.float32)
    assemble(tall, sa, sb, ya, yb, y_even)
    own_right[0:128, :] = jnp.transpose(tall[0])
    own_left[0:128, :] = jnp.transpose(tall[1])


def final_kernel(
    nz, post, solidp, post2, flow_own, ghost_own, own_right, own_left, meanrow, sa, sb, ya, yb, wy, wg,
    inflow, state_out,
    lhs, flow, inlet2, strip_left, strip_right, moving, still, ghost_moving, ghost_still,
    state, flow_out, tall, sems,
):
    height = state.shape[2]
    rows = height + 2 * PAD
    top = PAD + height
    kz = lax.axis_index("gz")
    ky = lax.axis_index("gy") * lax.axis_size("col") + lax.axis_index("col")
    y_even = lax.rem(ky, 2) == 0
    lane = lax.broadcasted_iota(jnp.int32, (8, 128), 1)
    sub = lax.broadcasted_iota(jnp.int32, (8, 128), 0)

    assemble(tall, sa, sb, ya, yb, jnp.logical_not(y_even))
    strip_left[0:128, 0:rows] = jnp.transpose(tall[0, 0:rows, :])
    strip_right[0:128, 0:rows] = jnp.transpose(tall[1, 0:rows, :])

    lane_h = lax.broadcasted_iota(jnp.int32, (Y_HALF, 128), 1)
    for c in range(3):
        at = slice(Y_FILTER + Y_HALF * c, Y_FILTER + Y_HALF * (c + 1))
        a, b = ya[at, :], yb[at, :]
        left, right = jnp.where(y_even, b, a), jnp.where(y_even, a, b)
        middle = rows * c + FIRST + Y_HALF
        lo, hi = slice(middle - Y_HALF, middle), slice(middle, middle + Y_HALF)
        lhs[lo, 0:128] = jnp.where(lane_h < 64, left, 0.0)
        lhs[hi, 0:128] = jnp.where(lane_h < 64, 0.0, left)
        lhs[lo, 128:256] = jnp.where(lane_h < 64, right, 0.0)
        lhs[hi, 128:256] = jnp.where(lane_h < 64, 0.0, right)
    flow[...] = flow_own[...] + dot3(lhs[...], wy[128:384, :])
    for c in range(3):
        flow_out[c] = flow[rows * c + PAD : rows * c + top, :]
    flow_copy = pltpu.make_async_copy(flow_out, inflow, sems.at[height // 8])
    flow_copy.start()
    b_end = float(taps()[0])
    column_flow = []
    for c in range(3):
        g = dot3(wg[:, 128:384], lhs[rows * c : rows * (c + 1), :], NT)
        g = jnp.concatenate([g, jnp.zeros((8, 128 - rows), jnp.float32)], axis=1)
        g = g + ghost_own[8 * c : 8 * c + 8, :]
        far = slice(Y_FAR + c, Y_FAR + c + 1)
        at = [g[n : n + 1, :] for n in range(4)]
        at[0] = at[0] + b_end * jnp.where(y_even, yb[far, :], ya[far, :])
        at[3] = at[3] + b_end * jnp.where(y_even, ya[far, :], yb[far, :])
        if c == 0:
            at = [v + meanrow[0:1, :] for v in at]
        column_flow.append(at)

    outside = ((lane < PAD) & (kz == 0)) | ((lane >= top) & (kz == nz - 1))
    sources = (
        ((strip_left, 0), (strip_left, 0), (own_left, 0)),
        ((own_left, 1), (strip_left, 1), (own_left, 1)),
        ((own_right, 0), (own_right, 0), (strip_right, 0)),
        ((strip_right, 1), (own_right, 1), (strip_right, 1)),
    )
    for column in range(4):
        def rows_of(start):
            return pl.ds(start, 8, stride=2)

        src, odd = sources[column][0]
        solid = src[rows_of(2 * FLAG_PLANE + odd), :] > 0.5
        g = [None] * 19
        for i in range(19):
            cx, cy, cz = DIRS[i]
            src, odd = sources[column][cy % 3]
            if cy == 0:
                start = 8 * Y_FLAT.index(i) + odd
            else:
                start = LANE_PLUS + 8 * Y_PLUS.index(i if cy == 1 else MIRROR_Y[i]) + odd
            v = src[rows_of(start - 2 * cx), :]
            if cx == 1:
                v = jnp.where(sub == 0, 0.0, v)
            elif cx == -1:
                v = jnp.where(sub == 3, src[rows_of(start), :], v)
            g[i] = v if cz == 0 else pltpu.roll(v, cz % 128, 1)
        us = [INLET * jnp.broadcast_to(column_flow[c][column], (8, 128)) for c in range(3)]
        eq = inlet_state(*us)
        put = (sub == 0) & jnp.logical_not(solid)
        moves = 1 if column < 2 else -1
        keep = [i for i in range(19) if DIRS[i][1] == moves or (DIRS[i][1] == 0 and column in (1, 2))]
        p = collide(g, solid, keep)
        for i in keep:
            value = jnp.where(outside, 0.0, jnp.where(put, eq[i], p[i]))[0:4, :]
            if DIRS[i][1]:
                n = Y_PLUS.index(i if moves == 1 else MIRROR_Y[i])
                moving[pl.ds(16 * n + (column + 2) % 4, 4, stride=4), :] = value
            else:
                still[pl.ds(8 * Y_FLAT.index(i) + 2 - column, 4, stride=2), :] = value
    ghost_moving[:, 0:80] = jnp.transpose(moving[0:80, :])
    ghost_still[:, 0:72] = jnp.transpose(still[0:72, :])

    def inlet_values(us, solid, planes, load):
        eq = inlet_state(*[INLET * u for u in us])
        for i in planes:
            j = OPP[i]
            source = streamed(j, 0)
            bounced = 0.0 if source is None else load(j, source)
            yield i, jnp.where(solid, bounced, eq[i])

    def moved(i, value):
        return pltpu.roll(value, DIRS[i][1] % 128, 1) if DIRS[i][1] else value

    def inlet(row):
        us = [flow[pl.ds(rows * c + row, 8), :] for c in range(3)]
        solid = solidp[0, pl.ds(row, 8), :] > 0.5
        load = lambda j, source: post[j, source, pl.ds(row - DIRS[j][2], 8), :]
        for i, value in inlet_values(us, solid, range(19), load):
            inlet2[i, pl.ds(row, 8), :] = moved(i, value)

    def inlet_ghosts():
        low, high = PAD - 1, top - 7

        def both(ref, shift, *lead):
            low_at, high_at = slice(low + shift, low + shift + 8), slice(high + shift, high + shift + 8)
            return both_ghosts(sub, ref[(*lead, low_at)], ref[(*lead, high_at)])

        us = [both(flow, rows * c) for c in range(3)]
        solid = both(solidp, 0, 0) > 0.5
        load = lambda j, source: both(post, -DIRS[j][2], j, source)
        beyond = ((sub < 4) & (kz == 0)) | ((sub >= 4) & (kz == nz - 1))
        for i, value in inlet_values(us, solid, INWARD, load):
            row, at = (PAD - 1, 0) if DIRS[i][2] == 1 else (top, 7)
            value = moved(i, jnp.where(beyond, 0.0, value))
            inlet2[i, row : row + 1, :] = value[at : at + 1, :]

    def out_copy(t):
        at = pl.ds(pl.multiple_of(t * 8, 8), 8)
        return pltpu.make_async_copy(state.at[:, :, at, :], state_out.at[:, :, at, :], sems.at[t])

    def last(t):
        row = pl.multiple_of(t * 8 + PAD, 8)
        us = [INLET * flow[pl.ds(rows * c + row, 8), :] for c in range(3)]
        eq = inlet_state(*us)
        solid = solidp[0, pl.ds(row, 8), :] > 0.5
        ends = (lane == 0) | (lane == 127)

        def read(i, source, ghost):
            at = pl.ds(row - DIRS[i][2], 8)
            v = inlet2[i, at, :] if source == 0 else post2[i, source - 1, at, :]
            where = ends if DIRS[i][1] == 0 else (lane < 2 if DIRS[i][1] == 1 else lane >= 126)
            return jnp.where(where, ghost, v)

        def write(i, x, value):
            if x == 0:
                value = jnp.where(solid, value, eq[i])
            state[i, x, pl.ds(row - PAD, 8), :] = value

        for i in Y_FLAT + Y_PLUS:
            both = [i] if DIRS[i][1] == 0 else [i, MIRROR_Y[i]]
            at = pl.ds(row - DIRS[i][2], 8)
            for source in range(4):
                targets = [x for x in range(4) if streamed(i, x) == source]
                if not targets:
                    continue
                if DIRS[i][1] == 0:
                    slot = 2 * (4 * Y_FLAT.index(i) + source)
                    ghost = pltpu.roll(ghost_still[at, :], (127 - slot) % 128, 1)
                else:
                    slot = 4 * (4 * Y_PLUS.index(i) + source)
                    ghost = pltpu.roll(ghost_moving[at, :], (126 - slot) % 128, 1)
                for j in both:
                    value = read(j, source, ghost)
                    for x in targets:
                        write(j, x, value)
            for j in both:
                if streamed(j, 0) is None:
                    write(j, 0, jnp.zeros((8, 128), jnp.float32))
        out_copy(t).start()

    inlet_ghosts()
    inlet(PAD)

    def main(t, carry):
        inlet(pl.multiple_of(t * 8 + PAD, 8))
        last(t - 1)
        return carry

    tiles = height // 8
    lax.fori_loop(1, tiles, main, 0, unroll=True)
    last(tiles - 1)
    for t in range(tiles):
        out_copy(t).wait()
    flow_copy.wait()


def swap_pairs(count, phase, distance=1):
    pairs = []
    for i in range(count):
        block = (i + phase * distance) // distance
        j = i + distance if block % 2 == 0 else i - distance
        if 0 <= j < count:
            pairs.append((i, j))
    return pairs


def ring_pairs(count, phase):
    if phase == 0:
        return [(i, i ^ 1) for i in range(count)]
    return [(i, (((i + 1) % count ^ 1) - 1) % count) for i in range(count)]


def vm(n):
    return [pl.BlockSpec(memory_space=pltpu.VMEM)] * n


def hbm(n):
    return [pl.BlockSpec(memory_space=pltpu.HBM)] * n


def f32(*shape):
    return jax.ShapeDtypeStruct(shape, jnp.float32)


def scratch(*shape):
    return pltpu.VMEM(shape, jnp.float32)


def flags(*shape):
    return pltpu.VMEM(shape, jnp.int32)


def params(mib):
    return pltpu.CompilerParams(vmem_limit_bytes=mib * 1024 * 1024)


def cost(flops, size):
    return pl.CostEstimate(flops=flops, bytes_accessed=size, transcendentals=0)


def shards(nz, ny, noise, mean_profile, lund_diag, lund_off, populations, mask):
    height, span = noise.shape[1], noise.shape[2]
    rows = height + 2 * PAD
    message = ROW_NOISE + 3 * height
    dma = pltpu.SemaphoreType.DMA
    here = lambda value: pltpu.with_memory_space_constraint(value, pltpu.HBM)
    mean_profile = mean_profile.reshape(1, height)
    operands = populations, mask, noise, mean_profile, lund_diag, lund_off

    za, zb = pl.pallas_call(
        lambda *refs: edge_kernel(nz, *refs),
        out_shape=(f32(message, 128), f32(message, 128)),
        in_specs=hbm(6),
        out_specs=vm(2),
        scratch_shapes=[
            scratch(19, 4, 16, 128), flags(4, 16, 128), scratch(1, height), scratch(3, height),
            scratch(3, height), scratch(20 * 4 * 16, 128), dma((13,)),
        ],
        compiler_params=params(8),
        name="edge_rows",
    )(*map(here, operands))

    z2 = pl.pallas_call(
        lambda *refs: far_kernel(height, *refs),
        out_shape=f32(16, 128),
        in_specs=vm(1),
        out_specs=pl.BlockSpec(memory_space=pltpu.VMEM),
        compiler_params=params(1),
        name="far_rows",
    )(za)

    ra = lax.ppermute(za, "gz", swap_pairs(nz, 0))
    rb = lax.ppermute(zb, "gz", swap_pairs(nz, 1))
    rc = lax.ppermute(z2, "gz", swap_pairs(nz, 0, 2))
    far = swap_pairs(nz, 1, 2)
    rd = lax.ppermute(z2, "gz", far) if far else jnp.zeros_like(z2)

    post, solidp, sa, sb = pl.pallas_call(
        lambda *refs: bulk_kernel(nz, *refs),
        out_shape=(f32(19, 4, rows, 128), f32(4, rows, 128), f32(height, 128), f32(height, 128)),
        in_specs=vm(2),
        out_specs=vm(4),
        compiler_params=params(4),
        cost_estimate=cost(4_000_000_000, 8_000_000),
        name="bulk",
    )(populations, mask)

    pa = lax.ppermute(sa, ("gy", "col"), ring_pairs(ny, 0))
    pb = lax.ppermute(sb, ("gy", "col"), ring_pairs(ny, 1))
    pick = np.zeros((8, 128), np.float32)
    pick[0, span - HW - 1] = pick[1, HW] = 1.0

    line = np.arange(rows) - PAD
    used = (line >= -1) & (line <= height)
    bandz = np.where(used[:, None], band(np.arange(-height, 2 * height), line).T, 0.0)
    post, solidp, ya, yb, linear, meanrow = pl.pallas_call(
        lambda *refs: column_kernel(nz, *refs),
        out_shape=(
            f32(19, 4, rows, 128), f32(4, rows, 128), f32(Y_MESSAGE, 128), f32(Y_MESSAGE, 128),
            f32(4, rows, 128), f32(8, 128),
        ),
        in_specs=vm(9),
        out_specs=vm(6),
        scratch_shapes=[
            scratch(3 * height, 384), scratch(rows, 384), scratch(3, 2, ROW_PARAM, 128),
        ],
        input_output_aliases={0: 0, 1: 1},
        compiler_params=params(4),
        name="columns",
    )(post, solidp, za, ra, rb, rc, rd, jnp.asarray(bandz, jnp.float32), jnp.asarray(pick))

    qa = lax.ppermute(ya, ("gy", "col"), ring_pairs(ny, 0))
    qb = lax.ppermute(yb, ("gy", "col"), ring_pairs(ny, 1))

    own = np.arange(span)
    left = np.arange(128) % 64 - 64
    right = np.arange(128) % 64 + span
    source = np.concatenate([own, left, right])
    wy = jnp.asarray(band(source, own))
    wg = np.zeros((8, 384), np.float32)
    wg[0:4] = band(source, np.array([-1, 0, span - 1, span])).T
    wg = jnp.asarray(wg)
    post2, flow_own, ghost_own, own_right, own_left = pl.pallas_call(
        lambda *refs: interior_kernel(nz, *refs),
        out_shape=(
            f32(19, 3, rows, 128), f32(3 * rows, 128), f32(24, 128), f32(144, 128), f32(144, 128),
        ),
        in_specs=vm(9),
        out_specs=vm(5),
        scratch_shapes=[scratch(2, 128, 128)],
        compiler_params=params(4),
        cost_estimate=cost(4_000_000_000, 8_000_000),
        name="interior",
    )(post, solidp, linear, sa, sb, ya, yb, wy, wg)
    inflow, state = pl.pallas_call(
        lambda *refs: final_kernel(nz, *refs),
        out_shape=(f32(3, height, span), f32(19, 4, height, span)),
        in_specs=vm(14),
        out_specs=hbm(2),
        scratch_shapes=[
            scratch(3 * rows, 256), scratch(3 * rows, 128), scratch(19, rows, 128),
            scratch(144, 128), scratch(144, 128), scratch(128, 128), scratch(128, 128),
            scratch(128, 128), scratch(128, 128), scratch(19, 4, height, span),
            scratch(3, height, span), scratch(2, 128, 128), dma((height // 8 + 1,)),
        ],
        compiler_params=params(8),
        name="stream",
    )(post, solidp, post2, flow_own, ghost_own, own_right, own_left, meanrow, pa, pb, qa, qb, wy, wg)
    return inflow, state


def solution(mesh):
    nz = mesh.shape["gz"]
    ny = mesh.shape["gy"] * mesh.shape["col"]
    in_specs = (
        P(None, "gz", ("gy", "col")),
        P("gz"),
        P(None, "gz"),
        P(None, "gz"),
        P(None, None, "gz", ("gy", "col")),
        P(None, "gz", ("gy", "col")),
    )
    out_specs = (P(None, "gz", ("gy", "col")), P(None, None, "gz", ("gy", "col")))

    def body(*args):
        return shards(nz, ny, *args)

    return jax.shard_map(body, mesh=mesh, in_specs=in_specs, out_specs=out_specs, check_vma=False)
```
